32 devices in a mesh: groups: 2 (over x), expert: 8 (over z, y), dp: 2 (over core).
Axes of the slice: x: 2, y: 2, z: 4, core: 2. Of those that a mesh axis runs over, the one named last changes fastest.
Arguments:
- tokens: bfloat16 [4, 1024, 6144], P(('groups', 'dp'), 'expert'), parts along dimension 0, may hold values from -6 to 6
- output_gradient: bfloat16 [4, 1024, 6144], P(('groups', 'dp'), 'expert'), parts along dimension 0, may hold values from -12 to 12
- token_expert_choice: int32 [4, 1024, 4], P(('groups', 'dp'), 'expert'), parts along dimension 0, may hold values from 0 to 15, as said below
- routing_weight_table: bfloat16 [4, 1024, 4], P(('groups', 'dp'), 'expert'), parts along dimension 0, may hold values from 0.049804688 to 0.59765625
- stored_gate_rows: bfloat16 [4, 288, 6144], P(('groups', 'dp'), None, 'expert'), parts along dimension 0, may hold values from -9 to 9
- stored_up_rows: bfloat16 [4, 288, 6144], P(('groups', 'dp'), None, 'expert'), parts along dimension 0, may hold values from -6 to 6
- gate_weight: bfloat16 [6144, 6144], P(None, 'expert'), may hold values from -0.078125 to 0.078125
- up_weight: bfloat16 [6144, 6144], P(None, 'expert'), may hold values from -0.078125 to 0.078125
- down_weight: bfloat16 [6144, 6144], P('expert'), may hold values from -0.078125 to 0.078125
- adapter_down_factor: bfloat16 [128, 6144], P('groups'), parts along dimension 0, may hold values from -0.078125 to 0.078125
- adapter_gate_factor: bfloat16 [128, 6144], P('groups', 'expert'), parts along dimension 0, may hold values from -0.75 to 0.75
- adapter_up_factor: bfloat16 [128, 6144], P('groups', 'expert'), parts along dimension 0, may hold values from -0.75 to 0.75
Outputs:
- input_gradient: bfloat16 [4, 1024, 6144], P(('groups', 'dp'), 'expert'), parts along dimension 0
- grad_lora_down: float32 [128, 6144], P('groups', 'expert'), parts along dimension 0
- grad_lora_gate: float32 [128, 6144], P('groups', 'expert'), parts along dimension 0
- grad_lora_up: float32 [128, 6144], P('groups', 'expert'), parts along dimension 0
The draws below stay inside these ranges and needn't reach their ends.
There are 2 independent parts, one for each index of `groups`. The reference program is written for one: setup_inputs(seed, part) draws one part's arguments, and reference() takes and returns one part's arrays. A program takes and returns all parts, laid end to end along the dimension named above; an argument that names none is the same for every part. Nothing has to cross between parts.
Inputs may be any that keep to these rules, and one draw needn't show every extreme that they name: `token_expert_choice`: each token names 4 different experts. Within the 128 tokens of one device (aligned blocks along the token dimension of each replica) expert 0 is named by 1 to 36 tokens, and in every replica some device's tokens name it exactly 36 times.
All inputs are finite; a program needn't handle non-finite values.
Results may differ from the reference program's by a relative error of at most 0.018.
Values may be sent and summed in bfloat16 or wider, within the bound.
No kernel may reach another device: no remote copies, remote signals or barrier semaphores. Data moves between devices by JAX's collectives and lax.ppermute only.
A program may use at most 128 MiB of HBM per device.

```python
import jax
import jax.numpy as jnp
from jax import lax

MODEL_DIM = 6144
EXPERTS = 16
TOP = 4
EXPERT_HIDDEN = 6144
ADAPTER_RANK = 64
TOK_DEV = 128
CAP = 36
HIDDEN_PER_SHARD = 768
SLOTS = 288
TOKENS = 1024
REPLICAS = 2
N_EXPERT = 8


def draw_token_expert_choice(key, part):
    key = jax.random.fold_in(key, 11)
    keys = jax.random.split(key, 5)
    counts = jax.random.randint(keys[0], (REPLICAS, N_EXPERT), 1, CAP + 1)
    peak = jax.random.randint(keys[1], (REPLICAS,), 0, N_EXPERT)
    counts = jnp.where(jnp.arange(N_EXPERT)[None, :] == peak[:, None], CAP, counts)
    block_keys = jax.random.split(keys[2], REPLICAS * N_EXPERT)
    ranks = jax.vmap(lambda one: jax.random.permutation(one, TOK_DEV))(block_keys).reshape(REPLICAS, N_EXPERT, TOK_DEV)
    include = (ranks < counts[:, :, None]).reshape(REPLICAS, TOKENS, 1)
    scores = jax.random.randint(keys[3], (REPLICAS, TOKENS, EXPERTS - 1), 0, 1 << 20) * 16 + jnp.arange(EXPERTS - 1)[None, None, :]
    others = jnp.argsort(scores, axis=-1)[:, :, :TOP] + 1
    spot = jax.random.randint(keys[4], (REPLICAS, TOKENS, 1), 0, TOP)
    selected_mask = jnp.where(include & (jnp.arange(TOP)[None, None, :] == spot), 0, others)
    return selected_mask.astype(jnp.int32)


def levels(rng, extent, shards, least, largest):
    gain = 1.0
    for axis_at, blocks in shards:
        steps = jax.random.uniform(jax.random.fold_in(jax.random.fold_in(rng, 6), axis_at), (blocks,), jnp.float32, least / len(shards), largest / len(shards))
        gain = gain * jnp.repeat(jnp.exp(steps), extent[axis_at] // blocks).reshape((-1,) + (1,) * (len(extent) - 1 - axis_at))
    return gain


def scatter_about(own_key, dims, spread, bound, cuts=(), kind=jnp.bfloat16):
    level = levels(own_key, dims, cuts, -0.22, 0.18) if cuts else 1.0
    values = jax.random.normal(own_key, dims, jnp.float32) * spread * level
    return jnp.minimum(jnp.maximum(values, -bound), bound).astype(kind)


def setup_inputs(seed: int = 0, part: int = 0) -> dict:
    key_of = jax.random.split(jax.random.key(seed), 13)
    part_splits = jax.random.split(jax.random.fold_in(key_of[12], part), 13)
    return {
        "tokens": scatter_about(part_splits[0], (REPLICAS, TOKENS, MODEL_DIM), 1.0, 6.0, ((0, 2), (1, 8))),
        "output_gradient": scatter_about(part_splits[1], (REPLICAS, TOKENS, MODEL_DIM), 2.0, 12.0, ((0, 2), (1, 8))),
        "token_expert_choice": draw_token_expert_choice(jax.random.fold_in(jax.random.fold_in(key_of[12], part), 71), part),
        "routing_weight_table": jnp.clip(0.049804688 + 0.54785156 * jax.random.uniform(part_splits[3], (REPLICAS, TOKENS, TOP), jnp.float32) ** levels(part_splits[3], (REPLICAS, TOKENS, TOP), ((0, 2), (1, 8)), -0.2, 0.2), 0.049804688, 0.59765625).astype(jnp.bfloat16),
        "stored_gate_rows": scatter_about(part_splits[4], (REPLICAS, SLOTS, EXPERT_HIDDEN), 1.5, 9.0, ((0, 2), (2, 8))),
        "stored_up_rows": scatter_about(part_splits[5], (REPLICAS, SLOTS, EXPERT_HIDDEN), 1.0, 6.0, ((0, 2), (2, 8))),
        "gate_weight": scatter_about(key_of[6], (MODEL_DIM, EXPERT_HIDDEN), MODEL_DIM ** -0.5, 0.078125, ((1, 8),)),
        "up_weight": scatter_about(key_of[7], (MODEL_DIM, EXPERT_HIDDEN), MODEL_DIM ** -0.5, 0.078125, ((1, 8),)),
        "down_weight": scatter_about(key_of[8], (EXPERT_HIDDEN, MODEL_DIM), MODEL_DIM ** -0.5, 0.078125, ((0, 8),)),
        "adapter_down_factor": scatter_about(part_splits[9], (ADAPTER_RANK, MODEL_DIM), MODEL_DIM ** -0.5, 0.078125),
        "adapter_gate_factor": scatter_about(part_splits[10], (ADAPTER_RANK, EXPERT_HIDDEN), ADAPTER_RANK ** -0.5, 0.75, ((1, 8),)),
        "adapter_up_factor": scatter_about(part_splits[11], (ADAPTER_RANK, EXPERT_HIDDEN), ADAPTER_RANK ** -0.5, 0.75, ((1, 8),)),
    }


SCALE = 0.25


def activation_grads(pre_gate, pre_up, grad_hidden):
    sigma = jax.nn.sigmoid(pre_gate)
    slope = sigma * (1.0 + pre_gate * (1.0 - sigma))
    gate_gradient = (grad_hidden * pre_up * slope).astype(jnp.bfloat16)
    up_gradient = (grad_hidden * pre_gate * sigma).astype(jnp.bfloat16)
    return gate_gradient, up_gradient


def shard_backward_step(input_rows, gradient_row_block, selected_mask, token_weight_rows, gate_preactivation, up_preactivation, gate_weight, up_weight, down_weight, adapter_down_factor, adapter_gate_factor, adapter_up_factor):
    adapter_product = jnp.dot(input_rows, adapter_down_factor.T, preferred_element_type=jnp.float32).astype(jnp.bfloat16)
    hit = selected_mask == 0
    named = jnp.any(hit, axis=1).astype(jnp.int32)
    weight_tok = jnp.sum(jnp.where(hit, token_weight_rows.astype(jnp.float32), jnp.float32(0.0)), axis=1)
    per_device = named.reshape(N_EXPERT, TOK_DEV)
    slot = (jnp.cumsum(per_device, axis=1) - 1).reshape(-1).astype(jnp.int32)
    block = (jnp.arange(TOKENS, dtype=jnp.int32) // TOK_DEV).astype(jnp.int32)
    row = jnp.where(named == 1, block * CAP + slot, SLOTS).astype(jnp.int32)
    source_table = jnp.full((SLOTS + 1,), TOKENS, jnp.int32).at[row].set(jnp.arange(TOKENS, dtype=jnp.int32))[:SLOTS]
    gate_table = jnp.zeros((SLOTS + 1,), jnp.float32).at[row].set(weight_tok)[:SLOTS]
    grad_padded = jnp.concatenate([gradient_row_block, jnp.zeros((1, MODEL_DIM), gradient_row_block.dtype)], axis=0)
    low_padded = jnp.concatenate([adapter_product, jnp.zeros((1, ADAPTER_RANK), adapter_product.dtype)], axis=0)
    slab_rows = grad_padded[source_table]
    low_rows = low_padded[source_table]

    def block_step(carried, index):
        reduced_total, low_summed = carried
        start_offset = (index * HIDDEN_PER_SHARD).astype(jnp.int32)
        down_part = lax.dynamic_slice_in_dim(down_weight, start_offset, HIDDEN_PER_SHARD, 0)
        gate_part = lax.dynamic_slice_in_dim(gate_weight, start_offset, HIDDEN_PER_SHARD, 1)
        up_part = lax.dynamic_slice_in_dim(up_weight, start_offset, HIDDEN_PER_SHARD, 1)
        pre_gate = lax.dynamic_slice_in_dim(gate_preactivation, start_offset, HIDDEN_PER_SHARD, 1).astype(jnp.float32)
        pre_up = lax.dynamic_slice_in_dim(up_preactivation, start_offset, HIDDEN_PER_SHARD, 1).astype(jnp.float32)
        gate_factor_slice = lax.dynamic_slice_in_dim(adapter_gate_factor, start_offset, HIDDEN_PER_SHARD, 1)
        up_factor_slice = lax.dynamic_slice_in_dim(adapter_up_factor, start_offset, HIDDEN_PER_SHARD, 1)
        grad_hidden = jnp.dot(slab_rows, down_part.T, preferred_element_type=jnp.float32) * gate_table[:, None]
        gate_gradient, up_gradient = activation_grads(pre_gate, pre_up, grad_hidden)
        partial_value = (jnp.dot(gate_gradient, gate_part.T, preferred_element_type=jnp.float32)
                   + jnp.dot(up_gradient, up_part.T, preferred_element_type=jnp.float32)).astype(jnp.bfloat16)
        low_partial = (SCALE * (jnp.dot(gate_gradient, gate_factor_slice.T, preferred_element_type=jnp.float32)
                                + jnp.dot(up_gradient, up_factor_slice.T, preferred_element_type=jnp.float32))).astype(jnp.bfloat16)
        partial_value, low_partial = lax.optimization_barrier((partial_value, low_partial))
        grad_gate = SCALE * jnp.dot(low_rows.T, gate_gradient, preferred_element_type=jnp.float32)
        grad_up = SCALE * jnp.dot(low_rows.T, up_gradient, preferred_element_type=jnp.float32)
        return (reduced_total + partial_value.astype(jnp.float32), low_summed + low_partial.astype(jnp.float32)), (grad_gate, grad_up)

    start = (jnp.zeros((SLOTS, MODEL_DIM), jnp.float32), jnp.zeros((SLOTS, ADAPTER_RANK), jnp.float32))
    (reduced_total, low_summed), (grad_gate, grad_up) = lax.scan(block_step, start, jnp.arange(N_EXPERT, dtype=jnp.int32))
    grad_gate = jnp.transpose(grad_gate, (1, 0, 2)).reshape(ADAPTER_RANK, EXPERT_HIDDEN)
    grad_up = jnp.transpose(grad_up, (1, 0, 2)).reshape(ADAPTER_RANK, EXPERT_HIDDEN)
    picked = jnp.minimum(row, SLOTS - 1).astype(jnp.int32)
    mask = (named == 1)[:, None]
    token_total_sum = jnp.where(mask, reduced_total[picked], jnp.float32(0.0))
    low_tok = jnp.where(mask, low_summed[picked], jnp.float32(0.0))
    adapter_rank_sum = low_tok.astype(jnp.bfloat16)
    input_gradient = (token_total_sum + jnp.dot(adapter_rank_sum, adapter_down_factor, preferred_element_type=jnp.float32)).astype(jnp.bfloat16)
    grad_down = jnp.dot(adapter_rank_sum.T, input_rows, preferred_element_type=jnp.float32)
    return input_gradient, grad_down, grad_gate, grad_up


def reference(tokens, output_gradient, token_expert_choice, routing_weight_table, stored_gate_rows, stored_up_rows, gate_weight, up_weight, down_weight, adapter_down_factor, adapter_gate_factor, adapter_up_factor):
    grads_in = []
    grad_down = jnp.zeros((ADAPTER_RANK, MODEL_DIM), jnp.float32)
    grad_gate = jnp.zeros((ADAPTER_RANK, EXPERT_HIDDEN), jnp.float32)
    grad_up = jnp.zeros((ADAPTER_RANK, EXPERT_HIDDEN), jnp.float32)
    for shard_number in range(REPLICAS):
        result = shard_backward_step(tokens[shard_number], output_gradient[shard_number], token_expert_choice[shard_number], routing_weight_table[shard_number],
                                  stored_gate_rows[shard_number], stored_up_rows[shard_number], gate_weight, up_weight, down_weight, adapter_down_factor, adapter_gate_factor, adapter_up_factor)
        grads_in.append(result[0])
        grad_down = grad_down + result[1]
        grad_gate = grad_gate + result[2]
        grad_up = grad_up + result[3]
    return jnp.stack(grads_in, axis=0), grad_down, grad_gate, grad_up
```

```python
import functools

import jax
import jax.numpy as jnp
from jax import lax
from jax.experimental import pallas as pl
from jax.experimental.pallas import tpu as pltpu
from jax.sharding import PartitionSpec as P

SCALE = 0.25
NT = (((1,), (1,)), ((), ()))
TN = (((0,), (0,)), ((), ()))
BF = jnp.bfloat16
F32 = jnp.float32
VMEM_LIMIT = 48 * 1024 * 1024


def ring_order(mesh):
    count = mesh.shape["expert"]
    plain = list(range(count))
    if count < 4 or count % 2:
        return plain
    snake = list(range(0, count, 2)) + list(range(count - 1, 0, -2))
    spots = [getattr(d, "coords", None) for d in mesh.devices[0, :, 0]]
    if any(s is None for s in spots):
        return snake if count == 8 else plain

    def length(order):
        hops = zip(order, order[1:] + order[:1])
        return sum(sum(abs(a - b) for a, b in zip(spots[i], spots[j])) for i, j in hops)

    return min((plain, snake), key=length)


def dot(a, b, dims=None):
    if dims is None:
        dims = (((1,), (0,)), ((), ()))
    return lax.dot_general(a, b, dims, preferred_element_type=F32)


def pick_rows(choice, capacity):
    tokens = choice.shape[1]
    named = jnp.max((choice == 0).astype(F32), axis=0, keepdims=True)
    before = lax.broadcasted_iota(jnp.int32, (tokens, tokens), 0)
    after = lax.broadcasted_iota(jnp.int32, (tokens, tokens), 1)
    upto = (before <= after).astype(BF)
    count = dot(jnp.broadcast_to(named, (8, tokens)).astype(BF), upto)[:1]
    slot = jnp.where(named > 0, count - 1.0, -1000.0).astype(jnp.int32)
    row = lax.broadcasted_iota(jnp.int32, (2 * capacity, tokens), 0)
    return (row == slot).astype(BF), (row - capacity == slot).astype(BF)


def prepare_kernel(capacity, choice_ref, weight_ref, grad_ref, tokens_ref, down_ref, block_ref):
    half = grad_ref.shape[1] // 2
    rank = down_ref.shape[0]
    choice = choice_ref[...]
    upper, lower = pick_rows(choice, capacity)
    block_ref[:, :half] = (dot(upper, grad_ref[:, :half]) + dot(lower, grad_ref[:, half:])).astype(BF)
    low = dot(tokens_ref[...], down_ref[...], NT).astype(BF)
    weight = jnp.sum(
        jnp.where(choice == 0, weight_ref[...].astype(F32), 0.0), axis=0, keepdims=True
    )
    column = jnp.sum(upper.astype(F32) * weight, axis=1, keepdims=True)
    block_ref[:, half : half + rank] = dot(upper, low).astype(BF)
    block_ref[:, half + rank :] = jnp.broadcast_to(column, (2 * capacity, rank)).astype(BF)


def hidden_kernel(capacity, slot, count, *refs):
    blocks, (gate_ref, up_ref, down_ref, dgate_ref, dup_ref, rows) = refs[:count], refs[count:]
    half = down_ref.shape[1] // 2
    rank = (blocks[0].shape[1] - half) // 2
    tall = rows.shape[0] // count

    @pl.when(pl.program_id(0) == 0)
    def _():
        for i, block in enumerate(blocks):
            rows[i * tall : i * tall + 2 * capacity, :] = block[:, :half]

    first = dot(rows[...], down_ref[:, :half], NT)
    second = dot(rows[...], down_ref[:, half:], NT)
    live = lax.broadcasted_iota(jnp.int32, (slot, first.shape[1]), 0) < capacity
    for i, block in enumerate(blocks):
        at = i * tall
        weight = block[:, half:].astype(F32)[:slot, rank : rank + 1]
        grad = (first[at : at + slot] + second[at + capacity : at + capacity + slot]) * weight
        grad = jnp.where(live, grad, 0.0)
        gate = gate_ref[i].astype(F32)
        up = up_ref[i].astype(F32)
        sig = 1.0 / (1.0 + jnp.exp(-gate))
        dgate_ref[i] = (grad * up * (sig * (1.0 + gate * (1.0 - sig)))).astype(BF)
        dup_ref[i] = (grad * gate * sig).astype(BF)


def partial_kernel(capacity, slot, groups, cut, *refs):
    members = sum(groups)
    pieces = len(groups)
    dgates, refs = refs[:pieces], refs[pieces:]
    dups, refs = refs[:pieces], refs[pieces:]
    extras, refs = refs[:members], refs[members:]
    (gate_a, gate_b, up_a, up_b, lora_gate, lora_up), refs = refs[:6], refs[6:]
    outs, refs = refs[: members + 1], refs[members + 1 :]
    low_out, lora_out, dgate, dup, low, tile = refs
    rank = lora_gate.shape[0]

    @pl.when(pl.program_id(0) == 0)
    def _():
        at = 0
        for size, dgate_ref, dup_ref in zip(groups, dgates, dups):
            for i in range(size):
                dgate[at : at + slot, :] = dgate_ref[i]
                dup[at : at + slot, :] = dup_ref[i]
                low[at : at + slot, :] = extras[at // slot][:slot, :rank]
                at += slot
        low_out[...] = SCALE * (dot(dgate[...], lora_gate[...], NT) + dot(dup[...], lora_up[...], NT))
        lora_out[:rank, :] = (SCALE * dot(low[...], dgate[...], TN)).astype(BF)
        lora_out[rank:, :] = (SCALE * dot(low[...], dup[...], TN)).astype(BF)

    first = dot(dgate[...], gate_a[...], NT) + dot(dup[...], up_a[...], NT)
    second = dot(dgate[...], gate_b[...], NT) + dot(dup[...], up_b[...], NT)
    for i in range(members):
        at = i * slot
        tile[:capacity, :] = first[at : at + capacity]
        tile[capacity:, :] = second[at : at + capacity]
        if i < members - 1:
            outs[i][...] = tile[...].astype(BF)
        else:
            outs[i][...] = tile[:cut, :].astype(BF)
            outs[i + 1][...] = tile[cut:, :].astype(BF)


def adapter_kernel(capacity, owner_ref, choice_ref, low_ref, tokens_ref, out_ref):
    upper, _ = pick_rows(choice_ref[...], capacity)
    low = dot(upper[: low_ref.shape[0]], low_ref[...], TN).astype(BF)
    out_ref[0] = dot(low, tokens_ref[...], TN).astype(BF)


def finish_kernel(capacity, choice_ref, left_ref, right_ref, own_ref, low_ref, down_ref, out_ref, low_tall):
    half = left_ref.shape[1]
    upper, lower = pick_rows(choice_ref[...], capacity)
    low = low_ref[...].astype(F32)[:capacity]
    zero = jnp.zeros_like(low)
    low_tall[:capacity, :] = low
    low_tall[capacity:, :] = zero
    low_upper = low_tall[...].astype(BF)
    low_tall[:capacity, :] = zero
    low_tall[capacity:, :] = low
    low_lower = low_tall[...].astype(BF)
    total = left_ref[...].astype(F32) + right_ref[...].astype(F32) + own_ref[...].astype(F32)
    total += dot(low_upper, down_ref[:, :half]) + dot(low_lower, down_ref[:, half:])
    total = total.astype(BF)
    out_ref[:, :half] = dot(upper, total, TN).astype(BF)
    out_ref[:, half:] = dot(lower, total, TN).astype(BF)


def params():
    return pltpu.CompilerParams(vmem_limit_bytes=VMEM_LIMIT)


def cost(flops, moved):
    return pl.CostEstimate(flops=int(flops), bytes_accessed=int(moved), transcendentals=0)


def on_device(
    ring,
    tokens,
    output_gradient,
    token_expert_choice,
    routing_weight_table,
    stored_gate_rows,
    stored_up_rows,
    gate_weight,
    up_weight,
    down_weight,
    adapter_down_factor,
    adapter_gate_factor,
    adapter_up_factor,
):
    n = len(ring)
    tokens, output_gradient = tokens[0], output_gradient[0]
    own_count, width = tokens.shape
    half = width // 2
    capacity = stored_gate_rows.shape[1] // n
    hidden = stored_gate_rows.shape[2]
    rank = adapter_down_factor.shape[0]
    tall = -(-2 * capacity // 16) * 16
    slot = -(-capacity // 8) * 8
    cut = capacity // 16 * 16
    wide = half + 2 * rank
    middle = n // 2
    choice = token_expert_choice[0].T
    weights = routing_weight_table[0].T

    me = lax.axis_index("expert")
    core = lax.axis_index("dp")
    place = [0] * n
    for i, e in enumerate(ring):
        place[e] = i
    to_right = [(ring[i], ring[(i + 1) % n]) for i in range(n)]
    to_left = [(ring[i], ring[(i - 1) % n]) for i in range(n)]
    passes = [[0, -1, 1]] + [[-s, s] for s in range(2, middle)] + [[middle]]
    order = [r for group in passes for r in group]
    owners = jnp.array(
        [[ring[(place[e] + r) % n] for r in order] for e in range(n)], jnp.int32
    )[me]
    paired = jnp.array(
        [[[(place[e ^ x] - place[e] - r) % n for r in order].index(0) for x in range(n)] for e in range(n)],
        jnp.int32,
    )[me]

    block = pl.pallas_call(
        functools.partial(prepare_kernel, capacity),
        out_shape=jax.ShapeDtypeStruct((2 * capacity, wide), BF),
        compiler_params=params(),
        cost_estimate=cost(4e8, 4.5e6),
        name="prepare",
    )(choice, weights, output_gradient, tokens, adapter_down_factor)

    def in_order(stored):
        rows = stored[0].reshape(n, capacity, hidden)[owners]
        return jnp.pad(rows, ((0, 0), (0, slot - capacity), (0, 0)))

    gate_rows, up_rows = in_order(stored_gate_rows), in_order(stored_up_rows)

    got = {0: block}
    rightward = leftward = block
    for s in range(1, middle):
        rightward = lax.ppermute(rightward, "expert", to_right)
        leftward = lax.ppermute(leftward, "expert", to_left)
        got[-s], got[s] = rightward, leftward
    got[middle] = jnp.concatenate(
        [
            lax.ppermute(rightward[:cut], "expert", to_right),
            lax.ppermute(leftward[cut:], "expert", to_left),
        ],
        axis=0,
    )

    columns = 256
    dgates, dups = [], []
    start = 0
    for group in passes:
        size = len(group)
        grads = jax.ShapeDtypeStruct((size, slot, hidden), BF)
        row_spec = pl.BlockSpec((size, slot, columns), lambda i: (0, 0, i))
        dgate, dup = pl.pallas_call(
            functools.partial(hidden_kernel, capacity, slot, size),
            grid=(hidden // columns,),
            in_specs=[pl.BlockSpec((2 * capacity, wide), lambda i: (0, 0))] * size
            + [row_spec, row_spec, pl.BlockSpec((columns, width), lambda i: (i, 0))],
            out_specs=[row_spec, row_spec],
            out_shape=[grads, grads],
            scratch_shapes=[pltpu.VMEM((size * tall, half), BF)],
            compiler_params=params(),
            cost_estimate=cost(2 * size * tall * width * hidden, 2 * hidden * width),
            name="hidden_rows",
        )(
            *[got[r] for r in group],
            gate_rows[start : start + size],
            up_rows[start : start + size],
            down_weight,
        )
        dgates.append(dgate)
        dups.append(dup)
        start += size

    steps = half // columns
    sizes = [len(group) for group in passes]
    whole = lambda shape: pl.BlockSpec(shape, lambda i: (0,) * len(shape))
    part_a = pl.BlockSpec((columns, hidden), lambda i: (i, 0))
    part_b = pl.BlockSpec((columns, hidden), lambda i: (i + steps, 0))
    heights = [2 * capacity] * (n - 1) + [cut, 2 * capacity - cut]
    results = pl.pallas_call(
        functools.partial(partial_kernel, capacity, slot, sizes, cut),
        grid=(steps,),
        in_specs=[whole((s, slot, hidden)) for s in sizes] * 2
        + [pl.BlockSpec((2 * capacity, 2 * rank), lambda i: (0, half // (2 * rank)))] * n
        + [part_a, part_b, part_a, part_b]
        + [whole((rank, hidden))] * 2,
        out_specs=[pl.BlockSpec((h, columns), lambda i: (0, i)) for h in heights]
        + [whole((n * slot, rank)), whole((2 * rank, hidden))],
        out_shape=[jax.ShapeDtypeStruct((h, half), BF) for h in heights]
        + [
            jax.ShapeDtypeStruct((n * slot, rank), F32),
            jax.ShapeDtypeStruct((2 * rank, hidden), BF),
        ],
        scratch_shapes=[
            pltpu.VMEM((n * slot, hidden), BF),
            pltpu.VMEM((n * slot, hidden), BF),
            pltpu.VMEM((n * slot, rank), BF),
            pltpu.VMEM((2 * capacity, columns), F32),
        ],
        compiler_params=params(),
        cost_estimate=cost(4 * n * slot * width * hidden, 4 * hidden * width),
        name="partials",
    )(
        *dgates,
        *dups,
        *[got[r] for r in order],
        gate_weight,
        gate_weight,
        up_weight,
        up_weight,
        adapter_gate_factor,
        adapter_up_factor,
    )
    own = dict(zip(order[:-1], results))
    last_a, last_b, low_part, lora_local = results[n - 1 :]

    def add(a, b):
        return (a.astype(F32) + b.astype(F32)).astype(BF)

    going_right = lax.ppermute(last_a, "expert", to_right)
    going_left = lax.ppermute(last_b, "expert", to_left)

    low = low_part.reshape(n, slot, rank)[paired]
    bit = 1
    while bit < n:
        pairs = low.reshape(low.shape[0] // 2, 2, slot, rank)
        other = lax.ppermute(pairs[:, 1], "expert", [(e, e ^ bit) for e in range(n)])
        low = pairs[:, 0] + other
        bit *= 2
    low = low[0].astype(BF)

    own_right = own[middle - 1]
    own_left = own[-(middle - 1)]
    going_right = jnp.concatenate(
        [add(own_right[:cut], going_right), own_right[cut:]], axis=0
    )
    going_left = jnp.concatenate([own_left[:cut], add(own_left[cut:], going_left)], axis=0)
    for s in range(middle - 1, 0, -1):
        going_right = lax.ppermute(going_right, "expert", to_right)
        going_left = lax.ppermute(going_left, "expert", to_left)
        if s > 1:
            going_right = add(going_right, own[s - 1])
            going_left = add(going_left, own[-(s - 1)])

    share = width // n
    columns_of = jnp.arange(n, dtype=jnp.int32) ^ me
    if share % 128 == 0:
        down = pl.pallas_call(
            functools.partial(adapter_kernel, capacity),
            grid_spec=pltpu.PrefetchScalarGridSpec(
                num_scalar_prefetch=1,
                grid=(n,),
                in_specs=[
                    pl.BlockSpec(choice.shape, lambda i, o: (0, 0)),
                    pl.BlockSpec((slot, rank), lambda i, o: (0, 0)),
                    pl.BlockSpec((own_count, share), lambda i, o: (0, o[i])),
                ],
                out_specs=pl.BlockSpec((1, rank, share), lambda i, o: (i, 0, 0)),
            ),
            out_shape=jax.ShapeDtypeStruct((n, rank, share), BF),
            compiler_params=params(),
            cost_estimate=cost(2 * own_count * rank * width, 2 * own_count * width),
            name="adapter_gradient",
        )(columns_of, choice, low, tokens)
    else:
        upper, _ = pick_rows(choice, capacity)
        low_tokens = dot(upper[:slot], low, TN).astype(BF)
        down = dot(low_tokens, tokens, TN).astype(BF).reshape(rank, n, share)
        down = down.transpose(1, 0, 2)[columns_of]

    swap = [(0, 1), (1, 0)]
    part = rank // 2
    keep = jnp.where(core == 0, down[:, :part], down[:, part:])
    send = jnp.where(core == 0, down[:, part:], down[:, :part])
    down = add(keep, lax.ppermute(send, "dp", swap))
    lora = lora_local.astype(F32) + lax.ppermute(lora_local, "dp", swap).astype(F32)
    bit = 1
    while bit < n:
        pairs = down.reshape(down.shape[0] // 2, 2, part, share)
        other = lax.ppermute(pairs[:, 1], "expert", [(e, e ^ bit) for e in range(n)])
        down = add(pairs[:, 0], other)
        bit *= 2
    down = down[0]
    there = lax.ppermute(down, "dp", swap)
    grad_down = jnp.where(
        core == 0, jnp.concatenate([down, there]), jnp.concatenate([there, down])
    ).astype(F32)

    input_gradient = pl.pallas_call(
        functools.partial(finish_kernel, capacity),
        out_shape=jax.ShapeDtypeStruct((own_count, width), BF),
        scratch_shapes=[pltpu.VMEM((2 * capacity, rank), F32)],
        compiler_params=params(),
        cost_estimate=cost(4e8, 4.5e6),
        name="finish",
    )(choice, going_right, going_left, own[0], low, adapter_down_factor)
    return (input_gradient[None], grad_down, lora[:rank], lora[rank:])


def solution(mesh):
    placed = (
        P(("groups", "dp"), "expert", None),
        P(("groups", "dp"), "expert", None),
        P(("groups", "dp"), "expert", None),
        P(("groups", "dp"), "expert", None),
        P(("groups", "dp"), None, "expert"),
        P(("groups", "dp"), None, "expert"),
        P(None, "expert"),
        P(None, "expert"),
        P("expert", None),
        P("groups", None),
        P("groups", "expert"),
        P("groups", "expert"),
    )
    return jax.shard_map(
        functools.partial(on_device, ring_order(mesh)),
        mesh=mesh,
        in_specs=placed,
        out_specs=(
            P(("groups", "dp"), "expert", None),
            P("groups", "expert"),
            P("groups", "expert"),
            P("groups", "expert"),
        ),
        check_vma=False,
    )
```

```python
import functools

import jax
import jax.numpy as jnp
from jax import lax
from jax.experimental import pallas as pl
from jax.experimental.pallas import tpu as pltpu
from jax.sharding import PartitionSpec as P

SCALE = 0.25
NT = (((1,), (1,)), ((), ()))
TN = (((0,), (0,)), ((), ()))
BF = jnp.bfloat16
F32 = jnp.float32
VMEM_LIMIT = 20 * 1024 * 1024
TILE = 256


def ring_order(mesh):
    count = mesh.shape["expert"]
    plain = list(range(count))
    if count < 4 or count % 2:
        return plain
    snake = list(range(0, count, 2)) + list(range(count - 1, 0, -2))
    spots = [getattr(d, "coords", None) for d in mesh.devices[0, :, 0]]
    if any(s is None for s in spots):
        return snake if count == 8 else plain

    def length(order):
        hops = zip(order, order[1:] + order[:1])
        return sum(sum(abs(a - b) for a, b in zip(spots[i], spots[j])) for i, j in hops)

    return min((plain, snake), key=length)


def dot(a, b, dims=None):
    if dims is None:
        dims = (((1,), (0,)), ((), ()))
    return lax.dot_general(a, b, dims, preferred_element_type=F32)


def pick_rows(choice, capacity):
    tokens = choice.shape[1]
    named = jnp.max((choice == 0).astype(F32), axis=0, keepdims=True)
    before = lax.broadcasted_iota(jnp.int32, (tokens, tokens), 0)
    after = lax.broadcasted_iota(jnp.int32, (tokens, tokens), 1)
    upto = (before <= after).astype(BF)
    count = dot(jnp.broadcast_to(named, (8, tokens)).astype(BF), upto)[:1]
    slot = jnp.where(named > 0, count - 1.0, -1000.0).astype(jnp.int32)
    row = lax.broadcasted_iota(jnp.int32, (2 * capacity, tokens), 0)
    return (row == slot).astype(BF), (row - capacity == slot).astype(BF)


def prepare_kernel(capacity, choice_hbm, weight_hbm, grad_hbm, tokens_hbm, down_hbm, block_ref,
                   choice_ref, weight_ref, grad_ref, tokens_ref, down_ref, sems):
    half = grad_ref.shape[1] // 2
    rank = down_ref.shape[0]
    pairs = [
        (choice_hbm, choice_ref),
        (grad_hbm.at[:, :half], grad_ref.at[:, :half]),
        (grad_hbm.at[:, half:], grad_ref.at[:, half:]),
        (weight_hbm, weight_ref),
        (down_hbm, down_ref),
        (tokens_hbm, tokens_ref),
    ]
    copies = [pltpu.make_async_copy(a, b, sems.at[i]) for i, (a, b) in enumerate(pairs)]
    for copy in copies:
        copy.start()
    copies[0].wait()
    choice = choice_ref[...]
    upper, lower = pick_rows(choice, capacity)
    copies[1].wait()
    first = dot(upper, grad_ref[:, :half])
    copies[2].wait()
    block_ref[:, :half] = (first + dot(lower, grad_ref[:, half:])).astype(BF)
    copies[3].wait()
    weight = jnp.sum(
        jnp.where(choice == 0, weight_ref[...].astype(F32), 0.0), axis=0, keepdims=True
    )
    column = jnp.sum(upper.astype(F32) * weight, axis=1, keepdims=True)
    block_ref[:, half + rank :] = jnp.broadcast_to(column, (2 * capacity, rank)).astype(BF)
    copies[4].wait()
    copies[5].wait()
    low = dot(tokens_ref[...], down_ref[...], NT).astype(BF)
    block_ref[:, half : half + rank] = dot(upper, low).astype(BF)


def hidden_kernel(capacity, slot, count, *refs):
    blocks, (gate_ref, up_ref, down_ref, dgate_ref, dup_ref, rows) = refs[:count], refs[count:]
    hidden, width = down_ref.shape
    half = width // 2
    rank = (blocks[0].shape[1] - half) // 2
    tall = rows.shape[0] // count
    for i, block in enumerate(blocks):
        rows[i * tall : i * tall + 2 * capacity, :] = block[:, :half]
    step = TILE if hidden % TILE == 0 else hidden
    live = lax.broadcasted_iota(jnp.int32, (slot, step), 0) < capacity
    for t in range(0, hidden, step):
        first = dot(rows[...], down_ref[t : t + step, :half], NT)
        second = dot(rows[...], down_ref[t : t + step, half:], NT)
        for i, block in enumerate(blocks):
            at = i * tall
            weight = block[:, half:].astype(F32)[:slot, rank : rank + 1]
            grad = (first[at : at + slot] + second[at + capacity : at + capacity + slot]) * weight
            grad = jnp.where(live, grad, 0.0)
            gate = gate_ref[i, :, t : t + step].astype(F32)
            up = up_ref[i, :, t : t + step].astype(F32)
            sig = 1.0 / (1.0 + jnp.exp(-gate))
            slope = sig * (1.0 + gate * (1.0 - sig))
            dgate_ref[i, :, t : t + step] = (grad * up * slope).astype(BF)
            dup_ref[i, :, t : t + step] = (grad * gate * sig).astype(BF)


def stack(groups, slot, sources, target):
    at = 0
    for size, source in zip(groups, sources):
        for i in range(size):
            target[at : at + slot, :] = source[i]
            at += slot


def low_kernel(slot, groups, *refs):
    members, pieces = sum(groups), len(groups)
    dgates, dups, extras = refs[:pieces], refs[pieces : 2 * pieces], refs[2 * pieces : 2 * pieces + members]
    lora_gate, lora_up, low_out, lora_out, dgate, dup, low = refs[2 * pieces + members :]
    rank = lora_gate.shape[0]
    stack(groups, slot, dgates, dgate)
    stack(groups, slot, dups, dup)
    for i, extra in enumerate(extras):
        low[i * slot : (i + 1) * slot, :] = extra[:slot, :rank]
    low_out[...] = SCALE * (dot(dgate[...], lora_gate[...], NT) + dot(dup[...], lora_up[...], NT))
    lora_out[:rank, :] = (SCALE * dot(low[...], dgate[...], TN)).astype(BF)
    lora_out[rank:, :] = (SCALE * dot(low[...], dup[...], TN)).astype(BF)


def partial_kernel(capacity, slot, groups, cut, *refs):
    members, pieces = sum(groups), len(groups)
    dgates, dups, refs = refs[:pieces], refs[pieces : 2 * pieces], refs[2 * pieces :]
    gate_ref, up_ref, outs, (dgate, dup, tile) = refs[0], refs[1], refs[2:-3], refs[-3:]
    half = gate_ref.shape[0] // 2
    stack(groups, slot, dgates, dgate)
    stack(groups, slot, dups, dup)

    for t in range(0, half, TILE):
        sums = []
        for at in (t, t + half):
            sums.append(
                dot(dgate[...], gate_ref[at : at + TILE, :], NT)
                + dot(dup[...], up_ref[at : at + TILE, :], NT)
            )
        for i in range(members):
            at = i * slot
            tile[:capacity, :] = sums[0][at : at + capacity]
            tile[capacity:, :] = sums[1][at : at + capacity]
            if cut:
                outs[0][:, t : t + TILE] = tile[:cut, :].astype(BF)
                outs[1][:, t : t + TILE] = tile[cut:, :].astype(BF)
            else:
                outs[i][:, t : t + TILE] = tile[...].astype(BF)


def adapter_kernel(capacity, owner_ref, choice_ref, low_ref, tokens_ref, out_ref):
    upper, _ = pick_rows(choice_ref[...], capacity)
    low = dot(upper[: low_ref.shape[0]], low_ref[...], TN).astype(BF)
    out_ref[0] = dot(low, tokens_ref[...], TN).astype(BF)


def finish_kernel(capacity, choice_ref, left_ref, right_ref, own_ref, low_ref, down_ref, out_ref, low_tall):
    half = left_ref.shape[1]
    upper, lower = pick_rows(choice_ref[...], capacity)
    low = low_ref[...].astype(F32)[:capacity]
    zero = jnp.zeros_like(low)
    low_tall[:capacity, :] = low
    low_tall[capacity:, :] = zero
    low_upper = low_tall[...].astype(BF)
    low_tall[:capacity, :] = zero
    low_tall[capacity:, :] = low
    low_lower = low_tall[...].astype(BF)
    total = left_ref[...].astype(F32) + right_ref[...].astype(F32) + own_ref[...].astype(F32)
    total += dot(low_upper, down_ref[:, :half]) + dot(low_lower, down_ref[:, half:])
    total = total.astype(BF)
    out_ref[:, :half] = dot(upper, total, TN).astype(BF)
    out_ref[:, half:] = dot(lower, total, TN).astype(BF)


def in_hbm(x):
    return pltpu.with_memory_space_constraint(x, pltpu.HBM)


def in_vmem(x):
    return pltpu.with_memory_space_constraint(x, pltpu.VMEM)


def params():
    return pltpu.CompilerParams(vmem_limit_bytes=VMEM_LIMIT)


def cost(flops, moved):
    return pl.CostEstimate(flops=int(flops), bytes_accessed=int(moved), transcendentals=0)


def on_device(
    ring,
    tokens,
    output_gradient,
    token_expert_choice,
    routing_weight_table,
    stored_gate_rows,
    stored_up_rows,
    gate_weight,
    up_weight,
    down_weight,
    adapter_down_factor,
    adapter_gate_factor,
    adapter_up_factor,
):
    n = len(ring)
    tokens, output_gradient = tokens[0], output_gradient[0]
    own_count, width = tokens.shape
    half = width // 2
    capacity = stored_gate_rows.shape[1] // n
    hidden = stored_gate_rows.shape[2]
    rank = adapter_down_factor.shape[0]
    tall = -(-2 * capacity // 16) * 16
    slot = -(-capacity // 8) * 8
    cut = capacity // 16 * 16
    wide = half + 2 * rank
    middle = n // 2
    choice = token_expert_choice[0].T
    weights = routing_weight_table[0].T

    me = lax.axis_index("expert")
    core = lax.axis_index("dp")
    place = [0] * n
    for i, e in enumerate(ring):
        place[e] = i
    to_right = [(ring[i], ring[(i + 1) % n]) for i in range(n)]
    to_left = [(ring[i], ring[(i - 1) % n]) for i in range(n)]
    passes = [[0, -1, 1]] + [[-s, s] for s in range(2, middle)] + [[middle]]
    order = [r for group in passes for r in group]
    owners = jnp.array(
        [[ring[(place[e] + r) % n] for r in order] for e in range(n)], jnp.int32
    )[me]
    paired = jnp.array(
        [[[(place[e ^ x] - place[e] - r) % n for r in order].index(0) for x in range(n)] for e in range(n)],
        jnp.int32,
    )[me]

    block = pl.pallas_call(
        functools.partial(prepare_kernel, capacity),
        in_specs=[pl.BlockSpec(memory_space=pl.ANY)] * 5,
        out_shape=jax.ShapeDtypeStruct((2 * capacity, wide), BF),
        scratch_shapes=[
            pltpu.VMEM(choice.shape, choice.dtype),
            pltpu.VMEM(weights.shape, BF),
            pltpu.VMEM(output_gradient.shape, BF),
            pltpu.VMEM(tokens.shape, BF),
            pltpu.VMEM(adapter_down_factor.shape, BF),
            pltpu.SemaphoreType.DMA((6,)),
        ],
        compiler_params=params(),
        cost_estimate=cost(4e8, 4.5e6),
        name="prepare",
    )(*[in_hbm(x) for x in (choice, weights, output_gradient, tokens, adapter_down_factor)])

    def in_order(stored):
        rows = stored[0].reshape(n, capacity, hidden)[owners]
        return jnp.pad(rows, ((0, 0), (0, slot - capacity), (0, 0)))

    gate_rows, up_rows = in_order(stored_gate_rows), in_order(stored_up_rows)

    got = {0: block}
    rightward = leftward = block
    for s in range(1, middle):
        rightward = lax.ppermute(rightward, "expert", to_right)
        leftward = lax.ppermute(leftward, "expert", to_left)
        got[-s], got[s] = rightward, leftward
    got[middle] = jnp.concatenate(
        [
            lax.ppermute(rightward[:cut], "expert", to_right),
            lax.ppermute(leftward[cut:], "expert", to_left),
        ],
        axis=0,
    )

    down_here, gate_here, up_here = in_vmem(down_weight), in_vmem(gate_weight), in_vmem(up_weight)
    dgates, dups = [], []
    start = 0
    for group in passes:
        size = len(group)
        grads = jax.ShapeDtypeStruct((size, slot, hidden), BF)
        dgate, dup = pl.pallas_call(
            functools.partial(hidden_kernel, capacity, slot, size),
            out_shape=[grads, grads],
            scratch_shapes=[pltpu.VMEM((size * tall, half), BF)],
            compiler_params=params(),
            cost_estimate=cost(2 * size * tall * width * hidden, 2 * hidden * width),
            name="hidden_rows",
        )(
            *[got[r] for r in group],
            gate_rows[start : start + size],
            up_rows[start : start + size],
            down_here,
        )
        dgates.append(dgate)
        dups.append(dup)
        start += size

    sizes = [len(group) for group in passes]
    low_part, lora_local = pl.pallas_call(
        functools.partial(low_kernel, slot, sizes),
        out_shape=[
            jax.ShapeDtypeStruct((n * slot, rank), F32),
            jax.ShapeDtypeStruct((2 * rank, hidden), BF),
        ],
        scratch_shapes=[
            pltpu.VMEM((n * slot, hidden), BF),
            pltpu.VMEM((n * slot, hidden), BF),
            pltpu.VMEM((n * slot, rank), BF),
        ],
        compiler_params=params(),
        cost_estimate=cost(8 * n * slot * rank * hidden, 4 * n * slot * hidden),
        name="low_rows",
    )(*dgates, *dups, *[got[r][:, half:] for r in order], adapter_gate_factor, adapter_up_factor)

    def partials(some, heights):
        count = sum(sizes[i] for i in some)
        return pl.pallas_call(
            functools.partial(
                partial_kernel, capacity, slot, [sizes[i] for i in some], cut if len(heights) > count else 0
            ),
            out_shape=[jax.ShapeDtypeStruct((h, half), BF) for h in heights],
            scratch_shapes=[
                pltpu.VMEM((count * slot, hidden), BF),
                pltpu.VMEM((count * slot, hidden), BF),
                pltpu.VMEM((2 * capacity, TILE), F32),
            ],
            compiler_params=params(),
            cost_estimate=cost(4 * count * slot * width * hidden, 4 * hidden * width),
            name="partials",
        )(*[dgates[i] for i in some], *[dups[i] for i in some], gate_here, up_here)

    last_a, last_b = partials([len(passes) - 1], [cut, 2 * capacity - cut])
    rest = list(range(len(passes) - 1))
    own = dict(zip(order[:-1], partials(rest, [2 * capacity] * (n - 1))))

    def add(a, b):
        return (a.astype(F32) + b.astype(F32)).astype(BF)

    going_right = lax.ppermute(last_a, "expert", to_right)
    going_left = lax.ppermute(last_b, "expert", to_left)

    low_part, going_right, going_left = lax.optimization_barrier((low_part, going_right, going_left))
    low = low_part.reshape(n, slot, rank)[paired]
    bit = 1
    while bit < n:
        pairs = low.reshape(low.shape[0] // 2, 2, slot, rank)
        other = lax.ppermute(pairs[:, 1], "expert", [(e, e ^ bit) for e in range(n)])
        low = pairs[:, 0] + other
        bit *= 2
    low = low[0].astype(BF)

    own_right = own[middle - 1]
    own_left = own[-(middle - 1)]
    going_right = jnp.concatenate(
        [add(own_right[:cut], going_right), own_right[cut:]], axis=0
    )
    going_left = jnp.concatenate([own_left[:cut], add(own_left[cut:], going_left)], axis=0)
    for s in range(middle - 1, 0, -1):
        going_right = lax.ppermute(going_right, "expert", to_right)
        going_left = lax.ppermute(going_left, "expert", to_left)
        if s > 1:
            going_right = add(going_right, own[s - 1])
            going_left = add(going_left, own[-(s - 1)])

    share = width // n
    columns_of = jnp.arange(n, dtype=jnp.int32) ^ me
    if share % 128 == 0:
        down = pl.pallas_call(
            functools.partial(adapter_kernel, capacity),
            grid_spec=pltpu.PrefetchScalarGridSpec(
                num_scalar_prefetch=1,
                grid=(n,),
                in_specs=[
                    pl.BlockSpec(choice.shape, lambda i, o: (0, 0)),
                    pl.BlockSpec((slot, rank), lambda i, o: (0, 0)),
                    pl.BlockSpec((own_count, share), lambda i, o: (0, o[i])),
                ],
                out_specs=pl.BlockSpec((1, rank, share), lambda i, o: (i, 0, 0)),
            ),
            out_shape=jax.ShapeDtypeStruct((n, rank, share), BF),
            compiler_params=params(),
            cost_estimate=cost(2 * own_count * rank * width, 2 * own_count * width),
            name="adapter_gradient",
        )(columns_of, choice, low, tokens)
    else:
        upper, _ = pick_rows(choice, capacity)
        low_tokens = dot(upper[:slot], low, TN).astype(BF)
        down = dot(low_tokens, tokens, TN).astype(BF).reshape(rank, n, share)
        down = down.transpose(1, 0, 2)[columns_of]

    swap = [(0, 1), (1, 0)]
    part = rank // 2
    keep = jnp.where(core == 0, down[:, :part], down[:, part:])
    send = jnp.where(core == 0, down[:, part:], down[:, :part])
    down = add(keep, lax.ppermute(send, "dp", swap))
    lora = lora_local.astype(F32) + lax.ppermute(lora_local, "dp", swap).astype(F32)
    bit = 1
    while bit < n:
        pairs = down.reshape(down.shape[0] // 2, 2, part, share)
        other = lax.ppermute(pairs[:, 1], "expert", [(e, e ^ bit) for e in range(n)])
        down = add(pairs[:, 0], other)
        bit *= 2
    down = down[0]
    there = lax.ppermute(down, "dp", swap)
    grad_down = jnp.where(
        core == 0, jnp.concatenate([down, there]), jnp.concatenate([there, down])
    ).astype(F32)

    input_gradient = pl.pallas_call(
        functools.partial(finish_kernel, capacity),
        out_shape=jax.ShapeDtypeStruct((own_count, width), BF),
        scratch_shapes=[pltpu.VMEM((2 * capacity, rank), F32)],
        compiler_params=params(),
        cost_estimate=cost(4e8, 4.5e6),
        name="finish",
    )(choice, going_right, going_left, own[0], low, adapter_down_factor)
    return (input_gradient[None], grad_down, lora[:rank], lora[rank:])


def solution(mesh):
    placed = (
        P(("groups", "dp"), "expert", None),
        P(("groups", "dp"), "expert", None),
        P(("groups", "dp"), "expert", None),
        P(("groups", "dp"), "expert", None),
        P(("groups", "dp"), None, "expert"),
        P(("groups", "dp"), None, "expert"),
        P(None, "expert"),
        P(None, "expert"),
        P("expert", None),
        P("groups", None),
        P("groups", "expert"),
        P("groups", "expert"),
    )
    return jax.shard_map(
        functools.partial(on_device, ring_order(mesh)),
        mesh=mesh,
        in_specs=placed,
        out_specs=(
            P(("groups", "dp"), "expert", None),
            P("groups", "expert"),
            P("groups", "expert"),
            P("groups", "expert"),
        ),
        check_vma=False,
    )
```

```python
import functools

import jax
import jax.numpy as jnp
from jax import lax
from jax.experimental import pallas as pl
from jax.experimental.pallas import tpu as pltpu
from jax.sharding import PartitionSpec as P

SCALE = 0.25
NT = (((1,), (1,)), ((), ()))
TN = (((0,), (0,)), ((), ()))
BF = jnp.bfloat16
F32 = jnp.float32
VMEM_LIMIT = 20 * 1024 * 1024
TILE = 256


def ring_order(mesh):
    count = mesh.shape["expert"]
    plain = list(range(count))
    if count < 4 or count % 2:
        return plain
    snake = list(range(0, count, 2)) + list(range(count - 1, 0, -2))
    spots = [getattr(d, "coords", None) for d in mesh.devices[0, :, 0]]
    if any(s is None for s in spots):
        return snake if count == 8 else plain

    def length(order):
        hops = zip(order, order[1:] + order[:1])
        return sum(sum(abs(a - b) for a, b in zip(spots[i], spots[j])) for i, j in hops)

    return min((plain, snake), key=length)


def dot(a, b, dims=None):
    if dims is None:
        dims = (((1,), (0,)), ((), ()))
    return lax.dot_general(a, b, dims, preferred_element_type=F32)


def pick_rows(choice, capacity):
    tokens = choice.shape[1]
    named = jnp.max((choice == 0).astype(F32), axis=0, keepdims=True)
    before = lax.broadcasted_iota(jnp.int32, (tokens, tokens), 0)
    after = lax.broadcasted_iota(jnp.int32, (tokens, tokens), 1)
    upto = (before <= after).astype(BF)
    count = dot(jnp.broadcast_to(named, (8, tokens)).astype(BF), upto)[:1]
    slot = jnp.where(named > 0, count - 1.0, -1000.0).astype(jnp.int32)
    row = lax.broadcasted_iota(jnp.int32, (2 * capacity, tokens), 0)
    return (row == slot).astype(BF), (row - capacity == slot).astype(BF)


def prepare_kernel(capacity, choice_hbm, weight_hbm, grad_hbm, tokens_hbm, down_hbm, block_ref,
                   choice_ref, weight_ref, grad_ref, tokens_ref, down_ref, sems):
    half = grad_ref.shape[1] // 2
    rank = down_ref.shape[0]
    pairs = [
        (choice_hbm, choice_ref),
        (grad_hbm.at[:, :half], grad_ref.at[:, :half]),
        (grad_hbm.at[:, half:], grad_ref.at[:, half:]),
        (weight_hbm, weight_ref),
        (down_hbm, down_ref),
        (tokens_hbm, tokens_ref),
    ]
    copies = [pltpu.make_async_copy(a, b, sems.at[i]) for i, (a, b) in enumerate(pairs)]
    for copy in copies:
        copy.start()
    copies[0].wait()
    choice = choice_ref[...]
    upper, lower = pick_rows(choice, capacity)
    copies[1].wait()
    first = dot(upper, grad_ref[:, :half])
    copies[2].wait()
    block_ref[:, :half] = (first + dot(lower, grad_ref[:, half:])).astype(BF)
    copies[3].wait()
    weight = jnp.sum(
        jnp.where(choice == 0, weight_ref[...].astype(F32), 0.0), axis=0, keepdims=True
    )
    column = jnp.sum(upper.astype(F32) * weight, axis=1, keepdims=True)
    block_ref[:, half + rank :] = jnp.broadcast_to(column, (2 * capacity, rank)).astype(BF)
    copies[4].wait()
    copies[5].wait()
    low = dot(tokens_ref[...], down_ref[...], NT).astype(BF)
    block_ref[:, half : half + rank] = dot(upper, low).astype(BF)


def hidden_kernel(capacity, slot, count, *refs):
    blocks, refs = refs[:count], refs[count:]
    (gate_ref, up_ref, down_ref, lora_gate, lora_up, dgate_ref, dup_ref), refs = refs[:7], refs[7:]
    lows, rows = refs[:count], refs[count]
    hidden, width = down_ref.shape
    half = width // 2
    rank = lora_gate.shape[0]
    tall = rows.shape[0] // count
    for i, block in enumerate(blocks):
        rows[i * tall : i * tall + 2 * capacity, :] = block[:, :half]
    step = TILE if hidden % TILE == 0 else hidden
    live = lax.broadcasted_iota(jnp.int32, (slot, step), 0) < capacity
    for t in range(0, hidden, step):
        first = dot(rows[...], down_ref[t : t + step, :half], NT)
        second = dot(rows[...], down_ref[t : t + step, half:], NT)
        for i, block in enumerate(blocks):
            at = i * tall
            weight = block[:, half:].astype(F32)[:slot, rank : rank + 1]
            grad = (first[at : at + slot] + second[at + capacity : at + capacity + slot]) * weight
            grad = jnp.where(live, grad, 0.0)
            gate = gate_ref[i, :, t : t + step].astype(F32)
            up = up_ref[i, :, t : t + step].astype(F32)
            sig = 1.0 / (1.0 + jnp.exp(-gate))
            slope = sig * (1.0 + gate * (1.0 - sig))
            dgate_ref[i, :, t : t + step] = (grad * up * slope).astype(BF)
            dup_ref[i, :, t : t + step] = (grad * gate * sig).astype(BF)
    for i in range(count):
        lows[i][...] = SCALE * (dot(dgate_ref[i], lora_gate[...], NT) + dot(dup_ref[i], lora_up[...], NT))


def stack(groups, slot, sources, target):
    at = 0
    for size, source in zip(groups, sources):
        for i in range(size):
            target[at : at + slot, :] = source[i]
            at += slot


def lora_kernel(slot, groups, *refs):
    members, pieces = sum(groups), len(groups)
    dgates, dups, extras = refs[:pieces], refs[pieces : 2 * pieces], refs[2 * pieces : 2 * pieces + members]
    lora_out, dgate, dup, low = refs[2 * pieces + members :]
    rank = lora_out.shape[0] // 2
    stack(groups, slot, dgates, dgate)
    stack(groups, slot, dups, dup)
    for i, extra in enumerate(extras):
        low[i * slot : (i + 1) * slot, :] = extra[:slot, :rank]
    lora_out[:rank, :] = (SCALE * dot(low[...], dgate[...], TN)).astype(BF)
    lora_out[rank:, :] = (SCALE * dot(low[...], dup[...], TN)).astype(BF)


def partial_kernel(capacity, slot, groups, cut, *refs):
    members, pieces = sum(groups), len(groups)
    dgates, dups, refs = refs[:pieces], refs[pieces : 2 * pieces], refs[2 * pieces :]
    gate_ref, up_ref, outs, (dgate, dup, tile) = refs[0], refs[1], refs[2:-3], refs[-3:]
    half = gate_ref.shape[0] // 2
    stack(groups, slot, dgates, dgate)
    stack(groups, slot, dups, dup)

    for t in range(0, half, TILE):
        sums = []
        for at in (t, t + half):
            sums.append(
                dot(dgate[...], gate_ref[at : at + TILE, :], NT)
                + dot(dup[...], up_ref[at : at + TILE, :], NT)
            )
        for i in range(members):
            at = i * slot
            tile[:capacity, :] = sums[0][at : at + capacity]
            tile[capacity:, :] = sums[1][at : at + capacity]
            if cut:
                outs[0][:, t : t + TILE] = tile[:cut, :].astype(BF)
                outs[1][:, t : t + TILE] = tile[cut:, :].astype(BF)
            else:
                outs[i][:, t : t + TILE] = tile[...].astype(BF)


def merge_kernel(cut, upper, part_ref, own_ref, out_ref):
    span, other = (slice(0, cut), slice(cut, None)) if upper else (slice(cut, None), slice(0, cut))
    out_ref[span, :] = (part_ref[...].astype(F32) + own_ref[span, :].astype(F32)).astype(BF)
    out_ref[other, :] = own_ref[other, :]


def adapter_kernel(capacity, count, where_ref, choice_ref, tokens_ref, *refs):
    lows, (low_ref, keep_ref, send_ref) = refs[:count], refs[count:]
    share = keep_ref.shape[2]
    part = keep_ref.shape[1]
    low = lows[0][...]
    for other in lows[1:]:
        low = low + other[...]
    low = low.astype(BF)
    low_ref[...] = low
    upper, _ = pick_rows(choice_ref[...], capacity)
    low = dot(upper[: low.shape[0]], low, TN).astype(BF)
    core = where_ref[count]
    for i in range(count):
        columns = pl.ds(pl.multiple_of(where_ref[i] * share, 128), share)
        down = dot(low, tokens_ref[:, columns], TN)
        keep_ref[i] = jnp.where(core == 0, down[:part], down[part:]).astype(BF)
        send_ref[i] = jnp.where(core == 0, down[part:], down[:part]).astype(BF)


def finish_kernel(capacity, choice_ref, left_ref, right_ref, own_ref, low_ref, down_ref, out_ref, low_tall):
    half = left_ref.shape[1]
    upper, lower = pick_rows(choice_ref[...], capacity)
    low = low_ref[...].astype(F32)[:capacity]
    zero = jnp.zeros_like(low)
    low_tall[:capacity, :] = low
    low_tall[capacity:, :] = zero
    low_upper = low_tall[...].astype(BF)
    low_tall[:capacity, :] = zero
    low_tall[capacity:, :] = low
    low_lower = low_tall[...].astype(BF)
    total = left_ref[...].astype(F32) + right_ref[...].astype(F32) + own_ref[...].astype(F32)
    total += dot(low_upper, down_ref[:, :half]) + dot(low_lower, down_ref[:, half:])
    total = total.astype(BF)
    out_ref[:, :half] = dot(upper, total, TN).astype(BF)
    out_ref[:, half:] = dot(lower, total, TN).astype(BF)


def in_hbm(x):
    return pltpu.with_memory_space_constraint(x, pltpu.HBM)


def in_vmem(x):
    return pltpu.with_memory_space_constraint(x, pltpu.VMEM)


def params():
    return pltpu.CompilerParams(vmem_limit_bytes=VMEM_LIMIT)


def cost(flops, moved):
    return pl.CostEstimate(flops=int(flops), bytes_accessed=int(moved), transcendentals=0)


def on_device(
    ring,
    tokens,
    output_gradient,
    token_expert_choice,
    routing_weight_table,
    stored_gate_rows,
    stored_up_rows,
    gate_weight,
    up_weight,
    down_weight,
    adapter_down_factor,
    adapter_gate_factor,
    adapter_up_factor,
):
    n = len(ring)
    tokens, output_gradient = tokens[0], output_gradient[0]
    own_count, width = tokens.shape
    half = width // 2
    capacity = stored_gate_rows.shape[1] // n
    hidden = stored_gate_rows.shape[2]
    rank = adapter_down_factor.shape[0]
    tall = -(-2 * capacity // 16) * 16
    slot = -(-capacity // 8) * 8
    cut = capacity // 16 * 16
    wide = half + 2 * rank
    middle = n // 2
    choice = token_expert_choice[0].T
    weights = routing_weight_table[0].T

    me = lax.axis_index("expert")
    core = lax.axis_index("dp")
    place = [0] * n
    for i, e in enumerate(ring):
        place[e] = i
    to_right = [(ring[i], ring[(i + 1) % n]) for i in range(n)]
    to_left = [(ring[i], ring[(i - 1) % n]) for i in range(n)]
    passes = [[0]] + [[-s, s] for s in range(1, middle)] + [[middle]]
    order = [r for group in passes for r in group]
    owners = jnp.array(
        [[ring[(place[e] + r) % n] for r in order] for e in range(n)], jnp.int32
    )[me]
    block = pl.pallas_call(
        functools.partial(prepare_kernel, capacity),
        in_specs=[pl.BlockSpec(memory_space=pl.ANY)] * 5,
        out_shape=jax.ShapeDtypeStruct((2 * capacity, wide), BF),
        scratch_shapes=[
            pltpu.VMEM(choice.shape, choice.dtype),
            pltpu.VMEM(weights.shape, BF),
            pltpu.VMEM(output_gradient.shape, BF),
            pltpu.VMEM(tokens.shape, BF),
            pltpu.VMEM(adapter_down_factor.shape, BF),
            pltpu.SemaphoreType.DMA((6,)),
        ],
        compiler_params=params(),
        cost_estimate=cost(4e8, 4.5e6),
        name="prepare",
    )(*[in_hbm(x) for x in (choice, weights, output_gradient, tokens, adapter_down_factor)])

    def in_order(stored):
        rows = stored[0].reshape(n, capacity, hidden)[owners]
        return jnp.pad(rows, ((0, 0), (0, slot - capacity), (0, 0)))

    gate_rows, up_rows = in_order(stored_gate_rows), in_order(stored_up_rows)

    down_here, gate_here, up_here = in_vmem(down_weight), in_vmem(gate_weight), in_vmem(up_weight)
    dgates, dups, lows = [], [], []
    got = {0: block}

    def hidden_pass(group):
        size, start = len(group), len(lows)
        grads = jax.ShapeDtypeStruct((size, slot, hidden), BF)
        results = pl.pallas_call(
            functools.partial(hidden_kernel, capacity, slot, size),
            out_shape=[grads, grads] + [jax.ShapeDtypeStruct((slot, rank), F32)] * size,
            scratch_shapes=[pltpu.VMEM((size * tall, half), BF)],
            compiler_params=params(),
            cost_estimate=cost(2 * size * tall * width * hidden, 2 * hidden * width),
            name="hidden_rows",
        )(
            *[got[r] for r in group],
            gate_rows[start : start + size],
            up_rows[start : start + size],
            down_here,
            adapter_gate_factor,
            adapter_up_factor,
        )
        dgates.append(results[0])
        dups.append(results[1])
        for r, low in zip(group, results[2:]):
            pairs = [(ring[i], ring[(i + r) % n]) for i in range(n)]
            lows.append(lax.ppermute(low, "expert", pairs) if r else low)

    rightward = leftward = block
    for s in range(1, middle + 1):
        if s < middle:
            rightward = lax.ppermute(rightward, "expert", to_right)
            leftward = lax.ppermute(leftward, "expert", to_left)
        else:
            rightward = lax.ppermute(rightward[:cut], "expert", to_right)
            leftward = lax.ppermute(leftward[cut:], "expert", to_left)
        arrived = list(lows)
        hidden_pass(passes[s - 1])
        rightward, leftward, dgates[-1], dups[-1], arrived = lax.optimization_barrier(
            (rightward, leftward, dgates[-1], dups[-1], arrived)
        )
        lows[: len(arrived)] = arrived
        if s < middle:
            got[-s], got[s] = rightward, leftward
    got[middle] = jnp.concatenate([rightward, leftward], axis=0)
    hidden_pass(passes[-1])

    sizes = [len(group) for group in passes]
    def partials(some, heights):
        count = sum(sizes[i] for i in some)
        return pl.pallas_call(
            functools.partial(
                partial_kernel, capacity, slot, [sizes[i] for i in some], cut if len(heights) > count else 0
            ),
            out_shape=[jax.ShapeDtypeStruct((h, half), BF) for h in heights],
            scratch_shapes=[
                pltpu.VMEM((count * slot, hidden), BF),
                pltpu.VMEM((count * slot, hidden), BF),
                pltpu.VMEM((2 * capacity, TILE), F32),
            ],
            compiler_params=params(),
            cost_estimate=cost(4 * count * slot * width * hidden, 4 * hidden * width),
            name="partials",
        )(*[dgates[i] for i in some], *[dups[i] for i in some], gate_here, up_here)

    last_a, last_b = partials([len(passes) - 1], [cut, 2 * capacity - cut])
    rest = list(range(len(passes) - 1))
    own = partials(rest, [2 * capacity] * (n - 1))

    def add(a, b):
        return (a.astype(F32) + b.astype(F32)).astype(BF)

    going_right = lax.ppermute(last_a, "expert", to_right)
    going_left = lax.ppermute(last_b, "expert", to_left)


    going_right, going_left, own = lax.optimization_barrier((going_right, going_left, own))
    own = dict(zip(order[:-1], own))

    def merge(upper, part, mine):
        return pl.pallas_call(
            functools.partial(merge_kernel, cut, upper),
            out_shape=jax.ShapeDtypeStruct(mine.shape, BF),
            compiler_params=params(),
            cost_estimate=cost(mine.size, 6 * mine.size),
            name="first_add",
        )(part, mine)

    going_right = merge(True, going_right, own[middle - 1])
    going_left = merge(False, going_left, own[-(middle - 1)])
    for s in range(middle - 1, 0, -1):
        going_right = lax.ppermute(going_right, "expert", to_right)
        going_left = lax.ppermute(going_left, "expert", to_left)
        if s > 1:
            going_right = add(going_right, own[s - 1])
            going_left = add(going_left, own[-(s - 1)])

    share = width // n
    part = rank // 2
    columns_of = jnp.arange(n, dtype=jnp.int32) ^ me
    if share % 128 == 0:
        split = jax.ShapeDtypeStruct((n, part, share), BF)
        whole = pl.BlockSpec(memory_space=pltpu.VMEM)
        low, keep, send = pl.pallas_call(
            functools.partial(adapter_kernel, capacity, n),
            in_specs=[pl.BlockSpec(memory_space=pltpu.SMEM)] + [whole] * (n + 2),
            out_shape=[jax.ShapeDtypeStruct((slot, rank), BF), split, split],
            compiler_params=params(),
            cost_estimate=cost(2 * own_count * rank * width, 2 * own_count * width),
            name="adapter_gradient",
        )(jnp.append(columns_of, core), choice, tokens, *lows)
    else:
        upper, _ = pick_rows(choice, capacity)
        low = sum(lows).astype(BF)
        low_tokens = dot(upper[:slot], low, TN).astype(BF)
        down = dot(low_tokens, tokens, TN).astype(BF).reshape(rank, n, share)
        down = down.transpose(1, 0, 2)[columns_of]
        keep = jnp.where(core == 0, down[:, :part], down[:, part:])
        send = jnp.where(core == 0, down[:, part:], down[:, :part])

    swap = [(0, 1), (1, 0)]
    down = add(keep, lax.ppermute(send, "dp", swap))
    extras, _ = lax.optimization_barrier(([got[r][:, half:] for r in order], down))
    lora_local = pl.pallas_call(
        functools.partial(lora_kernel, slot, sizes),
        out_shape=jax.ShapeDtypeStruct((2 * rank, hidden), BF),
        scratch_shapes=[
            pltpu.VMEM((n * slot, hidden), BF),
            pltpu.VMEM((n * slot, hidden), BF),
            pltpu.VMEM((n * slot, rank), BF),
        ],
        compiler_params=params(),
        cost_estimate=cost(4 * n * slot * rank * hidden, 4 * n * slot * hidden),
        name="lora_rows",
    )(*dgates, *dups, *extras)

    lora = lora_local.astype(F32) + lax.ppermute(lora_local, "dp", swap).astype(F32)
    bit = 1
    while bit < n:
        pairs = down.reshape(down.shape[0] // 2, 2, part, share)
        other = lax.ppermute(pairs[:, 1], "expert", [(e, e ^ bit) for e in range(n)])
        down = add(pairs[:, 0], other)
        bit *= 2
    down = down[0]
    there = lax.ppermute(down, "dp", swap)
    grad_down = jnp.where(
        core == 0, jnp.concatenate([down, there]), jnp.concatenate([there, down])
    ).astype(F32)

    input_gradient = pl.pallas_call(
        functools.partial(finish_kernel, capacity),
        out_shape=jax.ShapeDtypeStruct((own_count, width), BF),
        scratch_shapes=[pltpu.VMEM((2 * capacity, rank), F32)],
        compiler_params=params(),
        cost_estimate=cost(4e8, 4.5e6),
        name="finish",
    )(choice, going_right, going_left, own[0], low, adapter_down_factor)
    return (input_gradient[None], grad_down, lora[:rank], lora[rank:])


def solution(mesh):
    placed = (
        P(("groups", "dp"), "expert", None),
        P(("groups", "dp"), "expert", None),
        P(("groups", "dp"), "expert", None),
        P(("groups", "dp"), "expert", None),
        P(("groups", "dp"), None, "expert"),
        P(("groups", "dp"), None, "expert"),
        P(None, "expert"),
        P(None, "expert"),
        P("expert", None),
        P("groups", None),
        P("groups", "expert"),
        P("groups", "expert"),
    )
    return jax.shard_map(
        functools.partial(on_device, ring_order(mesh)),
        mesh=mesh,
        in_specs=placed,
        out_specs=(
            P(("groups", "dp"), "expert", None),
            P("groups", "expert"),
            P("groups", "expert"),
            P("groups", "expert"),
        ),
        check_vma=False,
    )
```

```python
import functools

import jax
import jax.numpy as jnp
from jax import lax
from jax.experimental import pallas as pl
from jax.experimental.pallas import tpu as pltpu
from jax.sharding import PartitionSpec as P

SCALE = 0.25
NT = (((1,), (1,)), ((), ()))
TN = (((0,), (0,)), ((), ()))
BF = jnp.bfloat16
F32 = jnp.float32
VMEM_LIMIT = 10 * 1024 * 1024
TILE = 256


def ring_order(mesh):
    count = mesh.shape["expert"]
    plain = list(range(count))
    if count < 4 or count % 2:
        return plain
    snake = list(range(0, count, 2)) + list(range(count - 1, 0, -2))
    spots = [getattr(d, "coords", None) for d in mesh.devices[0, :, 0]]
    if any(s is None for s in spots):
        return snake if count == 8 else plain

    def length(order):
        hops = zip(order, order[1:] + order[:1])
        return sum(sum(abs(a - b) for a, b in zip(spots[i], spots[j])) for i, j in hops)

    return min((plain, snake), key=length)


def dot(a, b, dims=None):
    if dims is None:
        dims = (((1,), (0,)), ((), ()))
    return lax.dot_general(a, b, dims, preferred_element_type=F32)


def pick_rows(choice, capacity):
    tokens = choice.shape[1]
    named = jnp.max((choice == 0).astype(F32), axis=0, keepdims=True)
    before = lax.broadcasted_iota(jnp.int32, (tokens, tokens), 0)
    after = lax.broadcasted_iota(jnp.int32, (tokens, tokens), 1)
    upto = (before <= after).astype(BF)
    count = dot(jnp.broadcast_to(named, (8, tokens)).astype(BF), upto)[:1]
    slot = jnp.where(named > 0, count - 1.0, -1000.0).astype(jnp.int32)
    row = lax.broadcasted_iota(jnp.int32, (2 * capacity, tokens), 0)
    return (row == slot).astype(BF), (row - capacity == slot).astype(BF)


def prepare_kernel(capacity, choice_hbm, weight_hbm, grad_hbm, tokens_hbm, down_hbm, block_ref,
                   choice_ref, weight_ref, grad_ref, tokens_ref, down_ref, sems):
    half = grad_ref.shape[1] // 2
    rank = down_ref.shape[0]
    pairs = [
        (choice_hbm, choice_ref),
        (grad_hbm.at[:, :half], grad_ref.at[:, :half]),
        (grad_hbm.at[:, half:], grad_ref.at[:, half:]),
        (weight_hbm, weight_ref),
        (down_hbm, down_ref),
        (tokens_hbm, tokens_ref),
    ]
    copies = [pltpu.make_async_copy(a, b, sems.at[i]) for i, (a, b) in enumerate(pairs)]
    for copy in copies:
        copy.start()
    copies[0].wait()
    choice = choice_ref[...]
    upper, lower = pick_rows(choice, capacity)
    copies[1].wait()
    first = dot(upper, grad_ref[:, :half])
    copies[2].wait()
    block_ref[:, :half] = (first + dot(lower, grad_ref[:, half:])).astype(BF)
    copies[3].wait()
    weight = jnp.sum(
        jnp.where(choice == 0, weight_ref[...].astype(F32), 0.0), axis=0, keepdims=True
    )
    column = jnp.sum(upper.astype(F32) * weight, axis=1, keepdims=True)
    block_ref[:, half + rank :] = jnp.broadcast_to(column, (2 * capacity, rank)).astype(BF)
    copies[4].wait()
    copies[5].wait()
    low = dot(tokens_ref[...], down_ref[...], NT).astype(BF)
    block_ref[:, half : half + rank] = dot(upper, low).astype(BF)


def hidden_kernel(capacity, slot, count, *refs):
    blocks, refs = refs[:count], refs[count:]
    (gate_ref, up_ref, down_ref, lora_gate, lora_up, dgate_ref, dup_ref, low_ref), refs = refs[:8], refs[8:]
    lows, rows = refs[:count], refs[count]
    hidden, width = down_ref.shape
    half = width // 2
    rank = lora_gate.shape[0]
    tall = rows.shape[0] // count
    for i, block in enumerate(blocks):
        rows[i * tall : i * tall + 2 * capacity, :] = block[:, :half]
    first = dot(down_ref[:, :half], rows[...], NT).T
    second = dot(down_ref[:, half:], rows[...], NT).T
    live = lax.broadcasted_iota(jnp.int32, (slot, hidden), 0) < capacity
    for i, block in enumerate(blocks):
        at = i * tall
        extra = block[:, half:]
        low_ref[i] = extra[:slot, :rank]
        weight = extra.astype(F32)[:slot, rank : rank + 1]
        grad = (first[at : at + slot] + second[at + capacity : at + capacity + slot]) * weight
        grad = jnp.where(live, grad, 0.0)
        gate = gate_ref[i].astype(F32)
        up = up_ref[i].astype(F32)
        sig = 1.0 / (1.0 + jnp.exp(-gate))
        slope = sig * (1.0 + gate * (1.0 - sig))
        dgate = (grad * up * slope).astype(BF)
        dup = (grad * gate * sig).astype(BF)
        dgate_ref[i] = dgate
        dup_ref[i] = dup
        lows[i][...] = SCALE * (dot(dgate, lora_gate[...], NT) + dot(dup, lora_up[...], NT))


def stack(groups, slot, sources, target):
    at = 0
    for size, source in zip(groups, sources):
        for i in range(size):
            target[at : at + slot, :] = source[i]
            at += slot


def lora_kernel(slot, groups, *refs):
    pieces = len(groups)
    dgates, dups, lows = refs[:pieces], refs[pieces : 2 * pieces], refs[2 * pieces : 3 * pieces]
    lora_out, dgate, dup, low = refs[3 * pieces :]
    rank = lora_out.shape[0] // 2
    stack(groups, slot, dgates, dgate)
    stack(groups, slot, dups, dup)
    stack(groups, slot, lows, low)
    lora_out[:rank, :] = (SCALE * dot(low[...], dgate[...], TN)).astype(BF)
    lora_out[rank:, :] = (SCALE * dot(low[...], dup[...], TN)).astype(BF)


def first_partial_kernel(capacity, slot, cut, dgate_in, dup_in, gate_ref, up_ref, top, rest, dgate, dup, tile):
    half = gate_ref.shape[0] // 2
    dgate[:slot, :] = dgate_in[0]
    dup[:slot, :] = dup_in[0]
    step = tile.shape[1]
    for t in range(0, half, step):
        for at, place in ((t, 0), (t + half, capacity)):
            total = dot(gate_ref[at : at + step, :], dgate[...], NT) + dot(up_ref[at : at + step, :], dup[...], NT)
            tile[place : place + capacity, :] = total.T[:capacity]
        top[:, t : t + step] = tile[:cut, :].astype(BF)
        rest[:, t : t + step] = tile[cut:, :].astype(BF)


def partial_kernel(capacity, slot, groups, *refs):
    members, pieces = sum(groups), len(groups)
    dgates, dups, refs = refs[:pieces], refs[pieces : 2 * pieces], refs[2 * pieces :]
    gate_ref, up_ref, outs, (dgate, dup, tile) = refs[0], refs[1], refs[2:-3], refs[-3:]
    half = gate_ref.shape[0] // 2
    stack(groups, slot, dgates, dgate)
    stack(groups, slot, dups, dup)

    for t in range(0, half, TILE):
        sums = []
        for at in (t, t + half):
            sums.append(
                dot(dgate[...], gate_ref[at : at + TILE, :], NT)
                + dot(dup[...], up_ref[at : at + TILE, :], NT)
            )
        for i in range(members):
            at = i * slot
            tile[:capacity, :] = sums[0][at : at + capacity]
            tile[capacity:, :] = sums[1][at : at + capacity]
            outs[i][:, t : t + TILE] = tile[...].astype(BF)


def merge_kernel(cut, upper, part_ref, own_ref, out_ref):
    span, other = (slice(0, cut), slice(cut, None)) if upper else (slice(cut, None), slice(0, cut))
    out_ref[span, :] = (part_ref[...].astype(F32) + own_ref[span, :].astype(F32)).astype(BF)
    out_ref[other, :] = own_ref[other, :]


def adapter_kernel(capacity, count, where_ref, choice_ref, tokens_ref, *refs):
    lows, (low_ref, keep_ref, send_ref) = refs[:count], refs[count:]
    share = keep_ref.shape[2]
    part = keep_ref.shape[1]
    low = lows[0][...]
    for other in lows[1:]:
        low = low + other[...]
    low = low.astype(BF)
    low_ref[...] = low
    upper, _ = pick_rows(choice_ref[...], capacity)
    low = dot(upper[: low.shape[0]], low, TN).astype(BF)
    core = where_ref[count]
    for i in range(count):
        columns = pl.ds(pl.multiple_of(where_ref[i] * share, 128), share)
        down = dot(low, tokens_ref[:, columns], TN)
        keep_ref[i] = jnp.where(core == 0, down[:part], down[part:]).astype(BF)
        send_ref[i] = jnp.where(core == 0, down[part:], down[:part]).astype(BF)


def finish_kernel(capacity, choice_ref, left_ref, right_ref, own_ref, low_ref, down_ref, out_ref, low_tall):
    half = left_ref.shape[1]
    upper, lower = pick_rows(choice_ref[...], capacity)
    low = low_ref[...].astype(F32)[:capacity]
    zero = jnp.zeros_like(low)
    low_tall[:capacity, :] = low
    low_tall[capacity:, :] = zero
    low_upper = low_tall[...].astype(BF)
    low_tall[:capacity, :] = zero
    low_tall[capacity:, :] = low
    low_lower = low_tall[...].astype(BF)
    total = left_ref[...].astype(F32) + right_ref[...].astype(F32) + own_ref[...].astype(F32)
    total += dot(low_upper, down_ref[:, :half]) + dot(low_lower, down_ref[:, half:])
    total = total.astype(BF)
    out_ref[:, :half] = dot(upper, total, TN).astype(BF)
    out_ref[:, half:] = dot(lower, total, TN).astype(BF)


def in_hbm(x):
    return pltpu.with_memory_space_constraint(x, pltpu.HBM)


def in_vmem(x):
    return pltpu.with_memory_space_constraint(x, pltpu.VMEM)


def params():
    return pltpu.CompilerParams(vmem_limit_bytes=VMEM_LIMIT)


def cost(flops, moved):
    return pl.CostEstimate(flops=int(flops), bytes_accessed=int(moved), transcendentals=0)


def on_device(
    ring,
    tokens,
    output_gradient,
    token_expert_choice,
    routing_weight_table,
    stored_gate_rows,
    stored_up_rows,
    gate_weight,
    up_weight,
    down_weight,
    adapter_down_factor,
    adapter_gate_factor,
    adapter_up_factor,
):
    n = len(ring)
    tokens, output_gradient = tokens[0], output_gradient[0]
    own_count, width = tokens.shape
    half = width // 2
    capacity = stored_gate_rows.shape[1] // n
    hidden = stored_gate_rows.shape[2]
    rank = adapter_down_factor.shape[0]
    tall = -(-2 * capacity // 128) * 128
    slot = -(-capacity // 8) * 8
    cut = capacity // 16 * 16
    wide = half + 2 * rank
    middle = n // 2
    choice = token_expert_choice[0].T
    weights = routing_weight_table[0].T

    me = lax.axis_index("expert")
    core = lax.axis_index("dp")
    place = [0] * n
    for i, e in enumerate(ring):
        place[e] = i
    to_right = [(ring[i], ring[(i + 1) % n]) for i in range(n)]
    to_left = [(ring[i], ring[(i - 1) % n]) for i in range(n)]
    passes = [[0]] + [[-s, s] for s in range(1, middle)] + [[middle]]
    order = [r for group in passes for r in group]
    owners = jnp.array(
        [[ring[(place[e] + r) % n] for r in order] for e in range(n)], jnp.int32
    )[me]
    block = pl.pallas_call(
        functools.partial(prepare_kernel, capacity),
        in_specs=[pl.BlockSpec(memory_space=pl.ANY)] * 5,
        out_shape=jax.ShapeDtypeStruct((2 * capacity, wide), BF),
        scratch_shapes=[
            pltpu.VMEM(choice.shape, choice.dtype),
            pltpu.VMEM(weights.shape, BF),
            pltpu.VMEM(output_gradient.shape, BF),
            pltpu.VMEM(tokens.shape, BF),
            pltpu.VMEM(adapter_down_factor.shape, BF),
            pltpu.SemaphoreType.DMA((6,)),
        ],
        compiler_params=params(),
        cost_estimate=cost(4e8, 4.5e6),
        name="prepare",
    )(*[in_hbm(x) for x in (choice, weights, output_gradient, tokens, adapter_down_factor)])

    def in_order(stored):
        rows = stored[0].reshape(n, capacity, hidden)[owners]
        return jnp.pad(rows, ((0, 0), (0, slot - capacity), (0, 0)))

    gate_rows, up_rows = in_order(stored_gate_rows), in_order(stored_up_rows)

    down_here, gate_here, up_here = in_vmem(down_weight), in_vmem(gate_weight), in_vmem(up_weight)
    dgates, dups, low_rows, lows = [], [], [], []
    got = {0: block}

    def hidden_pass(group):
        size, start = len(group), len(lows)
        grads = jax.ShapeDtypeStruct((size, slot, hidden), BF)
        results = pl.pallas_call(
            functools.partial(hidden_kernel, capacity, slot, size),
            out_shape=[grads, grads, jax.ShapeDtypeStruct((size, slot, rank), BF)]
            + [jax.ShapeDtypeStruct((slot, rank), F32)] * size,
            scratch_shapes=[pltpu.VMEM((size * tall, half), BF)],
            compiler_params=params(),
            cost_estimate=cost(2 * size * tall * width * hidden, 2 * hidden * width),
            name="hidden_rows",
        )(
            *[got[r] for r in group],
            gate_rows[start : start + size],
            up_rows[start : start + size],
            down_here,
            adapter_gate_factor,
            adapter_up_factor,
        )
        dgates.append(results[0])
        dups.append(results[1])
        low_rows.append(results[2])
        for r, low in zip(group, results[3:]):
            pairs = [(ring[i], ring[(i + r) % n]) for i in range(n)]
            lows.append(lax.ppermute(low, "expert", pairs) if r else low)

    rightward = leftward = block
    for s in range(1, middle + 1):
        if s < middle:
            rightward = lax.ppermute(rightward, "expert", to_right)
            leftward = lax.ppermute(leftward, "expert", to_left)
        else:
            rightward = lax.ppermute(rightward[:cut], "expert", to_right)
            leftward = lax.ppermute(leftward[cut:], "expert", to_left)
        arrived = list(lows)
        hidden_pass(passes[s - 1])
        rightward, leftward, dgates[-1], dups[-1], arrived = lax.optimization_barrier(
            (rightward, leftward, dgates[-1], dups[-1], arrived)
        )
        lows[: len(arrived)] = arrived
        if s < middle:
            got[-s], got[s] = rightward, leftward
    got[middle] = jnp.concatenate([rightward, leftward], axis=0)
    hidden_pass(passes[-1])

    sizes = [len(group) for group in passes]
    last_a, last_b = pl.pallas_call(
        functools.partial(first_partial_kernel, capacity, slot, cut),
        out_shape=[jax.ShapeDtypeStruct((h, half), BF) for h in (cut, 2 * capacity - cut)],
        scratch_shapes=[
            pltpu.VMEM((128, hidden), BF),
            pltpu.VMEM((128, hidden), BF),
            pltpu.VMEM((2 * capacity, half // 2), F32),
        ],
        compiler_params=params(),
        cost_estimate=cost(4 * slot * width * hidden, 4 * hidden * width),
        name="first_partial",
    )(dgates[-1], dups[-1], gate_here, up_here)
    lows, last_a, last_b = lax.optimization_barrier((lows, last_a, last_b))
    own = pl.pallas_call(
        functools.partial(partial_kernel, capacity, slot, sizes[:-1]),
        out_shape=[jax.ShapeDtypeStruct((2 * capacity, half), BF)] * (n - 1),
        scratch_shapes=[
            pltpu.VMEM(((n - 1) * slot, hidden), BF),
            pltpu.VMEM(((n - 1) * slot, hidden), BF),
            pltpu.VMEM((2 * capacity, TILE), F32),
        ],
        compiler_params=params(),
        cost_estimate=cost(4 * (n - 1) * slot * width * hidden, 4 * hidden * width),
        name="partials",
    )(*dgates[:-1], *dups[:-1], gate_here, up_here)

    def add(a, b):
        return (a.astype(F32) + b.astype(F32)).astype(BF)

    going_right = lax.ppermute(last_a, "expert", to_right)
    going_left = lax.ppermute(last_b, "expert", to_left)


    going_right, going_left, own = lax.optimization_barrier((going_right, going_left, own))
    own = dict(zip(order[:-1], own))

    def merge(upper, part, mine):
        return pl.pallas_call(
            functools.partial(merge_kernel, cut, upper),
            out_shape=jax.ShapeDtypeStruct(mine.shape, BF),
            compiler_params=params(),
            cost_estimate=cost(mine.size, 6 * mine.size),
            name="first_add",
        )(part, mine)

    going_right = merge(True, going_right, own[middle - 1])
    going_left = merge(False, going_left, own[-(middle - 1)])
    for s in range(middle - 1, 0, -1):
        going_right = lax.ppermute(going_right, "expert", to_right)
        going_left = lax.ppermute(going_left, "expert", to_left)
        if s > 1:
            going_right = add(going_right, own[s - 1])
            going_left = add(going_left, own[-(s - 1)])

    share = width // n
    part = rank // 2
    columns_of = jnp.arange(n, dtype=jnp.int32) ^ me
    if share % 128 == 0:
        split = jax.ShapeDtypeStruct((n, part, share), BF)
        whole = pl.BlockSpec(memory_space=pltpu.VMEM)
        low, keep, send = pl.pallas_call(
            functools.partial(adapter_kernel, capacity, n),
            in_specs=[pl.BlockSpec(memory_space=pltpu.SMEM)] + [whole] * (n + 2),
            out_shape=[jax.ShapeDtypeStruct((slot, rank), BF), split, split],
            compiler_params=params(),
            cost_estimate=cost(2 * own_count * rank * width, 2 * own_count * width),
            name="adapter_gradient",
        )(jnp.append(columns_of, core), choice, tokens, *lows)
    else:
        upper, _ = pick_rows(choice, capacity)
        low = sum(lows).astype(BF)
        low_tokens = dot(upper[:slot], low, TN).astype(BF)
        down = dot(low_tokens, tokens, TN).astype(BF).reshape(rank, n, share)
        down = down.transpose(1, 0, 2)[columns_of]
        keep = jnp.where(core == 0, down[:, :part], down[:, part:])
        send = jnp.where(core == 0, down[:, part:], down[:, :part])

    swap = [(0, 1), (1, 0)]
    down = add(keep, lax.ppermute(send, "dp", swap))
    extras, _ = lax.optimization_barrier((low_rows, down))
    lora_local = pl.pallas_call(
        functools.partial(lora_kernel, slot, sizes),
        out_shape=jax.ShapeDtypeStruct((2 * rank, hidden), BF),
        scratch_shapes=[
            pltpu.VMEM((n * slot, hidden), BF),
            pltpu.VMEM((n * slot, hidden), BF),
            pltpu.VMEM((n * slot, rank), BF),
        ],
        compiler_params=params(),
        cost_estimate=cost(4 * n * slot * rank * hidden, 4 * n * slot * hidden),
        name="lora_rows",
    )(*dgates, *dups, *extras)

    lora = lora_local.astype(F32) + lax.ppermute(lora_local, "dp", swap).astype(F32)
    bit = 1
    while bit < n:
        pairs = down.reshape(down.shape[0] // 2, 2, part, share)
        other = lax.ppermute(pairs[:, 1], "expert", [(e, e ^ bit) for e in range(n)])
        down = add(pairs[:, 0], other)
        bit *= 2
    down = down[0]
    there = lax.ppermute(down, "dp", swap)
    grad_down = jnp.where(
        core == 0, jnp.concatenate([down, there]), jnp.concatenate([there, down])
    ).astype(F32)

    input_gradient = pl.pallas_call(
        functools.partial(finish_kernel, capacity),
        out_shape=jax.ShapeDtypeStruct((own_count, width), BF),
        scratch_shapes=[pltpu.VMEM((2 * capacity, rank), F32)],
        compiler_params=params(),
        cost_estimate=cost(4e8, 4.5e6),
        name="finish",
    )(choice, going_right, going_left, own[0], low, adapter_down_factor)
    return (input_gradient[None], grad_down, lora[:rank], lora[rank:])


def solution(mesh):
    placed = (
        P(("groups", "dp"), "expert", None),
        P(("groups", "dp"), "expert", None),
        P(("groups", "dp"), "expert", None),
        P(("groups", "dp"), "expert", None),
        P(("groups", "dp"), None, "expert"),
        P(("groups", "dp"), None, "expert"),
        P(None, "expert"),
        P(None, "expert"),
        P("expert", None),
        P("groups", None),
        P("groups", "expert"),
        P("groups", "expert"),
    )
    return jax.shard_map(
        functools.partial(on_device, ring_order(mesh)),
        mesh=mesh,
        in_specs=placed,
        out_specs=(
            P(("groups", "dp"), "expert", None),
            P("groups", "expert"),
            P("groups", "expert"),
            P("groups", "expert"),
        ),
        check_vma=False,
    )
```

```python
import functools

import jax
import jax.numpy as jnp
from jax import lax
from jax.experimental import pallas as pl
from jax.experimental.pallas import tpu as pltpu
from jax.sharding import PartitionSpec as P

SCALE = 0.25
NT = (((1,), (1,)), ((), ()))
TN = (((0,), (0,)), ((), ()))
BF = jnp.bfloat16
F32 = jnp.float32
VMEM_LIMIT = 10 * 1024 * 1024
TILE = 256


def ring_order(mesh):
    count = mesh.shape["expert"]
    plain = list(range(count))
    if count < 4 or count % 2:
        return plain
    snake = list(range(0, count, 2)) + list(range(count - 1, 0, -2))
    spots = [getattr(d, "coords", None) for d in mesh.devices[0, :, 0]]
    if any(s is None for s in spots):
        return snake if count == 8 else plain

    def length(order):
        hops = zip(order, order[1:] + order[:1])
        return sum(sum(abs(a - b) for a, b in zip(spots[i], spots[j])) for i, j in hops)

    return min((plain, snake), key=length)


def dot(a, b, dims=None):
    if dims is None:
        dims = (((1,), (0,)), ((), ()))
    return lax.dot_general(a, b, dims, preferred_element_type=F32)


def pick_rows(choice, capacity):
    tokens = choice.shape[1]
    named = jnp.max((choice == 0).astype(F32), axis=0, keepdims=True)
    before = lax.broadcasted_iota(jnp.int32, (tokens, tokens), 0)
    after = lax.broadcasted_iota(jnp.int32, (tokens, tokens), 1)
    upto = (before <= after).astype(BF)
    count = dot(jnp.broadcast_to(named, (8, tokens)).astype(BF), upto)[:1]
    slot = jnp.where(named > 0, count - 1.0, -1000.0).astype(jnp.int32)
    row = lax.broadcasted_iota(jnp.int32, (2 * capacity, tokens), 0)
    return (row == slot).astype(BF), (row - capacity == slot).astype(BF)


def prepare_kernel(capacity, choice_hbm, weight_hbm, grad_hbm, tokens_hbm, down_hbm, top, rest,
                   choice_ref, weight_ref, grad_ref, tokens_ref, down_ref, sems):
    half = grad_ref.shape[1] // 2
    rank = down_ref.shape[0]
    pairs = [
        (choice_hbm, choice_ref),
        (grad_hbm.at[:, :half], grad_ref.at[:, :half]),
        (grad_hbm.at[:, half:], grad_ref.at[:, half:]),
        (weight_hbm, weight_ref),
        (down_hbm, down_ref),
        (tokens_hbm, tokens_ref),
    ]
    copies = [pltpu.make_async_copy(a, b, sems.at[i]) for i, (a, b) in enumerate(pairs)]
    for copy in copies:
        copy.start()
    copies[0].wait()
    choice = choice_ref[...]
    upper, lower = pick_rows(choice, capacity)
    copies[1].wait()
    first = dot(upper, grad_ref[:, :half])
    copies[2].wait()
    rows = (first + dot(lower, grad_ref[:, half:])).astype(BF)
    cut = top.shape[0]
    top[:, :half] = rows[:cut]
    rest[:, :half] = rows[cut:]
    copies[3].wait()
    weight = jnp.sum(
        jnp.where(choice == 0, weight_ref[...].astype(F32), 0.0), axis=0, keepdims=True
    )
    column = jnp.sum(upper.astype(F32) * weight, axis=1, keepdims=True)
    column = jnp.broadcast_to(column, (2 * capacity, rank)).astype(BF)
    top[:, half + rank :] = column[:cut]
    rest[:, half + rank :] = column[cut:]
    copies[4].wait()
    copies[5].wait()
    low = dot(tokens_ref[...], down_ref[...], NT).astype(BF)
    low = dot(upper, low).astype(BF)
    top[:, half : half + rank] = low[:cut]
    rest[:, half : half + rank] = low[cut:]


def place_here(place):
    me = lax.axis_index("expert")
    return me, sum(jnp.where(me == e, p, 0) for e, p in enumerate(place))


def reorder_kernel(place, capacity, gate_in, up_in, gate_out, up_out, tall):
    count, slot, hidden = gate_out.shape
    _, here = place_here(place)
    live = lax.broadcasted_iota(jnp.int32, (slot, hidden), 0) < capacity
    for source, target in ((gate_in, gate_out), (up_in, up_out)):
        tall[: count * capacity, :] = source[...].astype(F32)
        tall[count * capacity :, :] = jnp.zeros((slot, hidden), F32)
        for e in range(count):
            away = lax.rem(place[e] - here + count, count)
            at = jnp.where(2 * away < count, 2 * away, 2 * (count - away) - 1)
            rows = tall[e * capacity : e * capacity + slot, :]
            target[at] = jnp.where(live, rows, 0.0).astype(BF)


def low_order_kernel(ring, place, order, *refs):
    lows, (keep, send) = refs[:-2], refs[-2:]
    count = len(ring)
    me, here = place_here(place)
    for low, r in zip(lows, order):
        spot = lax.rem(here + r + count, count)
        owner = sum(jnp.where(spot == i, e, 0) for i, e in enumerate(ring))
        key = owner ^ me

        @pl.when(key % 2 == 0)
        def _(low=low, key=key):
            keep[key // 2] = low[...]

        @pl.when(key % 2 == 1)
        def _(low=low, key=key):
            send[key // 2] = low[...]


def halve_kernel(ours, theirs, *outs):
    count = ours.shape[0]
    for i in range(count):
        total = ours[i].astype(F32) + theirs[i].astype(F32)
        out = outs[i % len(outs)]
        out[i // len(outs)] = total.astype(out.dtype)


def hidden_kernel(capacity, slot, start, count, *refs):
    tops, rests, refs = refs[:count], refs[count : 2 * count], refs[2 * count :]
    (gate_ref, up_ref, down_ref, lora_gate, lora_up, dgate_ref, dup_ref, low_ref), refs = refs[:8], refs[8:]
    lows, rows = refs[:count], refs[count]
    hidden, width = down_ref.shape
    half = width // 2
    rank = lora_gate.shape[0]
    cut = tops[0].shape[0]
    tall = rows.shape[0] // count
    for i in range(count):
        rows[i * tall : i * tall + cut, :] = tops[i][:, :half]
        rows[i * tall + cut : i * tall + 2 * capacity, :] = rests[i][:, :half]
    first = dot(down_ref[:, :half], rows[...], NT).T
    second = dot(down_ref[:, half:], rows[...], NT).T
    live = lax.broadcasted_iota(jnp.int32, (slot, hidden), 0) < capacity
    for i in range(count):
        at = i * tall
        extra = tops[i][:, half:], rests[i][: slot - cut, half:]
        low_ref[i, :cut, :] = extra[0][:, :rank]
        low_ref[i, cut:, :] = extra[1][:, :rank]
        weight = jnp.concatenate([x.astype(F32)[:, rank : rank + 1] for x in extra], axis=0)
        grad = (first[at : at + slot] + second[at + capacity : at + capacity + slot]) * weight
        grad = jnp.where(live, grad, 0.0)
        gate = gate_ref[start + i].astype(F32)
        up = up_ref[start + i].astype(F32)
        sig = 1.0 / (1.0 + jnp.exp(-gate))
        slope = sig * (1.0 + gate * (1.0 - sig))
        dgate = (grad * up * slope).astype(BF)
        dup = (grad * gate * sig).astype(BF)
        dgate_ref[i] = dgate
        dup_ref[i] = dup
        lows[i][...] = SCALE * (dot(dgate, lora_gate[...], NT) + dot(dup, lora_up[...], NT))


def stack(groups, slot, sources, target):
    at = 0
    for size, source in zip(groups, sources):
        for i in range(size):
            target[at : at + slot, :] = source[i]
            at += slot


def lora_kernel(slot, groups, *refs):
    pieces = len(groups)
    dgates, dups, lows = refs[:pieces], refs[pieces : 2 * pieces], refs[2 * pieces : 3 * pieces]
    lora_out, dgate, dup, low = refs[3 * pieces :]
    rank = lora_out.shape[0] // 2
    stack(groups, slot, dgates, dgate)
    stack(groups, slot, dups, dup)
    stack(groups, slot, lows, low)
    lora_out[:rank, :] = (SCALE * dot(low[...], dgate[...], TN)).astype(BF)
    lora_out[rank:, :] = (SCALE * dot(low[...], dup[...], TN)).astype(BF)


def first_partial_kernel(capacity, slot, cut, dgate_in, dup_in, gate_ref, up_ref, top, rest, dgate, dup, tile):
    half = gate_ref.shape[0] // 2
    dgate[:slot, :] = dgate_in[0]
    dup[:slot, :] = dup_in[0]
    step = tile.shape[1]
    for t in range(0, half, step):
        for at, place in ((t, 0), (t + half, capacity)):
            total = dot(gate_ref[at : at + step, :], dgate[...], NT) + dot(up_ref[at : at + step, :], dup[...], NT)
            tile[place : place + capacity, :] = total.T[:capacity]
        top[:, t : t + step] = tile[:cut, :].astype(BF)
        rest[:, t : t + step] = tile[cut:, :].astype(BF)


def partial_kernel(capacity, slot, groups, *refs):
    members, pieces = sum(groups), len(groups)
    dgates, dups, refs = refs[:pieces], refs[pieces : 2 * pieces], refs[2 * pieces :]
    gate_ref, up_ref, outs, (dgate, dup, tile) = refs[0], refs[1], refs[2:-3], refs[-3:]
    half = gate_ref.shape[0] // 2
    stack(groups, slot, dgates, dgate)
    stack(groups, slot, dups, dup)

    for t in range(0, half, TILE):
        sums = []
        for at in (t, t + half):
            sums.append(
                dot(dgate[...], gate_ref[at : at + TILE, :], NT)
                + dot(dup[...], up_ref[at : at + TILE, :], NT)
            )
        for i in range(members):
            at = i * slot
            tile[:capacity, :] = sums[0][at : at + capacity]
            tile[capacity:, :] = sums[1][at : at + capacity]
            cut = outs[2 * i].shape[0]
            outs[2 * i][:, t : t + TILE] = tile[:cut, :].astype(BF)
            outs[2 * i + 1][:, t : t + TILE] = tile[cut:, :].astype(BF)


def adapter_kernel(capacity, choice_ref, tokens_ref, low_in, low_ref, keep_ref, send_ref):
    count, part, share = keep_ref.shape
    low = low_in[0].astype(BF)
    low_ref[...] = low
    upper, _ = pick_rows(choice_ref[...], capacity)
    low = dot(upper[: low.shape[0]], low, TN).astype(BF)
    me, core = lax.axis_index("expert"), lax.axis_index("dp")
    for i in range(count):
        columns = pl.ds(pl.multiple_of((me ^ i) * share, 128), share)
        down = dot(low, tokens_ref[:, columns], TN)
        keep_ref[i] = jnp.where(core == 0, down[:part], down[part:]).astype(BF)
        send_ref[i] = jnp.where(core == 0, down[part:], down[:part]).astype(BF)


def join_kernel(down_ref, there_ref, lora_ref, lora_there, down_out, gate_out, up_out):
    part = down_ref.shape[0]
    core = lax.axis_index("dp")
    down, there = down_ref[...].astype(F32), there_ref[...].astype(F32)
    down_out[:part, :] = jnp.where(core == 0, down, there)
    down_out[part:, :] = jnp.where(core == 0, there, down)
    rank = gate_out.shape[0]
    gate_out[...] = lora_ref[:rank, :].astype(F32) + lora_there[:rank, :].astype(F32)
    up_out[...] = lora_ref[rank:, :].astype(F32) + lora_there[rank:, :].astype(F32)


def finish_kernel(capacity, choice_ref, *refs):
    tops, rests, (low_ref, down_ref, out_ref, low_tall) = refs[:3], refs[3:6], refs[6:]
    cut, half = tops[0].shape
    upper, lower = pick_rows(choice_ref[...], capacity)
    low = low_ref[...].astype(F32)[:capacity]
    zero = jnp.zeros_like(low)
    low_tall[:capacity, :] = low
    low_tall[capacity:, :] = zero
    low_upper = low_tall[...].astype(BF)
    low_tall[:capacity, :] = zero
    low_tall[capacity:, :] = low
    low_lower = low_tall[...].astype(BF)
    adapter = dot(low_upper, down_ref[:, :half]) + dot(low_lower, down_ref[:, half:])
    top = sum(x[...].astype(F32) for x in tops) + adapter[:cut]
    rest = sum(x[...].astype(F32) for x in rests) + adapter[cut:]
    top, rest = top.astype(BF), rest.astype(BF)
    for pick, at in ((upper, 0), (lower, half)):
        picked = dot(pick[:cut], top, TN) + dot(pick[cut:], rest, TN)
        out_ref[:, at : at + half] = picked.astype(BF)


def in_hbm(x):
    return pltpu.with_memory_space_constraint(x, pltpu.HBM)


def in_vmem(x):
    return pltpu.with_memory_space_constraint(x, pltpu.VMEM)


def on_device(
    ring,
    tokens,
    output_gradient,
    token_expert_choice,
    routing_weight_table,
    stored_gate_rows,
    stored_up_rows,
    gate_weight,
    up_weight,
    down_weight,
    adapter_down_factor,
    adapter_gate_factor,
    adapter_up_factor,
):
    n = len(ring)
    tokens, output_gradient = tokens[0], output_gradient[0]
    own_count, width = tokens.shape
    half = width // 2
    capacity = stored_gate_rows.shape[1] // n
    hidden = stored_gate_rows.shape[2]
    rank = adapter_down_factor.shape[0]
    tall = -(-2 * capacity // 128) * 128
    slot = -(-capacity // 8) * 8
    cut = capacity // 16 * 16
    wide = half + 2 * rank
    middle = n // 2
    choice = token_expert_choice[0].T
    weights = routing_weight_table[0].T

    place = [0] * n
    for i, e in enumerate(ring):
        place[e] = i
    to_right = [(ring[i], ring[(i + 1) % n]) for i in range(n)]
    to_left = [(ring[i], ring[(i - 1) % n]) for i in range(n)]
    passes = [[0]] + [[-s, s] for s in range(1, middle)] + [[middle]]
    sizes = [len(group) for group in passes]
    order = [r for group in passes for r in group]
    heights = [cut, 2 * capacity - cut]

    def call(kernel, name, shapes, args, scratch=(), work=(0, 0), **more):
        return pl.pallas_call(
            kernel,
            out_shape=[jax.ShapeDtypeStruct(shape, dtype) for shape, dtype in shapes],
            scratch_shapes=list(scratch),
            compiler_params=pltpu.CompilerParams(vmem_limit_bytes=VMEM_LIMIT),
            cost_estimate=pl.CostEstimate(
                flops=int(work[0]), bytes_accessed=int(work[1]), transcendentals=0
            ),
            name=name,
            **more,
        )(*args)

    def right(x):
        return lax.ppermute(x, "expert", to_right)

    def left(x):
        return lax.ppermute(x, "expert", to_left)

    block = call(
        functools.partial(prepare_kernel, capacity),
        "prepare",
        [((h, wide), BF) for h in heights],
        [in_hbm(x) for x in (choice, weights, output_gradient, tokens, adapter_down_factor)],
        [
            pltpu.VMEM(choice.shape, choice.dtype),
            pltpu.VMEM(weights.shape, BF),
            pltpu.VMEM(output_gradient.shape, BF),
            pltpu.VMEM(tokens.shape, BF),
            pltpu.VMEM(adapter_down_factor.shape, BF),
            pltpu.SemaphoreType.DMA((6,)),
        ],
        (4e8, 4.5e6),
        in_specs=[pl.BlockSpec(memory_space=pl.ANY)] * 5,
    )
    gate_rows, up_rows = call(
        functools.partial(reorder_kernel, place, capacity),
        "reorder",
        [((n, slot, hidden), BF)] * 2,
        [stored_gate_rows[0], stored_up_rows[0]],
        [pltpu.VMEM((n * capacity + slot, hidden), F32)],
        (0, 8 * n * slot * hidden),
    )

    down_here, gate_here, up_here = in_vmem(down_weight), in_vmem(gate_weight), in_vmem(up_weight)
    dgates, dups, low_rows, lows = [], [], [], []
    got = {0: tuple(block)}

    def hidden_pass(group):
        size, start = len(group), len(lows)
        results = call(
            functools.partial(hidden_kernel, capacity, slot, start, size),
            "hidden_rows",
            [((size, slot, hidden), BF)] * 2
            + [((size, slot, rank), BF)]
            + [((slot, rank), F32)] * size,
            [got[r][0] for r in group]
            + [got[r][1] for r in group]
            + [gate_rows, up_rows, down_here, adapter_gate_factor, adapter_up_factor],
            [pltpu.VMEM((size * tall, half), BF)],
            (2 * size * tall * width * hidden, 2 * hidden * width),
        )
        dgates.append(results[0])
        dups.append(results[1])
        low_rows.append(results[2])
        lows.extend(results[3:])

    right_top, right_rest = left_top, left_rest = block
    for s in range(1, middle + 1):
        right_top, left_rest = right(right_top), left(left_rest)
        if s < middle:
            right_rest, left_top = right(right_rest), left(left_top)
        hidden_pass(passes[s - 1])
        if s < middle:
            right_rest, left_top, dgates[-1], dups[-1] = lax.optimization_barrier(
                (right_rest, left_top, dgates[-1], dups[-1])
            )
            got[-s], got[s] = (right_top, right_rest), (left_top, left_rest)
        else:
            right_top, left_rest, dgates[-1], dups[-1] = lax.optimization_barrier(
                (right_top, left_rest, dgates[-1], dups[-1])
            )
    got[middle] = (right_top, left_rest)
    hidden_pass(passes[-1])

    low_keep, low_send = call(
        functools.partial(low_order_kernel, ring, place, order),
        "low_order",
        [((n // 2, slot, rank), F32)] * 2,
        lows,
    )

    right_top, left_rest = call(
        functools.partial(first_partial_kernel, capacity, slot, cut),
        "first_partial",
        [((h, half), BF) for h in heights],
        [dgates[-1], dups[-1], gate_here, up_here],
        [
            pltpu.VMEM((128, hidden), BF),
            pltpu.VMEM((128, hidden), BF),
            pltpu.VMEM((2 * capacity, half // 2), F32),
        ],
        (4 * slot * width * hidden, 4 * hidden * width),
    )
    own = call(
        functools.partial(partial_kernel, capacity, slot, sizes[:-1]),
        "partials",
        [((h, half), BF) for h in heights] * (n - 1),
        [*dgates[:-1], *dups[:-1], gate_here, up_here],
        [
            pltpu.VMEM(((n - 1) * slot, hidden), BF),
            pltpu.VMEM(((n - 1) * slot, hidden), BF),
            pltpu.VMEM((2 * capacity, TILE), F32),
        ],
        (4 * (n - 1) * slot * width * hidden, 4 * hidden * width),
    )

    def add(a, b):
        return (a.astype(F32) + b.astype(F32)).astype(BF)

    def exchange(keep, send, bit):
        other = lax.ppermute(send, "expert", [(e, e ^ bit) for e in range(n)])
        count = keep.shape[0]
        parts = 2 if count > 1 else 1
        shape = (count // parts,) + keep.shape[1:]
        return list(call(halve_kernel, "halve", [(shape, keep.dtype)] * parts, [keep, other]))

    low_keep, right_top, left_rest = lax.optimization_barrier((low_keep, right_top, left_rest))
    right_top, left_rest = right(right_top), left(left_rest)
    low_keep, low_send = exchange(low_keep, low_send, 1)
    right_top, left_rest, low_keep, own = lax.optimization_barrier((right_top, left_rest, low_keep, own))
    own = {r: (own[2 * i], own[2 * i + 1]) for i, r in enumerate(order[:-1])}
    pair = exchange(low_keep, low_send, 2)
    for s in range(middle - 1, 0, -1):
        right_top, left_rest = add(right_top, own[s][0]), add(left_rest, own[-s][1])
        if s == middle - 1:
            right_rest, left_top = own[s][1], own[-s][0]
            pair[0], right_top, left_rest = lax.optimization_barrier((pair[0], right_top, left_rest))
        else:
            right_rest, left_top = add(right_rest, own[s][1]), add(left_top, own[-s][0])
        right_top, left_rest = right(right_top), left(left_rest)
        right_rest, left_top = right(right_rest), left(left_top)
    bit = 4
    while bit < n:
        pair = exchange(*pair, bit)
        bit *= 2
    low_total = pair[0]

    share = width // n
    part = rank // 2
    swap = [(0, 1), (1, 0)]
    if share % 128 == 0:
        low, keep, send = call(
            functools.partial(adapter_kernel, capacity),
            "adapter_gradient",
            [((slot, rank), BF)] + [((n, part, share), BF)] * 2,
            [choice, tokens, low_total],
            work=(2 * own_count * rank * width, 2 * own_count * width),
        )
    else:
        me, core = lax.axis_index("expert"), lax.axis_index("dp")
        upper, _ = pick_rows(choice, capacity)
        low = low_total[0].astype(BF)
        low_tokens = dot(upper[:slot], low, TN).astype(BF)
        down = dot(low_tokens, tokens, TN).astype(BF).reshape(rank, n, share)
        down = down.transpose(1, 0, 2)[jnp.arange(n, dtype=jnp.int32) ^ me]
        keep = jnp.where(core == 0, down[:, :part], down[:, part:])
        send = jnp.where(core == 0, down[:, part:], down[:, :part])
    other = lax.ppermute(send, "dp", swap)
    pair = call(halve_kernel, "halve", [((n // 2, part, share), BF)] * 2, [keep, other])
    low_rows, _ = lax.optimization_barrier((low_rows, pair))
    (lora,) = call(
        functools.partial(lora_kernel, slot, sizes),
        "lora_rows",
        [((2 * rank, hidden), BF)],
        [*dgates, *dups, *low_rows],
        [
            pltpu.VMEM((n * slot, hidden), BF),
            pltpu.VMEM((n * slot, hidden), BF),
            pltpu.VMEM((n * slot, rank), BF),
        ],
        (4 * n * slot * rank * hidden, 4 * n * slot * hidden),
    )
    lora_there = lax.ppermute(lora, "dp", swap)
    bit = 1
    while bit < n:
        pair = exchange(*pair, bit)
        bit *= 2
    down = pair[0][0]
    there = lax.ppermute(down, "dp", swap)
    grad_down, grad_gate, grad_up = call(
        join_kernel,
        "join",
        [((rank, hidden), F32)] * 3,
        [down, there, lora, lora_there],
    )

    (input_gradient,) = call(
        functools.partial(finish_kernel, capacity),
        "finish",
        [((own_count, width), BF)],
        [choice, right_top, left_top, own[0][0], right_rest, left_rest, own[0][1], low, adapter_down_factor],
        [pltpu.VMEM((2 * capacity, rank), F32)],
        (4e8, 4.5e6),
    )
    return (input_gradient[None], grad_down, grad_gate, grad_up)


def solution(mesh):
    placed = (
        P(("groups", "dp"), "expert", None),
        P(("groups", "dp"), "expert", None),
        P(("groups", "dp"), "expert", None),
        P(("groups", "dp"), "expert", None),
        P(("groups", "dp"), None, "expert"),
        P(("groups", "dp"), None, "expert"),
        P(None, "expert"),
        P(None, "expert"),
        P("expert", None),
        P("groups", None),
        P("groups", "expert"),
        P("groups", "expert"),
    )
    return jax.shard_map(
        functools.partial(on_device, ring_order(mesh)),
        mesh=mesh,
        in_specs=placed,
        out_specs=(
            P(("groups", "dp"), "expert", None),
            P("groups", "expert"),
            P("groups", "expert"),
            P("groups", "expert"),
        ),
        check_vma=False,
    )
```

```python
import functools

import jax
import jax.numpy as jnp
from jax import lax
from jax.experimental import pallas as pl
from jax.experimental.pallas import tpu as pltpu
from jax.sharding import PartitionSpec as P

SCALE = 0.25
NT = (((1,), (1,)), ((), ()))
TN = (((0,), (0,)), ((), ()))
BF = jnp.bfloat16
F32 = jnp.float32
VMEM_LIMIT = 10 * 1024 * 1024
TILE = 256


def ring_order(mesh):
    count = mesh.shape["expert"]
    plain = list(range(count))
    if count < 4 or count % 2:
        return plain
    snake = list(range(0, count, 2)) + list(range(count - 1, 0, -2))
    spots = [getattr(d, "coords", None) for d in mesh.devices[0, :, 0]]
    if any(s is None for s in spots):
        return snake if count == 8 else plain

    def length(order):
        hops = zip(order, order[1:] + order[:1])
        return sum(sum(abs(a - b) for a, b in zip(spots[i], spots[j])) for i, j in hops)

    return min((plain, snake), key=length)


def dot(a, b, dims=None):
    if dims is None:
        dims = (((1,), (0,)), ((), ()))
    return lax.dot_general(a, b, dims, preferred_element_type=F32)


def pick_rows(choice, capacity):
    tokens = choice.shape[1]
    named = jnp.max((choice == 0).astype(F32), axis=0, keepdims=True)
    before = lax.broadcasted_iota(jnp.int32, (tokens, tokens), 0)
    after = lax.broadcasted_iota(jnp.int32, (tokens, tokens), 1)
    upto = (before <= after).astype(BF)
    count = dot(jnp.broadcast_to(named, (8, tokens)).astype(BF), upto)[:1]
    slot = jnp.where(named > 0, count - 1.0, -1000.0).astype(jnp.int32)
    row = lax.broadcasted_iota(jnp.int32, (2 * capacity, tokens), 0)
    return (row == slot).astype(BF), (row - capacity == slot).astype(BF)


def prepare_kernel(capacity, choice_hbm, weight_hbm, grad_hbm, tokens_hbm, down_hbm, block_ref,
                   choice_ref, weight_ref, grad_ref, tokens_ref, down_ref, sems):
    half = grad_ref.shape[1] // 2
    rank = down_ref.shape[0]
    pairs = [
        (choice_hbm, choice_ref),
        (grad_hbm.at[:, :half], grad_ref.at[:, :half]),
        (grad_hbm.at[:, half:], grad_ref.at[:, half:]),
        (weight_hbm, weight_ref),
        (down_hbm, down_ref),
        (tokens_hbm, tokens_ref),
    ]
    copies = [pltpu.make_async_copy(a, b, sems.at[i]) for i, (a, b) in enumerate(pairs)]
    for copy in copies:
        copy.start()
    copies[0].wait()
    choice = choice_ref[...]
    upper, lower = pick_rows(choice, capacity)
    copies[1].wait()
    first = dot(upper, grad_ref[:, :half])
    copies[2].wait()
    block_ref[:, :half] = (first + dot(lower, grad_ref[:, half:])).astype(BF)
    copies[3].wait()
    weight = jnp.sum(
        jnp.where(choice == 0, weight_ref[...].astype(F32), 0.0), axis=0, keepdims=True
    )
    column = jnp.sum(upper.astype(F32) * weight, axis=1, keepdims=True)
    block_ref[:, half + rank :] = jnp.broadcast_to(column, (2 * capacity, rank)).astype(BF)
    copies[4].wait()
    copies[5].wait()
    low = dot(tokens_ref[...], down_ref[...], NT).astype(BF)
    block_ref[:, half : half + rank] = dot(upper, low).astype(BF)


def cut_kernel(right_in, left_in, top, rest):
    cut = top.shape[0]
    top[...] = right_in[:cut, :]
    rest[...] = left_in[cut:, :]


def merge_kernel(top_in, rest_in, own_right, own_left, right_out, left_out):
    cut = top_in.shape[0]
    right_out[:cut, :] = (top_in[...].astype(F32) + own_right[:cut, :].astype(F32)).astype(BF)
    right_out[cut:, :] = own_right[cut:, :]
    left_out[:cut, :] = own_left[:cut, :]
    left_out[cut:, :] = (rest_in[...].astype(F32) + own_left[cut:, :].astype(F32)).astype(BF)


def place_here(place):
    me = lax.axis_index("expert")
    return me, sum(jnp.where(me == e, p, 0) for e, p in enumerate(place))


def reorder_kernel(place, capacity, gate_in, up_in, gate_out, up_out, tall):
    count, slot, hidden = gate_out.shape
    _, here = place_here(place)
    live = lax.broadcasted_iota(jnp.int32, (slot, hidden), 0) < capacity
    for source, target in ((gate_in, gate_out), (up_in, up_out)):
        tall[: count * capacity, :] = source[...].astype(F32)
        tall[count * capacity :, :] = jnp.zeros((slot, hidden), F32)
        for e in range(count):
            away = lax.rem(place[e] - here + count, count)
            at = jnp.where(2 * away < count, 2 * away, 2 * (count - away) - 1)
            rows = tall[e * capacity : e * capacity + slot, :]
            target[at] = jnp.where(live, rows, 0.0).astype(BF)


def halve_kernel(ours, theirs, *outs):
    count = ours.shape[0]
    for i in range(count):
        total = ours[i].astype(F32) + theirs[i].astype(F32)
        out = outs[i % len(outs)]
        out[i // len(outs)] = total.astype(out.dtype)


def hidden_kernel(capacity, slot, start, count, pieces, *refs):
    blocks, refs = [refs[i * pieces : (i + 1) * pieces] for i in range(count)], refs[count * pieces :]
    (gate_ref, up_ref, down_ref, lora_gate, lora_up, dgate_ref, dup_ref, low_ref), refs = refs[:8], refs[8:]
    lows, rows = refs[:count], refs[count]
    hidden, width = down_ref.shape
    half = width // 2
    rank = lora_gate.shape[0]
    tall = rows.shape[0] // count
    for i, block in enumerate(blocks):
        at = i * tall
        for piece in block:
            rows[at : at + piece.shape[0], :] = piece[:, :half]
            at += piece.shape[0]
    if tall % 128 == 0:
        first = dot(down_ref[:, :half], rows[...], NT).T
        second = dot(down_ref[:, half:], rows[...], NT).T
    else:
        first = dot(rows[...], down_ref[:, :half], NT)
        second = dot(rows[...], down_ref[:, half:], NT)
    live = lax.broadcasted_iota(jnp.int32, (slot, hidden), 0) < capacity
    for i in range(count):
        at = i * tall
        extras, seen = [], 0
        for piece in blocks[i]:
            height = min(piece.shape[0], slot - seen)
            extras.append(piece[:height, half:])
            low_ref[i, seen : seen + height, :] = extras[-1][:, :rank]
            seen += height
        weight = jnp.concatenate([x.astype(F32)[:, rank : rank + 1] for x in extras], axis=0)
        grad = (first[at : at + slot] + second[at + capacity : at + capacity + slot]) * weight
        grad = jnp.where(live, grad, 0.0)
        gate = gate_ref[start + i].astype(F32)
        up = up_ref[start + i].astype(F32)
        sig = 1.0 / (1.0 + jnp.exp(-gate))
        slope = sig * (1.0 + gate * (1.0 - sig))
        dgate = (grad * up * slope).astype(BF)
        dup = (grad * gate * sig).astype(BF)
        dgate_ref[i] = dgate
        dup_ref[i] = dup
        lows[i][...] = SCALE * (dot(dgate, lora_gate[...], NT) + dot(dup, lora_up[...], NT))


def stack(groups, slot, sources, target):
    at = 0
    for size, source in zip(groups, sources):
        for i in range(size):
            target[at : at + slot, :] = source[i]
            at += slot


def lora_kernel(slot, groups, *refs):
    pieces = len(groups)
    dgates, dups, lows = refs[:pieces], refs[pieces : 2 * pieces], refs[2 * pieces : 3 * pieces]
    lora_out, dgate, dup, low = refs[3 * pieces :]
    rank = lora_out.shape[0] // 2
    stack(groups, slot, dgates, dgate)
    stack(groups, slot, dups, dup)
    stack(groups, slot, lows, low)
    lora_out[:rank, :] = (SCALE * dot(low[...], dgate[...], TN)).astype(BF)
    lora_out[rank:, :] = (SCALE * dot(low[...], dup[...], TN)).astype(BF)


def first_partial_kernel(capacity, slot, cut, dgate_in, dup_in, gate_ref, up_ref, top, rest, dgate, dup, tile):
    half = gate_ref.shape[0] // 2
    dgate[:slot, :] = dgate_in[0]
    dup[:slot, :] = dup_in[0]
    step = tile.shape[1]
    for t in range(0, half, step):
        for at, place in ((t, 0), (t + half, capacity)):
            total = dot(gate_ref[at : at + step, :], dgate[...], NT) + dot(up_ref[at : at + step, :], dup[...], NT)
            tile[place : place + capacity, :] = total.T[:capacity]
        top[:, t : t + step] = tile[:cut, :].astype(BF)
        rest[:, t : t + step] = tile[cut:, :].astype(BF)


def partial_kernel(capacity, slot, groups, *refs):
    members, pieces = sum(groups), len(groups)
    dgates, dups, refs = refs[:pieces], refs[pieces : 2 * pieces], refs[2 * pieces :]
    gate_ref, up_ref, outs, (dgate, dup, tile) = refs[0], refs[1], refs[2:-3], refs[-3:]
    half = gate_ref.shape[0] // 2
    stack(groups, slot, dgates, dgate)
    stack(groups, slot, dups, dup)

    for t in range(0, half, TILE):
        sums = []
        for at in (t, t + half):
            sums.append(
                dot(dgate[...], gate_ref[at : at + TILE, :], NT)
                + dot(dup[...], up_ref[at : at + TILE, :], NT)
            )
        for i in range(members):
            at = i * slot
            tile[:capacity, :] = sums[0][at : at + capacity]
            tile[capacity:, :] = sums[1][at : at + capacity]
            outs[i][:, t : t + TILE] = tile[...].astype(BF)


def adapter_kernel(capacity, choice_ref, tokens_ref, *refs):
    lows, (low_ref, keep_ref, send_ref) = refs[:-3], refs[-3:]
    count, part, share = keep_ref.shape
    low = sum(x[...] for x in lows).astype(BF)
    low_ref[...] = low
    upper, _ = pick_rows(choice_ref[...], capacity)
    low = dot(upper[: low.shape[0]], low, TN).astype(BF)
    me, core = lax.axis_index("expert"), lax.axis_index("dp")
    for i in range(count):
        columns = pl.ds(pl.multiple_of((me ^ i) * share, 128), share)
        down = dot(low, tokens_ref[:, columns], TN)
        keep_ref[i] = jnp.where(core == 0, down[:part], down[part:]).astype(BF)
        send_ref[i] = jnp.where(core == 0, down[part:], down[:part]).astype(BF)


def join_kernel(down_ref, there_ref, lora_ref, lora_there, down_out, gate_out, up_out):
    part = down_ref.shape[0]
    core = lax.axis_index("dp")
    down, there = down_ref[...].astype(F32), there_ref[...].astype(F32)
    down_out[:part, :] = jnp.where(core == 0, down, there)
    down_out[part:, :] = jnp.where(core == 0, there, down)
    rank = gate_out.shape[0]
    gate_out[...] = lora_ref[:rank, :].astype(F32) + lora_there[:rank, :].astype(F32)
    up_out[...] = lora_ref[rank:, :].astype(F32) + lora_there[rank:, :].astype(F32)


def finish_kernel(capacity, choice_ref, *refs):
    parts, (low_ref, down_ref, out_ref, low_tall) = refs[:3], refs[3:]
    half = parts[0].shape[1]
    upper, lower = pick_rows(choice_ref[...], capacity)
    low = low_ref[...].astype(F32)[:capacity]
    zero = jnp.zeros_like(low)
    low_tall[:capacity, :] = low
    low_tall[capacity:, :] = zero
    low_upper = low_tall[...].astype(BF)
    low_tall[:capacity, :] = zero
    low_tall[capacity:, :] = low
    low_lower = low_tall[...].astype(BF)
    total = sum(x[...].astype(F32) for x in parts)
    total += dot(low_upper, down_ref[:, :half]) + dot(low_lower, down_ref[:, half:])
    total = total.astype(BF)
    out_ref[:, :half] = dot(upper, total, TN).astype(BF)
    out_ref[:, half:] = dot(lower, total, TN).astype(BF)


def in_hbm(x):
    return pltpu.with_memory_space_constraint(x, pltpu.HBM)


def in_vmem(x):
    return pltpu.with_memory_space_constraint(x, pltpu.VMEM)


def on_device(
    ring,
    tokens,
    output_gradient,
    token_expert_choice,
    routing_weight_table,
    stored_gate_rows,
    stored_up_rows,
    gate_weight,
    up_weight,
    down_weight,
    adapter_down_factor,
    adapter_gate_factor,
    adapter_up_factor,
):
    n = len(ring)
    tokens, output_gradient = tokens[0], output_gradient[0]
    own_count, width = tokens.shape
    half = width // 2
    capacity = stored_gate_rows.shape[1] // n
    hidden = stored_gate_rows.shape[2]
    rank = adapter_down_factor.shape[0]
    tall = -(-2 * capacity // 128) * 128
    slot = -(-capacity // 8) * 8
    cut = capacity // 16 * 16
    wide = half + 2 * rank
    middle = n // 2
    choice = token_expert_choice[0].T
    weights = routing_weight_table[0].T

    place = [0] * n
    for i, e in enumerate(ring):
        place[e] = i
    to_right = [(ring[i], ring[(i + 1) % n]) for i in range(n)]
    to_left = [(ring[i], ring[(i - 1) % n]) for i in range(n)]
    passes = [[0, -1, 1]] + [[-s, s] for s in range(2, middle)] + [[middle]]
    sizes = [len(group) for group in passes]
    order = [r for group in passes for r in group]
    heights = [cut, 2 * capacity - cut]

    def call(kernel, name, shapes, args, scratch=(), work=(0, 0), **more):
        return pl.pallas_call(
            kernel,
            out_shape=[jax.ShapeDtypeStruct(shape, dtype) for shape, dtype in shapes],
            scratch_shapes=list(scratch),
            compiler_params=pltpu.CompilerParams(vmem_limit_bytes=VMEM_LIMIT),
            cost_estimate=pl.CostEstimate(
                flops=int(work[0]), bytes_accessed=int(work[1]), transcendentals=0
            ),
            name=name,
            **more,
        )(*args)

    def right(x):
        return lax.ppermute(x, "expert", to_right)

    def left(x):
        return lax.ppermute(x, "expert", to_left)

    (block,) = call(
        functools.partial(prepare_kernel, capacity),
        "prepare",
        [((2 * capacity, wide), BF)],
        [in_hbm(x) for x in (choice, weights, output_gradient, tokens, adapter_down_factor)],
        [
            pltpu.VMEM(choice.shape, choice.dtype),
            pltpu.VMEM(weights.shape, BF),
            pltpu.VMEM(output_gradient.shape, BF),
            pltpu.VMEM(tokens.shape, BF),
            pltpu.VMEM(adapter_down_factor.shape, BF),
            pltpu.SemaphoreType.DMA((6,)),
        ],
        (4e8, 4.5e6),
        in_specs=[pl.BlockSpec(memory_space=pl.ANY)] * 5,
    )
    gate_rows, up_rows = call(
        functools.partial(reorder_kernel, place, capacity),
        "reorder",
        [((n, slot, hidden), BF)] * 2,
        [stored_gate_rows[0], stored_up_rows[0]],
        [pltpu.VMEM((n * capacity + slot, hidden), F32)],
        (0, 8 * n * slot * hidden),
    )

    down_here, gate_here, up_here = in_vmem(down_weight), in_vmem(gate_weight), in_vmem(up_weight)
    dgates, dups, low_rows, lows = [], [], [], []
    got = {0: (block,)}

    def hidden_pass(group):
        size, start, pieces = len(group), len(lows), len(got[group[0]])
        tall = -(-2 * capacity // 128) * 128 if size < 3 else -(-2 * capacity // 16) * 16
        results = call(
            functools.partial(hidden_kernel, capacity, slot, start, size, pieces),
            "hidden_rows",
            [((size, slot, hidden), BF)] * 2
            + [((size, slot, rank), BF)]
            + [((slot, rank), F32)] * size,
            [piece for r in group for piece in got[r]]
            + [gate_rows, up_rows, down_here, adapter_gate_factor, adapter_up_factor],
            [pltpu.VMEM((size * tall, half), BF)],
            (2 * size * tall * width * hidden, 2 * hidden * width),
        )
        dgates.append(results[0])
        dups.append(results[1])
        low_rows.append(results[2])
        lows.extend(results[3:])

    def to_owner(at):
        r = order[at]
        lows[at] = lax.ppermute(lows[at], "expert", [(ring[i], ring[(i + r) % n]) for i in range(n)])

    going_right = going_left = block
    sent = [0, 0]
    for s in range(1, middle):
        going_right, going_left = right(going_right), left(going_left)
        if s == 1:
            going_right, going_left, gate_rows, up_rows = lax.optimization_barrier(
                (going_right, going_left, gate_rows, up_rows)
            )
        else:
            hidden_pass(passes[s - 2])
            going_right, going_left, dgates[-1], dups[-1], lows[: sent[1]] = lax.optimization_barrier(
                (going_right, going_left, dgates[-1], dups[-1], lows[: sent[1]])
            )
            sent = [sent[1], len(lows)]
            for at in range(max(sent[0], 1), sent[1]):
                to_owner(at)
        got[-s], got[s] = (going_right,), (going_left,)
    right_top, left_rest = call(
        cut_kernel, "cut", [((h, wide), BF) for h in heights], [going_right, going_left]
    )
    right_top, left_rest = right(right_top), left(left_rest)
    hidden_pass(passes[-2])
    right_top, left_rest, dgates[-1], dups[-1], lows[: sent[1]] = lax.optimization_barrier(
        (right_top, left_rest, dgates[-1], dups[-1], lows[: sent[1]])
    )
    for at in range(max(sent[1], 1), len(lows)):
        to_owner(at)
    got[middle] = (right_top, left_rest)
    hidden_pass(passes[-1])

    right_top, left_rest = call(
        functools.partial(first_partial_kernel, capacity, slot, cut),
        "first_partial",
        [((h, half), BF) for h in heights],
        [dgates[-1], dups[-1], gate_here, up_here],
        [
            pltpu.VMEM((128, hidden), BF),
            pltpu.VMEM((128, hidden), BF),
            pltpu.VMEM((2 * capacity, half // 2), F32),
        ],
        (4 * slot * width * hidden, 4 * hidden * width),
    )
    right_top, left_rest, lows[-1] = lax.optimization_barrier((right_top, left_rest, lows[-1]))
    own = call(
        functools.partial(partial_kernel, capacity, slot, sizes[:-1]),
        "partials",
        [((2 * capacity, half), BF)] * (n - 1),
        [*dgates[:-1], *dups[:-1], gate_here, up_here],
        [
            pltpu.VMEM(((n - 1) * slot, hidden), BF),
            pltpu.VMEM(((n - 1) * slot, hidden), BF),
            pltpu.VMEM((2 * capacity, TILE), F32),
        ],
        (4 * (n - 1) * slot * width * hidden, 4 * hidden * width),
    )

    def add(a, b):
        return (a.astype(F32) + b.astype(F32)).astype(BF)

    def exchange(keep, send, bit):
        other = lax.ppermute(send, "expert", [(e, e ^ bit) for e in range(n)])
        count = keep.shape[0]
        parts = 2 if count > 1 else 1
        shape = (count // parts,) + keep.shape[1:]
        return call(halve_kernel, "halve", [(shape, keep.dtype)] * parts, [keep, other])

    right_top, left_rest = right(right_top), left(left_rest)
    to_owner(n - 1)
    right_top, left_rest, own, lows = lax.optimization_barrier((right_top, left_rest, own, lows))
    own = dict(zip(order[:-1], own))
    going_right, going_left = call(
        merge_kernel,
        "first_add",
        [((2 * capacity, half), BF)] * 2,
        [right_top, left_rest, own[middle - 1], own[1 - middle]],
    )

    share = width // n
    part = rank // 2
    swap = [(0, 1), (1, 0)]

    def adapter_gradient():
        if share % 128 == 0:
            low, keep, send = call(
                functools.partial(adapter_kernel, capacity),
                "adapter_gradient",
                [((slot, rank), BF)] + [((n, part, share), BF)] * 2,
                [choice, tokens, *lows],
                work=(2 * own_count * rank * width, 2 * own_count * width),
            )
        else:
            me, core = lax.axis_index("expert"), lax.axis_index("dp")
            upper, _ = pick_rows(choice, capacity)
            low = sum(lows).astype(BF)
            low_tokens = dot(upper[:slot], low, TN).astype(BF)
            down = dot(low_tokens, tokens, TN).astype(BF).reshape(rank, n, share)
            down = down.transpose(1, 0, 2)[jnp.arange(n, dtype=jnp.int32) ^ me]
            keep = jnp.where(core == 0, down[:, :part], down[:, part:])
            send = jnp.where(core == 0, down[:, part:], down[:, :part])
        other = lax.ppermute(send, "dp", swap)
        return low, call(halve_kernel, "halve", [((n // 2, part, share), BF)] * 2, [keep, other])

    def lora_gradients():
        (local,) = call(
            functools.partial(lora_kernel, slot, sizes),
            "lora_rows",
            [((2 * rank, hidden), BF)],
            [*dgates, *dups, *low_rows],
            [
                pltpu.VMEM((n * slot, hidden), BF),
                pltpu.VMEM((n * slot, hidden), BF),
                pltpu.VMEM((n * slot, rank), BF),
            ],
            (4 * n * slot * rank * hidden, 4 * n * slot * hidden),
        )
        return local, lax.ppermute(local, "dp", swap)

    bits = [1 << i for i in range(n.bit_length() - 1)]
    for hop, s in enumerate(range(middle - 1, 0, -1)):
        going_right, going_left = right(going_right), left(going_left)
        if hop == 0:
            low, pair = adapter_gradient()
        elif hop == 1:
            for bit in bits[:2]:
                pair = exchange(*pair, bit)
            low_rows, pair = lax.optimization_barrier((low_rows, pair))
        if s > 1:
            going_right, going_left, pair = lax.optimization_barrier((going_right, going_left, pair))
            going_right, going_left = add(going_right, own[s - 1]), add(going_left, own[1 - s])
    lora, lora_there = lora_gradients()
    for bit in bits[2:]:
        pair = exchange(*pair, bit)
    down = pair[0][0]
    there = lax.ppermute(down, "dp", swap)
    grad_down, grad_gate, grad_up = call(
        join_kernel,
        "join",
        [((rank, hidden), F32)] * 3,
        [down, there, lora, lora_there],
    )

    (input_gradient,) = call(
        functools.partial(finish_kernel, capacity),
        "finish",
        [((own_count, width), BF)],
        [choice, going_right, going_left, own[0], low, adapter_down_factor],
        [pltpu.VMEM((2 * capacity, rank), F32)],
        (4e8, 4.5e6),
    )
    return (input_gradient[None], grad_down, grad_gate, grad_up)


def solution(mesh):
    placed = (
        P(("groups", "dp"), "expert", None),
        P(("groups", "dp"), "expert", None),
        P(("groups", "dp"), "expert", None),
        P(("groups", "dp"), "expert", None),
        P(("groups", "dp"), None, "expert"),
        P(("groups", "dp"), None, "expert"),
        P(None, "expert"),
        P(None, "expert"),
        P("expert", None),
        P("groups", None),
        P("groups", "expert"),
        P("groups", "expert"),
    )
    return jax.shard_map(
        functools.partial(on_device, ring_order(mesh)),
        mesh=mesh,
        in_specs=placed,
        out_specs=(
            P(("groups", "dp"), "expert", None),
            P("groups", "expert"),
            P("groups", "expert"),
            P("groups", "expert"),
        ),
        check_vma=False,
    )
```

```python
import functools

import jax
import jax.numpy as jnp
from jax import lax
from jax.experimental import pallas as pl
from jax.experimental.pallas import tpu as pltpu
from jax.sharding import PartitionSpec as P

SCALE = 0.25
NT = (((1,), (1,)), ((), ()))
TN = (((0,), (0,)), ((), ()))
BF = jnp.bfloat16
F32 = jnp.float32
VMEM_LIMIT = 10 * 1024 * 1024
TILE = 256


def ring_order(mesh):
    count = mesh.shape["expert"]
    plain = list(range(count))
    if count < 4 or count % 2:
        return plain
    snake = list(range(0, count, 2)) + list(range(count - 1, 0, -2))
    spots = [getattr(d, "coords", None) for d in mesh.devices[0, :, 0]]
    if any(s is None for s in spots):
        return snake if count == 8 else plain

    def length(order):
        hops = zip(order, order[1:] + order[:1])
        return sum(sum(abs(a - b) for a, b in zip(spots[i], spots[j])) for i, j in hops)

    return min((plain, snake), key=length)


def dot(a, b, dims=None):
    if dims is None:
        dims = (((1,), (0,)), ((), ()))
    return lax.dot_general(a, b, dims, preferred_element_type=F32)


def pick_rows(choice, capacity):
    tokens = choice.shape[1]
    named = jnp.max((choice == 0).astype(F32), axis=0, keepdims=True)
    before = lax.broadcasted_iota(jnp.int32, (tokens, tokens), 0)
    after = lax.broadcasted_iota(jnp.int32, (tokens, tokens), 1)
    upto = (before <= after).astype(BF)
    count = dot(jnp.broadcast_to(named, (8, tokens)).astype(BF), upto)[:1]
    slot = jnp.where(named > 0, count - 1.0, -1000.0).astype(jnp.int32)
    row = lax.broadcasted_iota(jnp.int32, (2 * capacity, tokens), 0)
    return (row == slot).astype(BF), (row - capacity == slot).astype(BF)


def prepare_kernel(capacity, choice_hbm, weight_hbm, grad_hbm, tokens_hbm, down_hbm, block_ref,
                   choice_ref, weight_ref, grad_ref, tokens_ref, down_ref, sems):
    half = grad_ref.shape[1] // 2
    rank = down_ref.shape[0]
    pairs = [
        (choice_hbm, choice_ref),
        (grad_hbm.at[:, :half], grad_ref.at[:, :half]),
        (grad_hbm.at[:, half:], grad_ref.at[:, half:]),
        (weight_hbm, weight_ref),
        (down_hbm, down_ref),
        (tokens_hbm, tokens_ref),
    ]
    copies = [pltpu.make_async_copy(a, b, sems.at[i]) for i, (a, b) in enumerate(pairs)]
    for copy in copies:
        copy.start()
    copies[0].wait()
    choice = choice_ref[...]
    upper, lower = pick_rows(choice, capacity)
    copies[1].wait()
    first = dot(upper, grad_ref[:, :half])
    copies[2].wait()
    block_ref[:, :half] = (first + dot(lower, grad_ref[:, half:])).astype(BF)
    copies[3].wait()
    weight = jnp.sum(
        jnp.where(choice == 0, weight_ref[...].astype(F32), 0.0), axis=0, keepdims=True
    )
    column = jnp.sum(upper.astype(F32) * weight, axis=1, keepdims=True)
    block_ref[:, half + rank :] = jnp.broadcast_to(column, (2 * capacity, rank)).astype(BF)
    copies[4].wait()
    copies[5].wait()
    low = dot(tokens_ref[...], down_ref[...], NT).astype(BF)
    block_ref[:, half : half + rank] = dot(upper, low).astype(BF)


def cut_kernel(right_in, left_in, top, rest):
    cut = top.shape[0]
    top[...] = right_in[:cut, :]
    rest[...] = left_in[cut:, :]


def merge_kernel(top_in, rest_in, own_right, own_left, right_out, left_out):
    cut = top_in.shape[0]
    right_out[:cut, :] = (top_in[...].astype(F32) + own_right[:cut, :].astype(F32)).astype(BF)
    right_out[cut:, :] = own_right[cut:, :]
    left_out[:cut, :] = own_left[:cut, :]
    left_out[cut:, :] = (rest_in[...].astype(F32) + own_left[cut:, :].astype(F32)).astype(BF)


def place_here(place):
    me = lax.axis_index("expert")
    return me, sum(jnp.where(me == e, p, 0) for e, p in enumerate(place))


def reorder_kernel(place, capacity, gate_in, up_in, gate_out, up_out, tall):
    count, slot, hidden = gate_out.shape
    _, here = place_here(place)
    live = lax.broadcasted_iota(jnp.int32, (slot, hidden), 0) < capacity
    for source, target in ((gate_in, gate_out), (up_in, up_out)):
        tall[: count * capacity, :] = source[...].astype(F32)
        tall[count * capacity :, :] = jnp.zeros((slot, hidden), F32)
        for e in range(count):
            away = lax.rem(place[e] - here + count, count)
            at = jnp.where(2 * away < count, 2 * away, 2 * (count - away) - 1)
            rows = tall[e * capacity : e * capacity + slot, :]
            target[at] = jnp.where(live, rows, 0.0).astype(BF)


def low_order_kernel(ring, place, order, *refs):
    lows, out = refs[:-1], refs[-1]
    count = len(ring)
    _, here = place_here(place)
    for low, r in zip(lows, order):
        spot = lax.rem(here + r + count, count)
        owner = sum(jnp.where(spot == i, e, 0) for i, e in enumerate(ring))
        out[owner] = low[...]


def add_kernel(ours, theirs, out):
    out[...] = (ours[...].astype(F32) + theirs[...].astype(F32)).astype(out.dtype)


def sum_kernel(parts, out):
    out[...] = sum(parts[i].astype(F32) for i in range(parts.shape[0])).astype(out.dtype)


def hidden_kernel(capacity, slot, start, count, pieces, *refs):
    blocks, refs = [refs[i * pieces : (i + 1) * pieces] for i in range(count)], refs[count * pieces :]
    (gate_ref, up_ref, down_ref, lora_gate, lora_up, dgate_ref, dup_ref, low_ref), refs = refs[:8], refs[8:]
    lows, rows = refs[:count], refs[count]
    hidden, width = down_ref.shape
    half = width // 2
    rank = lora_gate.shape[0]
    tall = rows.shape[0] // count
    for i, block in enumerate(blocks):
        at = i * tall
        for piece in block:
            rows[at : at + piece.shape[0], :] = piece[:, :half]
            at += piece.shape[0]
    if tall % 128 == 0:
        first = dot(down_ref[:, :half], rows[...], NT).T
        second = dot(down_ref[:, half:], rows[...], NT).T
    else:
        first = dot(rows[...], down_ref[:, :half], NT)
        second = dot(rows[...], down_ref[:, half:], NT)
    live = lax.broadcasted_iota(jnp.int32, (slot, hidden), 0) < capacity
    for i in range(count):
        at = i * tall
        extras, seen = [], 0
        for piece in blocks[i]:
            height = min(piece.shape[0], slot - seen)
            extras.append(piece[:height, half:])
            low_ref[i, seen : seen + height, :] = extras[-1][:, :rank]
            seen += height
        weight = jnp.concatenate([x.astype(F32)[:, rank : rank + 1] for x in extras], axis=0)
        grad = (first[at : at + slot] + second[at + capacity : at + capacity + slot]) * weight
        grad = jnp.where(live, grad, 0.0)
        gate = gate_ref[start + i].astype(F32)
        up = up_ref[start + i].astype(F32)
        sig = 1.0 / (1.0 + jnp.exp(-gate))
        slope = sig * (1.0 + gate * (1.0 - sig))
        dgate = (grad * up * slope).astype(BF)
        dup = (grad * gate * sig).astype(BF)
        dgate_ref[i] = dgate
        dup_ref[i] = dup
        lows[i][...] = SCALE * (dot(dgate, lora_gate[...], NT) + dot(dup, lora_up[...], NT))


def stack(groups, slot, sources, target):
    at = 0
    for size, source in zip(groups, sources):
        for i in range(size):
            target[at : at + slot, :] = source[i]
            at += slot


def lora_kernel(slot, groups, *refs):
    pieces = len(groups)
    dgates, dups, lows = refs[:pieces], refs[pieces : 2 * pieces], refs[2 * pieces : 3 * pieces]
    lora_out, dgate, dup, low = refs[3 * pieces :]
    rank = lora_out.shape[0] // 2
    stack(groups, slot, dgates, dgate)
    stack(groups, slot, dups, dup)
    stack(groups, slot, lows, low)
    lora_out[:rank, :] = (SCALE * dot(low[...], dgate[...], TN)).astype(BF)
    lora_out[rank:, :] = (SCALE * dot(low[...], dup[...], TN)).astype(BF)


def first_partial_kernel(capacity, slot, cut, dgate_in, dup_in, gate_ref, up_ref, top, rest, dgate, dup, tile):
    half = gate_ref.shape[0] // 2
    dgate[:slot, :] = dgate_in[0]
    dup[:slot, :] = dup_in[0]
    step = tile.shape[1]
    for t in range(0, half, step):
        for at, place in ((t, 0), (t + half, capacity)):
            total = dot(gate_ref[at : at + step, :], dgate[...], NT) + dot(up_ref[at : at + step, :], dup[...], NT)
            tile[place : place + capacity, :] = total.T[:capacity]
        top[:, t : t + step] = tile[:cut, :].astype(BF)
        rest[:, t : t + step] = tile[cut:, :].astype(BF)


def partial_kernel(capacity, slot, groups, *refs):
    members, pieces = sum(groups), len(groups)
    dgates, dups, refs = refs[:pieces], refs[pieces : 2 * pieces], refs[2 * pieces :]
    gate_ref, up_ref, outs, (dgate, dup, tile) = refs[0], refs[1], refs[2:-3], refs[-3:]
    half = gate_ref.shape[0] // 2
    stack(groups, slot, dgates, dgate)
    stack(groups, slot, dups, dup)

    for t in range(0, half, TILE):
        sums = []
        for at in (t, t + half):
            sums.append(
                dot(dgate[...], gate_ref[at : at + TILE, :], NT)
                + dot(dup[...], up_ref[at : at + TILE, :], NT)
            )
        for i in range(members):
            at = i * slot
            tile[:capacity, :] = sums[0][at : at + capacity]
            tile[capacity:, :] = sums[1][at : at + capacity]
            outs[i][:, t : t + TILE] = tile[...].astype(BF)


def adapter_kernel(capacity, choice_ref, tokens_ref, lows, low_ref, keep_ref, send_ref):
    count, part, share = keep_ref.shape
    low = sum(lows[i] for i in range(count)).astype(BF)
    low_ref[...] = low
    upper, _ = pick_rows(choice_ref[...], capacity)
    low = dot(upper[: low.shape[0]], low, TN).astype(BF)
    core = lax.axis_index("dp")
    for i in range(count):
        down = dot(low, tokens_ref[:, i * share : (i + 1) * share], TN)
        keep_ref[i] = jnp.where(core == 0, down[:part], down[part:]).astype(BF)
        send_ref[i] = jnp.where(core == 0, down[part:], down[:part]).astype(BF)


def join_kernel(down_ref, there_ref, lora_ref, lora_there, down_out, gate_out, up_out):
    part = down_ref.shape[0]
    core = lax.axis_index("dp")
    down, there = down_ref[...].astype(F32), there_ref[...].astype(F32)
    down_out[:part, :] = jnp.where(core == 0, down, there)
    down_out[part:, :] = jnp.where(core == 0, there, down)
    rank = gate_out.shape[0]
    gate_out[...] = lora_ref[:rank, :].astype(F32) + lora_there[:rank, :].astype(F32)
    up_out[...] = lora_ref[rank:, :].astype(F32) + lora_there[rank:, :].astype(F32)


def finish_kernel(capacity, choice_ref, *refs):
    parts, (low_ref, down_ref, out_ref, low_tall) = refs[:3], refs[3:]
    half = parts[0].shape[1]
    upper, lower = pick_rows(choice_ref[...], capacity)
    low = low_ref[...].astype(F32)[:capacity]
    zero = jnp.zeros_like(low)
    low_tall[:capacity, :] = low
    low_tall[capacity:, :] = zero
    low_upper = low_tall[...].astype(BF)
    low_tall[:capacity, :] = zero
    low_tall[capacity:, :] = low
    low_lower = low_tall[...].astype(BF)
    total = sum(x[...].astype(F32) for x in parts)
    total += dot(low_upper, down_ref[:, :half]) + dot(low_lower, down_ref[:, half:])
    total = total.astype(BF)
    out_ref[:, :half] = dot(upper, total, TN).astype(BF)
    out_ref[:, half:] = dot(lower, total, TN).astype(BF)


def in_hbm(x):
    return pltpu.with_memory_space_constraint(x, pltpu.HBM)


def in_vmem(x):
    return pltpu.with_memory_space_constraint(x, pltpu.VMEM)


def on_device(
    ring,
    tokens,
    output_gradient,
    token_expert_choice,
    routing_weight_table,
    stored_gate_rows,
    stored_up_rows,
    gate_weight,
    up_weight,
    down_weight,
    adapter_down_factor,
    adapter_gate_factor,
    adapter_up_factor,
):
    n = len(ring)
    tokens, output_gradient = tokens[0], output_gradient[0]
    own_count, width = tokens.shape
    half = width // 2
    capacity = stored_gate_rows.shape[1] // n
    hidden = stored_gate_rows.shape[2]
    rank = adapter_down_factor.shape[0]
    tall = -(-2 * capacity // 128) * 128
    slot = -(-capacity // 8) * 8
    cut = capacity // 16 * 16
    wide = half + 2 * rank
    middle = n // 2
    choice = token_expert_choice[0].T
    weights = routing_weight_table[0].T

    place = [0] * n
    for i, e in enumerate(ring):
        place[e] = i
    to_right = [(ring[i], ring[(i + 1) % n]) for i in range(n)]
    to_left = [(ring[i], ring[(i - 1) % n]) for i in range(n)]
    passes = [[0, -1, 1]] + [[-s, s] for s in range(2, middle)] + [[middle]]
    sizes = [len(group) for group in passes]
    order = [r for group in passes for r in group]
    heights = [cut, 2 * capacity - cut]

    def call(kernel, name, shapes, args, scratch=(), work=(0, 0), **more):
        return pl.pallas_call(
            kernel,
            out_shape=[jax.ShapeDtypeStruct(shape, dtype) for shape, dtype in shapes],
            scratch_shapes=list(scratch),
            compiler_params=pltpu.CompilerParams(vmem_limit_bytes=VMEM_LIMIT),
            cost_estimate=pl.CostEstimate(
                flops=int(work[0]), bytes_accessed=int(work[1]), transcendentals=0
            ),
            name=name,
            **more,
        )(*args)

    def right(x):
        return lax.ppermute(x, "expert", to_right)

    def left(x):
        return lax.ppermute(x, "expert", to_left)

    (block,) = call(
        functools.partial(prepare_kernel, capacity),
        "prepare",
        [((2 * capacity, wide), BF)],
        [in_hbm(x) for x in (choice, weights, output_gradient, tokens, adapter_down_factor)],
        [
            pltpu.VMEM(choice.shape, choice.dtype),
            pltpu.VMEM(weights.shape, BF),
            pltpu.VMEM(output_gradient.shape, BF),
            pltpu.VMEM(tokens.shape, BF),
            pltpu.VMEM(adapter_down_factor.shape, BF),
            pltpu.SemaphoreType.DMA((6,)),
        ],
        (4e8, 4.5e6),
        in_specs=[pl.BlockSpec(memory_space=pl.ANY)] * 5,
    )
    gate_rows, up_rows = call(
        functools.partial(reorder_kernel, place, capacity),
        "reorder",
        [((n, slot, hidden), BF)] * 2,
        [stored_gate_rows[0], stored_up_rows[0]],
        [pltpu.VMEM((n * capacity + slot, hidden), F32)],
        (0, 8 * n * slot * hidden),
    )

    down_here, gate_here, up_here = in_vmem(down_weight), in_vmem(gate_weight), in_vmem(up_weight)
    dgates, dups, low_rows, lows = [], [], [], []
    got = {0: (block,)}

    def hidden_pass(group):
        size, start, pieces = len(group), len(lows), len(got[group[0]])
        tall = -(-2 * capacity // 128) * 128 if size < 3 else -(-2 * capacity // 16) * 16
        results = call(
            functools.partial(hidden_kernel, capacity, slot, start, size, pieces),
            "hidden_rows",
            [((size, slot, hidden), BF)] * 2
            + [((size, slot, rank), BF)]
            + [((slot, rank), F32)] * size,
            [piece for r in group for piece in got[r]]
            + [gate_rows, up_rows, down_here, adapter_gate_factor, adapter_up_factor],
            [pltpu.VMEM((size * tall, half), BF)],
            (2 * size * tall * width * hidden, 2 * hidden * width),
        )
        dgates.append(results[0])
        dups.append(results[1])
        low_rows.append(results[2])
        lows.extend(results[3:])

    going_right = going_left = block
    for s in range(1, middle):
        going_right, going_left = right(going_right), left(going_left)
        if s == 1:
            going_right, going_left, gate_rows, up_rows = lax.optimization_barrier(
                (going_right, going_left, gate_rows, up_rows)
            )
        else:
            hidden_pass(passes[s - 2])
            going_right, going_left, dgates[-1], dups[-1] = lax.optimization_barrier(
                (going_right, going_left, dgates[-1], dups[-1])
            )
        got[-s], got[s] = (going_right,), (going_left,)
    right_top, left_rest = call(
        cut_kernel, "cut", [((h, wide), BF) for h in heights], [going_right, going_left]
    )
    right_top, left_rest = right(right_top), left(left_rest)
    hidden_pass(passes[-2])
    right_top, left_rest, dgates[-1], dups[-1] = lax.optimization_barrier(
        (right_top, left_rest, dgates[-1], dups[-1])
    )
    got[middle] = (right_top, left_rest)
    hidden_pass(passes[-1])
    (low_parts,) = call(
        functools.partial(low_order_kernel, ring, place, order), "low_order", [((n, slot, rank), F32)], lows
    )
    low_parts = lax.all_to_all(low_parts, "expert", 0, 0)

    right_top, left_rest = call(
        functools.partial(first_partial_kernel, capacity, slot, cut),
        "first_partial",
        [((h, half), BF) for h in heights],
        [dgates[-1], dups[-1], gate_here, up_here],
        [
            pltpu.VMEM((128, hidden), BF),
            pltpu.VMEM((128, hidden), BF),
            pltpu.VMEM((2 * capacity, half // 2), F32),
        ],
        (4 * slot * width * hidden, 4 * hidden * width),
    )
    own = call(
        functools.partial(partial_kernel, capacity, slot, sizes[:-1]),
        "partials",
        [((2 * capacity, half), BF)] * (n - 1),
        [*dgates[:-1], *dups[:-1], gate_here, up_here],
        [
            pltpu.VMEM(((n - 1) * slot, hidden), BF),
            pltpu.VMEM(((n - 1) * slot, hidden), BF),
            pltpu.VMEM((2 * capacity, TILE), F32),
        ],
        (4 * (n - 1) * slot * width * hidden, 4 * hidden * width),
    )

    def add(a, b):
        return (a.astype(F32) + b.astype(F32)).astype(BF)

    right_top, left_rest = right(right_top), left(left_rest)
    right_top, left_rest, low_parts, own = lax.optimization_barrier((right_top, left_rest, low_parts, own))
    own = dict(zip(order[:-1], own))
    going_right, going_left = call(
        merge_kernel,
        "first_add",
        [((2 * capacity, half), BF)] * 2,
        [right_top, left_rest, own[middle - 1], own[1 - middle]],
    )

    share = width // n
    part = rank // 2
    swap = [(0, 1), (1, 0)]

    def adapter_gradient():
        if share % 128 == 0:
            low, keep, send = call(
                functools.partial(adapter_kernel, capacity),
                "adapter_gradient",
                [((slot, rank), BF)] + [((n, part, share), BF)] * 2,
                [choice, tokens, low_parts],
                work=(2 * own_count * rank * width, 2 * own_count * width),
            )
        else:
            core = lax.axis_index("dp")
            upper, _ = pick_rows(choice, capacity)
            low = jnp.sum(low_parts, axis=0).astype(BF)
            low_tokens = dot(upper[:slot], low, TN).astype(BF)
            down = dot(low_tokens, tokens, TN).astype(BF).reshape(rank, n, share)
            down = down.transpose(1, 0, 2)
            keep = jnp.where(core == 0, down[:, :part], down[:, part:])
            send = jnp.where(core == 0, down[:, part:], down[:, :part])
        other = lax.ppermute(send, "dp", swap)
        return low, call(add_kernel, "add_dp", [((n, part, share), BF)], [keep, other])[0]

    def lora_gradients():
        (local,) = call(
            functools.partial(lora_kernel, slot, sizes),
            "lora_rows",
            [((2 * rank, hidden), BF)],
            [*dgates, *dups, *low_rows],
            [
                pltpu.VMEM((n * slot, hidden), BF),
                pltpu.VMEM((n * slot, hidden), BF),
                pltpu.VMEM((n * slot, rank), BF),
            ],
            (4 * n * slot * rank * hidden, 4 * n * slot * hidden),
        )
        return local, lax.ppermute(local, "dp", swap)

    for hop, s in enumerate(range(middle - 1, 0, -1)):
        going_right, going_left = right(going_right), left(going_left)
        if hop == 0:
            low, parts = adapter_gradient()
            going_right, going_left, parts = lax.optimization_barrier((going_right, going_left, parts))
            parts = lax.all_to_all(parts, "expert", 0, 0)
        if s > 1:
            going_right, going_left = add(going_right, own[s - 1]), add(going_left, own[1 - s])
    low_rows, parts = lax.optimization_barrier((low_rows, parts))
    lora, lora_there = lora_gradients()
    (down,) = call(sum_kernel, "sum_expert", [((part, share), BF)], [parts])
    there = lax.ppermute(down, "dp", swap)
    grad_down, grad_gate, grad_up = call(
        join_kernel,
        "join",
        [((rank, hidden), F32)] * 3,
        [down, there, lora, lora_there],
    )

    (input_gradient,) = call(
        functools.partial(finish_kernel, capacity),
        "finish",
        [((own_count, width), BF)],
        [choice, going_right, going_left, own[0], low, adapter_down_factor],
        [pltpu.VMEM((2 * capacity, rank), F32)],
        (4e8, 4.5e6),
    )
    return (input_gradient[None], grad_down, grad_gate, grad_up)


def solution(mesh):
    placed = (
        P(("groups", "dp"), "expert", None),
        P(("groups", "dp"), "expert", None),
        P(("groups", "dp"), "expert", None),
        P(("groups", "dp"), "expert", None),
        P(("groups", "dp"), None, "expert"),
        P(("groups", "dp"), None, "expert"),
        P(None, "expert"),
        P(None, "expert"),
        P("expert", None),
        P("groups", None),
        P("groups", "expert"),
        P("groups", "expert"),
    )
    return jax.shard_map(
        functools.partial(on_device, ring_order(mesh)),
        mesh=mesh,
        in_specs=placed,
        out_specs=(
            P(("groups", "dp"), "expert", None),
            P("groups", "expert"),
            P("groups", "expert"),
            P("groups", "expert"),
        ),
        check_vma=False,
    )
```

```python
import functools

import jax
import jax.numpy as jnp
from jax import lax
from jax.experimental import pallas as pl
from jax.experimental.pallas import tpu as pltpu
from jax.sharding import PartitionSpec as P

SCALE = 0.25
NT = (((1,), (1,)), ((), ()))
TN = (((0,), (0,)), ((), ()))
BF = jnp.bfloat16
F32 = jnp.float32
VMEM_LIMIT = 10 * 1024 * 1024
TILE = 256


def ring_order(mesh):
    count = mesh.shape["expert"]
    plain = list(range(count))
    if count < 4 or count % 2:
        return plain
    snake = list(range(0, count, 2)) + list(range(count - 1, 0, -2))
    spots = [getattr(d, "coords", None) for d in mesh.devices[0, :, 0]]
    if any(s is None for s in spots):
        return snake if count == 8 else plain

    def length(order):
        hops = zip(order, order[1:] + order[:1])
        return sum(sum(abs(a - b) for a, b in zip(spots[i], spots[j])) for i, j in hops)

    return min((plain, snake), key=length)


def dot(a, b, dims=None):
    if dims is None:
        dims = (((1,), (0,)), ((), ()))
    return lax.dot_general(a, b, dims, preferred_element_type=F32)


def pick_rows(choice, capacity):
    tokens = choice.shape[1]
    named = jnp.max((choice == 0).astype(F32), axis=0, keepdims=True)
    before = lax.broadcasted_iota(jnp.int32, (tokens, tokens), 0)
    after = lax.broadcasted_iota(jnp.int32, (tokens, tokens), 1)
    upto = (before <= after).astype(BF)
    count = dot(jnp.broadcast_to(named, (8, tokens)).astype(BF), upto)[:1]
    slot = jnp.where(named > 0, count - 1.0, -1000.0).astype(jnp.int32)
    row = lax.broadcasted_iota(jnp.int32, (2 * capacity, tokens), 0)
    return (row == slot).astype(BF), (row - capacity == slot).astype(BF)


def prepare_kernel(capacity, choice_hbm, weight_hbm, grad_hbm, tokens_hbm, down_hbm, block_ref,
                   choice_ref, weight_ref, grad_ref, tokens_ref, down_ref, sems):
    half = grad_ref.shape[1] // 2
    rank = down_ref.shape[0]
    pairs = [
        (choice_hbm, choice_ref),
        (grad_hbm.at[:, :half], grad_ref.at[:, :half]),
        (grad_hbm.at[:, half:], grad_ref.at[:, half:]),
        (weight_hbm, weight_ref),
        (down_hbm, down_ref),
        (tokens_hbm, tokens_ref),
    ]
    copies = [pltpu.make_async_copy(a, b, sems.at[i]) for i, (a, b) in enumerate(pairs)]
    for copy in copies:
        copy.start()
    copies[0].wait()
    choice = choice_ref[...]
    upper, lower = pick_rows(choice, capacity)
    copies[1].wait()
    first = dot(upper, grad_ref[:, :half])
    copies[2].wait()
    block_ref[:, :half] = (first + dot(lower, grad_ref[:, half:])).astype(BF)
    copies[3].wait()
    weight = jnp.sum(
        jnp.where(choice == 0, weight_ref[...].astype(F32), 0.0), axis=0, keepdims=True
    )
    column = jnp.sum(upper.astype(F32) * weight, axis=1, keepdims=True)
    block_ref[:, half + rank :] = jnp.broadcast_to(column, (2 * capacity, rank)).astype(BF)
    copies[4].wait()
    copies[5].wait()
    low = dot(tokens_ref[...], down_ref[...], NT).astype(BF)
    block_ref[:, half : half + rank] = dot(upper, low).astype(BF)


def cut_kernel(right_in, left_in, top, rest):
    cut = top.shape[0]
    top[...] = right_in[:cut, :]
    rest[...] = left_in[cut:, :]


def merge_kernel(top_in, rest_in, own_right, own_left, right_out, left_out):
    cut = top_in.shape[0]
    right_out[:cut, :] = (top_in[...].astype(F32) + own_right[:cut, :].astype(F32)).astype(BF)
    right_out[cut:, :] = own_right[cut:, :]
    left_out[:cut, :] = own_left[:cut, :]
    left_out[cut:, :] = (rest_in[...].astype(F32) + own_left[cut:, :].astype(F32)).astype(BF)


def place_here(place):
    me = lax.axis_index("expert")
    return me, sum(jnp.where(me == e, p, 0) for e, p in enumerate(place))


def reorder_kernel(place, capacity, gate_in, up_in, gate_out, up_out, tall):
    count, slot, hidden = gate_out.shape
    _, here = place_here(place)
    live = lax.broadcasted_iota(jnp.int32, (slot, hidden), 0) < capacity
    for source, target in ((gate_in, gate_out), (up_in, up_out)):
        tall[: count * capacity, :] = source[...].astype(F32)
        tall[count * capacity :, :] = jnp.zeros((slot, hidden), F32)
        for e in range(count):
            away = lax.rem(place[e] - here + count, count)
            at = jnp.where(2 * away < count, 2 * away, 2 * (count - away) - 1)
            rows = tall[e * capacity : e * capacity + slot, :]
            target[at] = jnp.where(live, rows, 0.0).astype(BF)


def low_order_kernel(ring, place, order, *refs):
    lows, (keep, send) = refs[:-2], refs[-2:]
    count = len(ring)
    me, here = place_here(place)
    for low, r in zip(lows, order):
        spot = lax.rem(here + r + count, count)
        owner = sum(jnp.where(spot == i, e, 0) for i, e in enumerate(ring))
        key = owner ^ me

        @pl.when(key % 2 == 0)
        def _(low=low, key=key):
            keep[key // 2] = low[...]

        @pl.when(key % 2 == 1)
        def _(low=low, key=key):
            send[key // 2] = low[...]


def halve_kernel(ours, theirs, *outs):
    count = ours.shape[0]
    for i in range(count):
        total = ours[i].astype(F32) + theirs[i].astype(F32)
        out = outs[i % len(outs)]
        out[i // len(outs)] = total.astype(out.dtype)


def hidden_kernel(capacity, slot, start, count, pieces, *refs):
    blocks, refs = [refs[i * pieces : (i + 1) * pieces] for i in range(count)], refs[count * pieces :]
    (gate_ref, up_ref, down_ref, lora_gate, lora_up, dgate_ref, dup_ref, low_ref), refs = refs[:8], refs[8:]
    lows, rows = refs[:count], refs[count]
    hidden, width = down_ref.shape
    half = width // 2
    rank = lora_gate.shape[0]
    tall = rows.shape[0] // count
    for i, block in enumerate(blocks):
        at = i * tall
        for piece in block:
            rows[at : at + piece.shape[0], :] = piece[:, :half]
            at += piece.shape[0]
    if tall % 128 == 0:
        first = dot(down_ref[:, :half], rows[...], NT).T
        second = dot(down_ref[:, half:], rows[...], NT).T
    else:
        first = dot(rows[...], down_ref[:, :half], NT)
        second = dot(rows[...], down_ref[:, half:], NT)
    live = lax.broadcasted_iota(jnp.int32, (slot, hidden), 0) < capacity
    for i in range(count):
        at = i * tall
        extras, seen = [], 0
        for piece in blocks[i]:
            height = min(piece.shape[0], slot - seen)
            extras.append(piece[:height, half:])
            low_ref[i, seen : seen + height, :] = extras[-1][:, :rank]
            seen += height
        weight = jnp.concatenate([x.astype(F32)[:, rank : rank + 1] for x in extras], axis=0)
        grad = (first[at : at + slot] + second[at + capacity : at + capacity + slot]) * weight
        grad = jnp.where(live, grad, 0.0)
        gate = gate_ref[start + i].astype(F32)
        up = up_ref[start + i].astype(F32)
        sig = 1.0 / (1.0 + jnp.exp(-gate))
        slope = sig * (1.0 + gate * (1.0 - sig))
        dgate = (grad * up * slope).astype(BF)
        dup = (grad * gate * sig).astype(BF)
        dgate_ref[i] = dgate
        dup_ref[i] = dup
        lows[i][...] = SCALE * (dot(dgate, lora_gate[...], NT) + dot(dup, lora_up[...], NT))


def stack(groups, slot, sources, target):
    at = 0
    for size, source in zip(groups, sources):
        for i in range(size):
            target[at : at + slot, :] = source[i]
            at += slot


def lora_kernel(slot, groups, *refs):
    pieces = len(groups)
    dgates, dups, lows = refs[:pieces], refs[pieces : 2 * pieces], refs[2 * pieces : 3 * pieces]
    lora_out, dgate, dup, low = refs[3 * pieces :]
    rank = lora_out.shape[0] // 2
    stack(groups, slot, dgates, dgate)
    stack(groups, slot, dups, dup)
    stack(groups, slot, lows, low)
    lora_out[:rank, :] = (SCALE * dot(low[...], dgate[...], TN)).astype(BF)
    lora_out[rank:, :] = (SCALE * dot(low[...], dup[...], TN)).astype(BF)


def partial_kernel(capacity, slot, groups, cut, *refs):
    members, pieces = sum(groups), len(groups)
    dgates, dups, refs = refs[:pieces], refs[pieces : 2 * pieces], refs[2 * pieces :]
    gate_ref, up_ref, outs, (dgate, dup, tile) = refs[0], refs[1], refs[2:-3], refs[-3:]
    half = gate_ref.shape[0] // 2
    stack(groups, slot, dgates, dgate)
    stack(groups, slot, dups, dup)

    for t in range(0, half, TILE):
        sums = []
        for at in (t, t + half):
            sums.append(
                dot(dgate[...], gate_ref[at : at + TILE, :], NT)
                + dot(dup[...], up_ref[at : at + TILE, :], NT)
            )
        for i in range(members):
            at = i * slot
            tile[:capacity, :] = sums[0][at : at + capacity]
            tile[capacity:, :] = sums[1][at : at + capacity]
            if i < members - 1:
                outs[i][:, t : t + TILE] = tile[...].astype(BF)
            else:
                outs[i][:, t : t + TILE] = tile[:cut, :].astype(BF)
                outs[i + 1][:, t : t + TILE] = tile[cut:, :].astype(BF)


def adapter_kernel(capacity, choice_ref, tokens_ref, low_in, low_ref, keep_ref, send_ref):
    count, part, share = keep_ref.shape
    low = low_in[0].astype(BF)
    low_ref[...] = low
    upper, _ = pick_rows(choice_ref[...], capacity)
    low = dot(upper[: low.shape[0]], low, TN).astype(BF)
    me, core = lax.axis_index("expert"), lax.axis_index("dp")
    for i in range(count):
        columns = pl.ds(pl.multiple_of((me ^ i) * share, 128), share)
        down = dot(low, tokens_ref[:, columns], TN)
        keep_ref[i] = jnp.where(core == 0, down[:part], down[part:]).astype(BF)
        send_ref[i] = jnp.where(core == 0, down[part:], down[:part]).astype(BF)


def join_kernel(down_ref, there_ref, lora_ref, lora_there, down_out, gate_out, up_out):
    part = down_ref.shape[0]
    core = lax.axis_index("dp")
    down, there = down_ref[...].astype(F32), there_ref[...].astype(F32)
    down_out[:part, :] = jnp.where(core == 0, down, there)
    down_out[part:, :] = jnp.where(core == 0, there, down)
    rank = gate_out.shape[0]
    gate_out[...] = lora_ref[:rank, :].astype(F32) + lora_there[:rank, :].astype(F32)
    up_out[...] = lora_ref[rank:, :].astype(F32) + lora_there[rank:, :].astype(F32)


def finish_kernel(capacity, choice_ref, *refs):
    parts, (low_ref, down_ref, out_ref, low_tall) = refs[:3], refs[3:]
    half = parts[0].shape[1]
    upper, lower = pick_rows(choice_ref[...], capacity)
    low = low_ref[...].astype(F32)[:capacity]
    zero = jnp.zeros_like(low)
    low_tall[:capacity, :] = low
    low_tall[capacity:, :] = zero
    low_upper = low_tall[...].astype(BF)
    low_tall[:capacity, :] = zero
    low_tall[capacity:, :] = low
    low_lower = low_tall[...].astype(BF)
    total = sum(x[...].astype(F32) for x in parts)
    total += dot(low_upper, down_ref[:, :half]) + dot(low_lower, down_ref[:, half:])
    total = total.astype(BF)
    out_ref[:, :half] = dot(upper, total, TN).astype(BF)
    out_ref[:, half:] = dot(lower, total, TN).astype(BF)


def in_hbm(x):
    return pltpu.with_memory_space_constraint(x, pltpu.HBM)


def in_vmem(x):
    return pltpu.with_memory_space_constraint(x, pltpu.VMEM)


def on_device(
    ring,
    tokens,
    output_gradient,
    token_expert_choice,
    routing_weight_table,
    stored_gate_rows,
    stored_up_rows,
    gate_weight,
    up_weight,
    down_weight,
    adapter_down_factor,
    adapter_gate_factor,
    adapter_up_factor,
):
    n = len(ring)
    tokens, output_gradient = tokens[0], output_gradient[0]
    own_count, width = tokens.shape
    half = width // 2
    capacity = stored_gate_rows.shape[1] // n
    hidden = stored_gate_rows.shape[2]
    rank = adapter_down_factor.shape[0]
    tall = -(-2 * capacity // 128) * 128
    slot = -(-capacity // 8) * 8
    cut = capacity // 16 * 16
    wide = half + 2 * rank
    middle = n // 2
    choice = token_expert_choice[0].T
    weights = routing_weight_table[0].T

    place = [0] * n
    for i, e in enumerate(ring):
        place[e] = i
    to_right = [(ring[i], ring[(i + 1) % n]) for i in range(n)]
    to_left = [(ring[i], ring[(i - 1) % n]) for i in range(n)]
    passes = [[0, -1, 1]] + [[-s, s] for s in range(2, middle)] + [[middle]]
    sizes = [len(group) for group in passes]
    order = [r for group in passes for r in group]
    heights = [cut, 2 * capacity - cut]

    def call(kernel, name, shapes, args, scratch=(), work=(0, 0), **more):
        return pl.pallas_call(
            kernel,
            out_shape=[jax.ShapeDtypeStruct(shape, dtype) for shape, dtype in shapes],
            scratch_shapes=list(scratch),
            compiler_params=pltpu.CompilerParams(vmem_limit_bytes=VMEM_LIMIT),
            cost_estimate=pl.CostEstimate(
                flops=int(work[0]), bytes_accessed=int(work[1]), transcendentals=0
            ),
            name=name,
            **more,
        )(*args)

    def right(x):
        return lax.ppermute(x, "expert", to_right)

    def left(x):
        return lax.ppermute(x, "expert", to_left)

    (block,) = call(
        functools.partial(prepare_kernel, capacity),
        "prepare",
        [((2 * capacity, wide), BF)],
        [in_hbm(x) for x in (choice, weights, output_gradient, tokens, adapter_down_factor)],
        [
            pltpu.VMEM(choice.shape, choice.dtype),
            pltpu.VMEM(weights.shape, BF),
            pltpu.VMEM(output_gradient.shape, BF),
            pltpu.VMEM(tokens.shape, BF),
            pltpu.VMEM(adapter_down_factor.shape, BF),
            pltpu.SemaphoreType.DMA((6,)),
        ],
        (4e8, 4.5e6),
        in_specs=[pl.BlockSpec(memory_space=pl.ANY)] * 5,
    )
    gate_rows, up_rows = call(
        functools.partial(reorder_kernel, place, capacity),
        "reorder",
        [((n, slot, hidden), BF)] * 2,
        [stored_gate_rows[0], stored_up_rows[0]],
        [pltpu.VMEM((n * capacity + slot, hidden), F32)],
        (0, 8 * n * slot * hidden),
    )

    down_here, gate_here, up_here = in_vmem(down_weight), in_vmem(gate_weight), in_vmem(up_weight)
    dgates, dups, low_rows, lows = [], [], [], []
    got = {0: (block,)}

    def hidden_pass(group):
        size, start, pieces = len(group), len(lows), len(got[group[0]])
        tall = -(-2 * capacity // 128) * 128 if size < 3 else -(-2 * capacity // 16) * 16
        results = call(
            functools.partial(hidden_kernel, capacity, slot, start, size, pieces),
            "hidden_rows",
            [((size, slot, hidden), BF)] * 2
            + [((size, slot, rank), BF)]
            + [((slot, rank), F32)] * size,
            [piece for r in group for piece in got[r]]
            + [gate_rows, up_rows, down_here, adapter_gate_factor, adapter_up_factor],
            [pltpu.VMEM((size * tall, half), BF)],
            (2 * size * tall * width * hidden, 2 * hidden * width),
        )
        dgates.append(results[0])
        dups.append(results[1])
        low_rows.append(results[2])
        lows.extend(results[3:])

    going_right = going_left = block
    for s in range(1, middle):
        going_right, going_left = right(going_right), left(going_left)
        if s == 1:
            going_right, going_left, gate_rows, up_rows = lax.optimization_barrier(
                (going_right, going_left, gate_rows, up_rows)
            )
        else:
            hidden_pass(passes[s - 2])
            going_right, going_left, dgates[-1], dups[-1] = lax.optimization_barrier(
                (going_right, going_left, dgates[-1], dups[-1])
            )
        got[-s], got[s] = (going_right,), (going_left,)
    right_top, left_rest = call(
        cut_kernel, "cut", [((h, wide), BF) for h in heights], [going_right, going_left]
    )
    right_top, left_rest = right(right_top), left(left_rest)
    hidden_pass(passes[-2])
    right_top, left_rest, dgates[-1], dups[-1] = lax.optimization_barrier(
        (right_top, left_rest, dgates[-1], dups[-1])
    )
    got[middle] = (right_top, left_rest)
    hidden_pass(passes[-1])

    low_keep, low_send = call(
        functools.partial(low_order_kernel, ring, place, order),
        "low_order",
        [((n // 2, slot, rank), F32)] * 2,
        lows,
    )
    *own, right_top, left_rest = call(
        functools.partial(partial_kernel, capacity, slot, sizes, cut),
        "partials",
        [((2 * capacity, half), BF)] * (n - 1) + [((h, half), BF) for h in heights],
        [*dgates, *dups, gate_here, up_here],
        [
            pltpu.VMEM((n * slot, hidden), BF),
            pltpu.VMEM((n * slot, hidden), BF),
            pltpu.VMEM((2 * capacity, TILE), F32),
        ],
        (4 * n * slot * width * hidden, 4 * hidden * width),
    )
    own = dict(zip(order[:-1], own))

    def add(a, b):
        return (a.astype(F32) + b.astype(F32)).astype(BF)

    def exchange(keep, send, bit):
        other = lax.ppermute(send, "expert", [(e, e ^ bit) for e in range(n)])
        count = keep.shape[0]
        parts = 2 if count > 1 else 1
        shape = (count // parts,) + keep.shape[1:]
        return call(halve_kernel, "halve", [(shape, keep.dtype)] * parts, [keep, other])

    low_keep, right_top, left_rest = lax.optimization_barrier((low_keep, right_top, left_rest))
    right_top, left_rest = right(right_top), left(left_rest)
    bits = [1 << i for i in range(n.bit_length() - 1)]
    pair = [low_keep, low_send]
    pair = exchange(*pair, bits[0])
    right_top, left_rest, pair = lax.optimization_barrier((right_top, left_rest, pair))
    going_right, going_left = call(
        merge_kernel,
        "first_add",
        [((2 * capacity, half), BF)] * 2,
        [right_top, left_rest, own[middle - 1], own[1 - middle]],
    )

    share = width // n
    part = rank // 2
    swap = [(0, 1), (1, 0)]

    def adapter_gradient(low_total):
        if share % 128 == 0:
            low, keep, send = call(
                functools.partial(adapter_kernel, capacity),
                "adapter_gradient",
                [((slot, rank), BF)] + [((n, part, share), BF)] * 2,
                [choice, tokens, low_total],
                work=(2 * own_count * rank * width, 2 * own_count * width),
            )
        else:
            me, core = lax.axis_index("expert"), lax.axis_index("dp")
            upper, _ = pick_rows(choice, capacity)
            low = low_total[0].astype(BF)
            low_tokens = dot(upper[:slot], low, TN).astype(BF)
            down = dot(low_tokens, tokens, TN).astype(BF).reshape(rank, n, share)
            down = down.transpose(1, 0, 2)[jnp.arange(n, dtype=jnp.int32) ^ me]
            keep = jnp.where(core == 0, down[:, :part], down[:, part:])
            send = jnp.where(core == 0, down[:, part:], down[:, :part])
        other = lax.ppermute(send, "dp", swap)
        return low, call(halve_kernel, "halve", [((n // 2, part, share), BF)] * 2, [keep, other])

    def lora_gradients():
        (local,) = call(
            functools.partial(lora_kernel, slot, sizes),
            "lora_rows",
            [((2 * rank, hidden), BF)],
            [*dgates, *dups, *low_rows],
            [
                pltpu.VMEM((n * slot, hidden), BF),
                pltpu.VMEM((n * slot, hidden), BF),
                pltpu.VMEM((n * slot, rank), BF),
            ],
            (4 * n * slot * rank * hidden, 4 * n * slot * hidden),
        )
        return local, lax.ppermute(local, "dp", swap)

    for hop, s in enumerate(range(middle - 1, 0, -1)):
        going_right, going_left = right(going_right), left(going_left)
        if hop == 0:
            for bit in bits[1:]:
                pair = exchange(*pair, bit)
            low, pair = adapter_gradient(pair[0])
        elif hop == 1:
            pair = exchange(*pair, bits[0])
            low_rows, pair = lax.optimization_barrier((low_rows, pair))
        if s > 1:
            going_right, going_left, pair = lax.optimization_barrier((going_right, going_left, pair))
            going_right, going_left = add(going_right, own[s - 1]), add(going_left, own[1 - s])
    lora, lora_there = lora_gradients()
    for bit in bits[1:]:
        pair = exchange(*pair, bit)
    down = pair[0][0]
    there = lax.ppermute(down, "dp", swap)
    grad_down, grad_gate, grad_up = call(
        join_kernel,
        "join",
        [((rank, hidden), F32)] * 3,
        [down, there, lora, lora_there],
    )

    (input_gradient,) = call(
        functools.partial(finish_kernel, capacity),
        "finish",
        [((own_count, width), BF)],
        [choice, going_right, going_left, own[0], low, adapter_down_factor],
        [pltpu.VMEM((2 * capacity, rank), F32)],
        (4e8, 4.5e6),
    )
    return (input_gradient[None], grad_down, grad_gate, grad_up)


def solution(mesh):
    placed = (
        P(("groups", "dp"), "expert", None),
        P(("groups", "dp"), "expert", None),
        P(("groups", "dp"), "expert", None),
        P(("groups", "dp"), "expert", None),
        P(("groups", "dp"), None, "expert"),
        P(("groups", "dp"), None, "expert"),
        P(None, "expert"),
        P(None, "expert"),
        P("expert", None),
        P("groups", None),
        P("groups", "expert"),
        P("groups", "expert"),
    )
    return jax.shard_map(
        functools.partial(on_device, ring_order(mesh)),
        mesh=mesh,
        in_specs=placed,
        out_specs=(
            P(("groups", "dp"), "expert", None),
            P("groups", "expert"),
            P("groups", "expert"),
            P("groups", "expert"),
        ),
        check_vma=False,
    )
```

```python
import functools

import jax
import jax.numpy as jnp
from jax import lax
from jax.experimental import pallas as pl
from jax.experimental.pallas import tpu as pltpu
from jax.sharding import PartitionSpec as P

SCALE = 0.25
NT = (((1,), (1,)), ((), ()))
TN = (((0,), (0,)), ((), ()))
BF = jnp.bfloat16
F32 = jnp.float32
VMEM_LIMIT = 10 * 1024 * 1024
TILE = 256


def ring_order(mesh):
    count = mesh.shape["expert"]
    plain = list(range(count))
    if count < 4 or count % 2:
        return plain
    snake = list(range(0, count, 2)) + list(range(count - 1, 0, -2))
    spots = [getattr(d, "coords", None) for d in mesh.devices[0, :, 0]]
    if any(s is None for s in spots):
        return snake if count == 8 else plain

    def length(order):
        hops = zip(order, order[1:] + order[:1])
        return sum(sum(abs(a - b) for a, b in zip(spots[i], spots[j])) for i, j in hops)

    return min((plain, snake), key=length)


def dot(a, b, dims=None):
    if dims is None:
        dims = (((1,), (0,)), ((), ()))
    return lax.dot_general(a, b, dims, preferred_element_type=F32)


def pick_rows(choice, capacity):
    tokens = choice.shape[1]
    named = jnp.max((choice == 0).astype(F32), axis=0, keepdims=True)
    before = lax.broadcasted_iota(jnp.int32, (tokens, tokens), 0)
    after = lax.broadcasted_iota(jnp.int32, (tokens, tokens), 1)
    upto = (before <= after).astype(BF)
    count = dot(jnp.broadcast_to(named, (8, tokens)).astype(BF), upto)[:1]
    slot = jnp.where(named > 0, count - 1.0, -1000.0).astype(jnp.int32)
    row = lax.broadcasted_iota(jnp.int32, (2 * capacity, tokens), 0)
    return (row == slot).astype(BF), (row - capacity == slot).astype(BF)


def prepare_kernel(capacity, choice_hbm, weight_hbm, grad_hbm, tokens_hbm, down_hbm, top, rest,
                   choice_ref, weight_ref, grad_ref, tokens_ref, down_ref, sems):
    half = grad_ref.shape[1] // 2
    rank = down_ref.shape[0]
    pairs = [
        (choice_hbm, choice_ref),
        (grad_hbm.at[:, :half], grad_ref.at[:, :half]),
        (grad_hbm.at[:, half:], grad_ref.at[:, half:]),
        (weight_hbm, weight_ref),
        (down_hbm, down_ref),
        (tokens_hbm, tokens_ref),
    ]
    copies = [pltpu.make_async_copy(a, b, sems.at[i]) for i, (a, b) in enumerate(pairs)]
    for copy in copies:
        copy.start()
    copies[0].wait()
    choice = choice_ref[...]
    upper, lower = pick_rows(choice, capacity)
    copies[1].wait()
    first = dot(upper, grad_ref[:, :half])
    copies[2].wait()
    rows = (first + dot(lower, grad_ref[:, half:])).astype(BF)
    cut = top.shape[0]
    top[:, :half] = rows[:cut]
    rest[:, :half] = rows[cut:]
    copies[3].wait()
    weight = jnp.sum(
        jnp.where(choice == 0, weight_ref[...].astype(F32), 0.0), axis=0, keepdims=True
    )
    column = jnp.sum(upper.astype(F32) * weight, axis=1, keepdims=True)
    column = jnp.broadcast_to(column, (2 * capacity, rank)).astype(BF)
    top[:, half + rank :] = column[:cut]
    rest[:, half + rank :] = column[cut:]
    copies[4].wait()
    copies[5].wait()
    low = dot(tokens_ref[...], down_ref[...], NT).astype(BF)
    low = dot(upper, low).astype(BF)
    top[:, half : half + rank] = low[:cut]
    rest[:, half : half + rank] = low[cut:]


def place_here(place):
    me = lax.axis_index("expert")
    return me, sum(jnp.where(me == e, p, 0) for e, p in enumerate(place))


def reorder_kernel(place, capacity, gate_in, up_in, *refs):
    gate_out, up_out, tall = refs[-3:]
    count, slot, hidden = gate_out.shape
    _, here = place_here(place)
    live = lax.broadcasted_iota(jnp.int32, (slot, hidden), 0) < capacity
    for source, target in ((gate_in, gate_out), (up_in, up_out)):
        tall[: count * capacity, :] = source[...].astype(F32)
        tall[count * capacity :, :] = jnp.zeros((slot, hidden), F32)
        for e in range(count):
            away = lax.rem(place[e] - here + count, count)
            at = jnp.where(2 * away < count, 2 * away, 2 * (count - away) - 1)
            rows = tall[e * capacity : e * capacity + slot, :]
            target[at] = jnp.where(live, rows, 0.0).astype(BF)


def low_order_kernel(ring, place, order, *refs):
    lows, (keep, send) = refs[:-2], refs[-2:]
    count = len(ring)
    me, here = place_here(place)
    for low, r in zip(lows, order):
        spot = lax.rem(here + r + count, count)
        owner = sum(jnp.where(spot == i, e, 0) for i, e in enumerate(ring))
        key = owner ^ me

        @pl.when(key % 2 == 0)
        def _(low=low, key=key):
            keep[key // 2] = low[...]

        @pl.when(key % 2 == 1)
        def _(low=low, key=key):
            send[key // 2] = low[...]


def halve_kernel(ours, theirs, *outs):
    count = ours.shape[0]
    for i in range(count):
        total = ours[i].astype(F32) + theirs[i].astype(F32)
        out = outs[i % len(outs)]
        out[i // len(outs)] = total.astype(out.dtype)


def hidden_kernel(capacity, slot, start, count, pieces, *refs):
    blocks, refs = [refs[i * pieces : (i + 1) * pieces] for i in range(count)], refs[count * pieces :]
    (gate_ref, up_ref, down_ref, lora_gate, lora_up, dgate_ref, dup_ref, low_ref), refs = refs[:8], refs[8:]
    lows, rows = refs[:count], refs[count]
    hidden, width = down_ref.shape
    half = width // 2
    rank = lora_gate.shape[0]
    tall = rows.shape[0] // count
    for i, block in enumerate(blocks):
        at = i * tall
        for piece in block:
            rows[at : at + piece.shape[0], :] = piece[:, :half]
            at += piece.shape[0]
    if tall % 128 == 0:
        first = dot(down_ref[:, :half], rows[...], NT).T
        second = dot(down_ref[:, half:], rows[...], NT).T
    else:
        first = dot(rows[...], down_ref[:, :half], NT)
        second = dot(rows[...], down_ref[:, half:], NT)
    live = lax.broadcasted_iota(jnp.int32, (slot, hidden), 0) < capacity
    for i in range(count):
        at = i * tall
        extras, seen = [], 0
        for piece in blocks[i]:
            height = min(piece.shape[0], slot - seen)
            extras.append(piece[:height, half:])
            low_ref[i, seen : seen + height, :] = extras[-1][:, :rank]
            seen += height
        weight = jnp.concatenate([x.astype(F32)[:, rank : rank + 1] for x in extras], axis=0)
        grad = (first[at : at + slot] + second[at + capacity : at + capacity + slot]) * weight
        grad = jnp.where(live, grad, 0.0)
        gate = gate_ref[start + i].astype(F32)
        up = up_ref[start + i].astype(F32)
        sig = 1.0 / (1.0 + jnp.exp(-gate))
        slope = sig * (1.0 + gate * (1.0 - sig))
        dgate = (grad * up * slope).astype(BF)
        dup = (grad * gate * sig).astype(BF)
        dgate_ref[i] = dgate
        dup_ref[i] = dup
        lows[i][...] = SCALE * (dot(dgate, lora_gate[...], NT) + dot(dup, lora_up[...], NT))


def stack(groups, slot, sources, target):
    at = 0
    for size, source in zip(groups, sources):
        for i in range(size):
            target[at : at + slot, :] = source[i]
            at += slot


def lora_kernel(slot, groups, *refs):
    pieces = len(groups)
    dgates, dups, lows = refs[:pieces], refs[pieces : 2 * pieces], refs[2 * pieces : 3 * pieces]
    lora_out, dgate, dup, low = refs[3 * pieces :]
    rank = lora_out.shape[0] // 2
    stack(groups, slot, dgates, dgate)
    stack(groups, slot, dups, dup)
    stack(groups, slot, lows, low)
    lora_out[:rank, :] = (SCALE * dot(low[...], dgate[...], TN)).astype(BF)
    lora_out[rank:, :] = (SCALE * dot(low[...], dup[...], TN)).astype(BF)


def partial_kernel(capacity, slot, groups, cut, *refs):
    members, pieces = sum(groups), len(groups)
    dgates, dups, refs = refs[:pieces], refs[pieces : 2 * pieces], refs[2 * pieces :]
    gate_ref, up_ref, outs, (dgate, dup, tile) = refs[0], refs[1], refs[2:-3], refs[-3:]
    half = gate_ref.shape[0] // 2
    stack(groups, slot, dgates, dgate)
    stack(groups, slot, dups, dup)

    for t in range(0, half, TILE):
        sums = []
        for at in (t, t + half):
            sums.append(
                dot(dgate[...], gate_ref[at : at + TILE, :], NT)
                + dot(dup[...], up_ref[at : at + TILE, :], NT)
            )
        for i in range(members):
            at = i * slot
            tile[:capacity, :] = sums[0][at : at + capacity]
            tile[capacity:, :] = sums[1][at : at + capacity]
            outs[2 * i][:, t : t + TILE] = tile[:cut, :].astype(BF)
            outs[2 * i + 1][:, t : t + TILE] = tile[cut:, :].astype(BF)


def adapter_kernel(capacity, choice_ref, tokens_ref, low_in, low_ref, keep_ref, send_ref):
    count, part, share = keep_ref.shape
    low = low_in[0].astype(BF)
    low_ref[...] = low
    upper, _ = pick_rows(choice_ref[...], capacity)
    low = dot(upper[: low.shape[0]], low, TN).astype(BF)
    me, core = lax.axis_index("expert"), lax.axis_index("dp")
    for i in range(count):
        columns = pl.ds(pl.multiple_of((me ^ i) * share, 128), share)
        down = dot(low, tokens_ref[:, columns], TN)
        keep_ref[i] = jnp.where(core == 0, down[:part], down[part:]).astype(BF)
        send_ref[i] = jnp.where(core == 0, down[part:], down[:part]).astype(BF)


def join_kernel(down_ref, there_ref, lora_ref, lora_there, down_out, gate_out, up_out):
    part = down_ref.shape[0]
    core = lax.axis_index("dp")
    down, there = down_ref[...].astype(F32), there_ref[...].astype(F32)
    down_out[:part, :] = jnp.where(core == 0, down, there)
    down_out[part:, :] = jnp.where(core == 0, there, down)
    rank = gate_out.shape[0]
    gate_out[...] = lora_ref[:rank, :].astype(F32) + lora_there[:rank, :].astype(F32)
    up_out[...] = lora_ref[rank:, :].astype(F32) + lora_there[rank:, :].astype(F32)


def finish_kernel(capacity, choice_ref, *refs):
    tops, rests, (low_ref, down_ref, out_ref, low_tall) = refs[:3], refs[3:6], refs[6:]
    cut, half = tops[0].shape
    upper, lower = pick_rows(choice_ref[...], capacity)
    low = low_ref[...].astype(F32)[:capacity]
    zero = jnp.zeros_like(low)
    low_tall[:capacity, :] = low
    low_tall[capacity:, :] = zero
    low_upper = low_tall[...].astype(BF)
    low_tall[:capacity, :] = zero
    low_tall[capacity:, :] = low
    low_lower = low_tall[...].astype(BF)
    adapter = dot(low_upper, down_ref[:, :half]) + dot(low_lower, down_ref[:, half:])
    top = sum(x[...].astype(F32) for x in tops) + adapter[:cut]
    rest = sum(x[...].astype(F32) for x in rests) + adapter[cut:]
    top, rest = top.astype(BF), rest.astype(BF)
    for pick, at in ((upper, 0), (lower, half)):
        picked = dot(pick[:cut], top, TN) + dot(pick[cut:], rest, TN)
        out_ref[:, at : at + half] = picked.astype(BF)


def in_hbm(x):
    return pltpu.with_memory_space_constraint(x, pltpu.HBM)


def in_vmem(x):
    return pltpu.with_memory_space_constraint(x, pltpu.VMEM)


def on_device(
    ring,
    tokens,
    output_gradient,
    token_expert_choice,
    routing_weight_table,
    stored_gate_rows,
    stored_up_rows,
    gate_weight,
    up_weight,
    down_weight,
    adapter_down_factor,
    adapter_gate_factor,
    adapter_up_factor,
):
    n = len(ring)
    tokens, output_gradient = tokens[0], output_gradient[0]
    own_count, width = tokens.shape
    half = width // 2
    capacity = stored_gate_rows.shape[1] // n
    hidden = stored_gate_rows.shape[2]
    rank = adapter_down_factor.shape[0]
    tall = -(-2 * capacity // 128) * 128
    slot = -(-capacity // 8) * 8
    cut = capacity // 16 * 16
    wide = half + 2 * rank
    middle = n // 2
    choice = token_expert_choice[0].T
    weights = routing_weight_table[0].T

    place = [0] * n
    for i, e in enumerate(ring):
        place[e] = i
    to_right = [(ring[i], ring[(i + 1) % n]) for i in range(n)]
    to_left = [(ring[i], ring[(i - 1) % n]) for i in range(n)]
    passes = [[0, -1, 1]] + [[-s, s] for s in range(2, middle)] + [[middle]]
    sizes = [len(group) for group in passes]
    order = [r for group in passes for r in group]
    heights = [cut, 2 * capacity - cut]

    def call(kernel, name, shapes, args, scratch=(), work=(0, 0), **more):
        return pl.pallas_call(
            kernel,
            out_shape=[jax.ShapeDtypeStruct(shape, dtype) for shape, dtype in shapes],
            scratch_shapes=list(scratch),
            compiler_params=pltpu.CompilerParams(vmem_limit_bytes=VMEM_LIMIT),
            cost_estimate=pl.CostEstimate(flops=1, bytes_accessed=1, transcendentals=0),
            name=name,
            **more,
        )(*args)

    def right(x):
        return lax.ppermute(x, "expert", to_right)

    def left(x):
        return lax.ppermute(x, "expert", to_left)

    block = call(
        functools.partial(prepare_kernel, capacity),
        "prepare",
        [((h, wide), BF) for h in heights],
        [in_hbm(x) for x in (choice, weights, output_gradient, tokens, adapter_down_factor)],
        [
            pltpu.VMEM(choice.shape, choice.dtype),
            pltpu.VMEM(weights.shape, BF),
            pltpu.VMEM(output_gradient.shape, BF),
            pltpu.VMEM(tokens.shape, BF),
            pltpu.VMEM(adapter_down_factor.shape, BF),
            pltpu.SemaphoreType.DMA((6,)),
        ],
        (4e8, 4.5e6),
        in_specs=[pl.BlockSpec(memory_space=pl.ANY)] * 5,
    )
    down_here, gate_here, up_here = in_vmem(down_weight), in_vmem(gate_weight), in_vmem(up_weight)
    gate_factor, up_factor = in_vmem(adapter_gate_factor), in_vmem(adapter_up_factor)
    gate_rows, up_rows = call(
        functools.partial(reorder_kernel, place, capacity),
        "reorder",
        [((n, slot, hidden), BF)] * 2,
        [stored_gate_rows[0], stored_up_rows[0], down_here, gate_factor, up_factor],
        [pltpu.VMEM((n * capacity + slot, hidden), F32)],
        (0, 8 * n * slot * hidden),
    )

    dgates, dups, low_rows, lows = [], [], [], []
    got = {0: tuple(block)}

    def hidden_pass(group):
        size, start, pieces = len(group), len(lows), len(got[group[0]])
        tall = -(-2 * capacity // 128) * 128 if size < 3 else -(-2 * capacity // 16) * 16
        results = call(
            functools.partial(hidden_kernel, capacity, slot, start, size, pieces),
            "hidden_rows",
            [((size, slot, hidden), BF)] * 2
            + [((size, slot, rank), BF)]
            + [((slot, rank), F32)] * size,
            [piece for r in group for piece in got[r]]
            + [gate_rows, up_rows, down_here, gate_factor, up_factor],
            [pltpu.VMEM((size * tall, half), BF)],
            (2 * size * tall * width * hidden, 2 * hidden * width),
        )
        dgates.append(results[0])
        dups.append(results[1])
        low_rows.append(results[2])
        lows.extend(results[3:])

    right_top, right_rest = left_top, left_rest = block
    for s in range(1, middle):
        right_top, left_rest = right(right_top), left(left_rest)
        if s == 1:
            right_top, left_rest, gate_rows, up_rows = lax.optimization_barrier(
                (right_top, left_rest, gate_rows, up_rows)
            )
        right_rest, left_top = right(right_rest), left(left_top)
        if s > 1:
            hidden_pass(passes[s - 2])
            right_rest, left_top, dgates[-1], dups[-1] = lax.optimization_barrier(
                (right_rest, left_top, dgates[-1], dups[-1])
            )
        got[-s], got[s] = (right_top, right_rest), (left_top, left_rest)
    right_top, left_rest = right(right_top), left(left_rest)
    hidden_pass(passes[-2])
    right_top, left_rest, dgates[-1], dups[-1] = lax.optimization_barrier(
        (right_top, left_rest, dgates[-1], dups[-1])
    )
    got[middle] = (right_top, left_rest)
    hidden_pass(passes[-1])

    low_keep, low_send = call(
        functools.partial(low_order_kernel, ring, place, order),
        "low_order",
        [((n // 2, slot, rank), F32)] * 2,
        lows,
    )
    own = call(
        functools.partial(partial_kernel, capacity, slot, sizes, cut),
        "partials",
        [((h, half), BF) for h in heights] * n,
        [*dgates, *dups, gate_here, up_here],
        [
            pltpu.VMEM((n * slot, hidden), BF),
            pltpu.VMEM((n * slot, hidden), BF),
            pltpu.VMEM((2 * capacity, TILE), F32),
        ],
        (4 * n * slot * width * hidden, 4 * hidden * width),
    )
    def add(a, b):
        return (a.astype(F32) + b.astype(F32)).astype(BF)

    def exchange(keep, send, bit):
        other = lax.ppermute(send, "expert", [(e, e ^ bit) for e in range(n)])
        count = keep.shape[0]
        parts = 2 if count > 1 else 1
        shape = (count // parts,) + keep.shape[1:]
        return call(halve_kernel, "halve", [(shape, keep.dtype)] * parts, [keep, other])

    bits = [1 << i for i in range(n.bit_length() - 1)]
    pair = exchange(low_keep, low_send, bits[0])
    pair, own = lax.optimization_barrier((pair, own))
    own = {r: (own[2 * i], own[2 * i + 1]) for i, r in enumerate(order)}
    right_top, left_rest = right(own[middle][0]), left(own[middle][1])
    right_rest, left_top = right(own[middle - 1][1]), left(own[1 - middle][0])
    pair = exchange(*pair, bits[1])
    right_top, left_rest, pair = lax.optimization_barrier((right_top, left_rest, pair))

    share = width // n
    part = rank // 2
    swap = [(0, 1), (1, 0)]

    def adapter_gradient(low_total):
        if share % 128 == 0:
            low, keep, send = call(
                functools.partial(adapter_kernel, capacity),
                "adapter_gradient",
                [((slot, rank), BF)] + [((n, part, share), BF)] * 2,
                [choice, tokens, low_total],
                work=(2 * own_count * rank * width, 2 * own_count * width),
            )
        else:
            me, core = lax.axis_index("expert"), lax.axis_index("dp")
            upper, _ = pick_rows(choice, capacity)
            low = low_total[0].astype(BF)
            low_tokens = dot(upper[:slot], low, TN).astype(BF)
            down = dot(low_tokens, tokens, TN).astype(BF).reshape(rank, n, share)
            down = down.transpose(1, 0, 2)[jnp.arange(n, dtype=jnp.int32) ^ me]
            keep = jnp.where(core == 0, down[:, :part], down[:, part:])
            send = jnp.where(core == 0, down[:, part:], down[:, :part])
        other = lax.ppermute(send, "dp", swap)
        return low, call(halve_kernel, "halve", [((n // 2, part, share), BF)] * 2, [keep, other])

    def lora_gradients():
        (local,) = call(
            functools.partial(lora_kernel, slot, sizes),
            "lora_rows",
            [((2 * rank, hidden), BF)],
            [*dgates, *dups, *low_rows],
            [
                pltpu.VMEM((n * slot, hidden), BF),
                pltpu.VMEM((n * slot, hidden), BF),
                pltpu.VMEM((n * slot, rank), BF),
            ],
            (4 * n * slot * rank * hidden, 4 * n * slot * hidden),
        )
        return local, lax.ppermute(local, "dp", swap)

    for hop, s in enumerate(range(middle - 1, 0, -1)):
        right_top, left_rest = add(right_top, own[s][0]), add(left_rest, own[-s][1])
        right_top, left_rest = right(right_top), left(left_rest)
        if hop == 0:
            for bit in bits[2:]:
                pair = exchange(*pair, bit)
        if hop == 2:
            pair = exchange(*pair, bits[1])
        if s > 1:
            right_rest, left_top, pair = lax.optimization_barrier((right_rest, left_top, pair))
            right_rest, left_top = add(right_rest, own[s - 1][1]), add(left_top, own[1 - s][0])
            right_rest, left_top = right(right_rest), left(left_top)
            if hop == 0:
                low, pair = adapter_gradient(pair[0])
            if hop == 1:
                pair = exchange(*pair, bits[0])
                low_rows, pair = lax.optimization_barrier((low_rows, pair))
            right_top, left_rest, pair = lax.optimization_barrier((right_top, left_rest, pair))
    lora, lora_there = lora_gradients()
    for bit in bits[2 if middle > 3 else 1 :]:
        pair = exchange(*pair, bit)
    down = pair[0][0]
    there = lax.ppermute(down, "dp", swap)
    grad_down, grad_gate, grad_up = call(
        join_kernel,
        "join",
        [((rank, hidden), F32)] * 3,
        [down, there, lora, lora_there],
    )

    (input_gradient,) = call(
        functools.partial(finish_kernel, capacity),
        "finish",
        [((own_count, width), BF)],
        [choice, right_top, left_top, own[0][0], right_rest, left_rest, own[0][1], low, adapter_down_factor],
        [pltpu.VMEM((2 * capacity, rank), F32)],
        (4e8, 4.5e6),
    )
    return (input_gradient[None], grad_down, grad_gate, grad_up)


def solution(mesh):
    placed = (
        P(("groups", "dp"), "expert", None),
        P(("groups", "dp"), "expert", None),
        P(("groups", "dp"), "expert", None),
        P(("groups", "dp"), "expert", None),
        P(("groups", "dp"), None, "expert"),
        P(("groups", "dp"), None, "expert"),
        P(None, "expert"),
        P(None, "expert"),
        P("expert", None),
        P("groups", None),
        P("groups", "expert"),
        P("groups", "expert"),
    )
    return jax.shard_map(
        functools.partial(on_device, ring_order(mesh)),
        mesh=mesh,
        in_specs=placed,
        out_specs=(
            P(("groups", "dp"), "expert", None),
            P("groups", "expert"),
            P("groups", "expert"),
            P("groups", "expert"),
        ),
        check_vma=False,
    )
```

```python
import functools

import jax
import jax.numpy as jnp
from jax import lax
from jax.experimental import pallas as pl
from jax.experimental.pallas import tpu as pltpu
from jax.sharding import PartitionSpec as P

SCALE = 0.25
NT = (((1,), (1,)), ((), ()))
TN = (((0,), (0,)), ((), ()))
BF = jnp.bfloat16
F32 = jnp.float32
VMEM_LIMIT = 10 * 1024 * 1024
TILE = 256


def ring_order(mesh):
    count = mesh.shape["expert"]
    plain = list(range(count))
    if count < 4 or count % 2:
        return plain
    snake = list(range(0, count, 2)) + list(range(count - 1, 0, -2))
    spots = [getattr(d, "coords", None) for d in mesh.devices[0, :, 0]]
    if any(s is None for s in spots):
        return snake if count == 8 else plain

    def length(order):
        hops = zip(order, order[1:] + order[:1])
        return sum(sum(abs(a - b) for a, b in zip(spots[i], spots[j])) for i, j in hops)

    return min((plain, snake), key=length)


def dot(a, b, dims=None):
    if dims is None:
        dims = (((1,), (0,)), ((), ()))
    return lax.dot_general(a, b, dims, preferred_element_type=F32)


def pick_rows(choice, capacity):
    tokens = choice.shape[1]
    named = jnp.max((choice == 0).astype(F32), axis=0, keepdims=True)
    before = lax.broadcasted_iota(jnp.int32, (tokens, tokens), 0)
    after = lax.broadcasted_iota(jnp.int32, (tokens, tokens), 1)
    upto = (before <= after).astype(BF)
    count = dot(jnp.broadcast_to(named, (8, tokens)).astype(BF), upto)[:1]
    slot = jnp.where(named > 0, count - 1.0, -1000.0).astype(jnp.int32)
    row = lax.broadcasted_iota(jnp.int32, (2 * capacity, tokens), 0)
    return (row == slot).astype(BF), (row - capacity == slot).astype(BF)


def prepare_kernel(capacity, choice_hbm, weight_hbm, grad_hbm, tokens_hbm, down_hbm, block_ref,
                   choice_ref, weight_ref, grad_ref, tokens_ref, down_ref, sems):
    half = grad_ref.shape[1] // 2
    rank = down_ref.shape[0]
    pairs = [
        (choice_hbm, choice_ref),
        (grad_hbm.at[:, :half], grad_ref.at[:, :half]),
        (grad_hbm.at[:, half:], grad_ref.at[:, half:]),
        (weight_hbm, weight_ref),
        (down_hbm, down_ref),
        (tokens_hbm, tokens_ref),
    ]
    copies = [pltpu.make_async_copy(a, b, sems.at[i]) for i, (a, b) in enumerate(pairs)]
    for copy in copies:
        copy.start()
    copies[0].wait()
    choice = choice_ref[...]
    upper, lower = pick_rows(choice, capacity)
    copies[1].wait()
    first = dot(upper, grad_ref[:, :half])
    copies[2].wait()
    block_ref[:, :half] = (first + dot(lower, grad_ref[:, half:])).astype(BF)
    copies[3].wait()
    weight = jnp.sum(
        jnp.where(choice == 0, weight_ref[...].astype(F32), 0.0), axis=0, keepdims=True
    )
    column = jnp.sum(upper.astype(F32) * weight, axis=1, keepdims=True)
    block_ref[:, half + rank :] = jnp.broadcast_to(column, (2 * capacity, rank)).astype(BF)
    copies[4].wait()
    copies[5].wait()
    low = dot(tokens_ref[...], down_ref[...], NT).astype(BF)
    block_ref[:, half : half + rank] = dot(upper, low).astype(BF)


def cut_kernel(right_in, left_in, top, rest):
    cut = top.shape[0]
    top[...] = right_in[:cut, :]
    rest[...] = left_in[cut:, :]


def place_here(place):
    me = lax.axis_index("expert")
    return me, sum(jnp.where(me == e, p, 0) for e, p in enumerate(place))


def reorder_kernel(place, capacity, gate_in, up_in, gate_out, up_out, tall):
    count, slot, hidden = gate_out.shape
    _, here = place_here(place)
    live = lax.broadcasted_iota(jnp.int32, (slot, hidden), 0) < capacity
    for source, target in ((gate_in, gate_out), (up_in, up_out)):
        tall[: count * capacity, :] = source[...].astype(F32)
        tall[count * capacity :, :] = jnp.zeros((slot, hidden), F32)
        for e in range(count):
            away = lax.rem(place[e] - here + count, count)
            at = jnp.where(2 * away < count, 2 * away, 2 * (count - away) - 1)
            rows = tall[e * capacity : e * capacity + slot, :]
            target[at] = jnp.where(live, rows, 0.0).astype(BF)


def low_order_kernel(ring, place, order, *refs):
    lows, (keep, send) = refs[:-2], refs[-2:]
    count = len(ring)
    me, here = place_here(place)
    for low, r in zip(lows, order):
        spot = lax.rem(here + r + count, count)
        owner = sum(jnp.where(spot == i, e, 0) for i, e in enumerate(ring))
        key = owner ^ me

        @pl.when(key % 2 == 0)
        def _(low=low, key=key):
            keep[key // 2] = low[...]

        @pl.when(key % 2 == 1)
        def _(low=low, key=key):
            send[key // 2] = low[...]


def halve_kernel(ours, theirs, *outs):
    count = ours.shape[0]
    for i in range(count):
        total = ours[i].astype(F32) + theirs[i].astype(F32)
        out = outs[i % len(outs)]
        out[i // len(outs)] = total.astype(out.dtype)


def hidden_kernel(capacity, slot, start, count, pieces, *refs):
    blocks, refs = [refs[i * pieces : (i + 1) * pieces] for i in range(count)], refs[count * pieces :]
    (gate_ref, up_ref, down_ref, lora_gate, lora_up, dgate_ref, dup_ref, low_ref), refs = refs[:8], refs[8:]
    lows, rows = refs[:count], refs[count]
    hidden, width = down_ref.shape
    half = width // 2
    rank = lora_gate.shape[0]
    tall = rows.shape[0] // count
    for i, block in enumerate(blocks):
        at = i * tall
        for piece in block:
            rows[at : at + piece.shape[0], :] = piece[:, :half]
            at += piece.shape[0]
    if tall % 128 == 0:
        first = dot(down_ref[:, :half], rows[...], NT).T
        second = dot(down_ref[:, half:], rows[...], NT).T
    else:
        first = dot(rows[...], down_ref[:, :half], NT)
        second = dot(rows[...], down_ref[:, half:], NT)
    live = lax.broadcasted_iota(jnp.int32, (slot, hidden), 0) < capacity
    for i in range(count):
        at = i * tall
        extras, seen = [], 0
        for piece in blocks[i]:
            height = min(piece.shape[0], slot - seen)
            extras.append(piece[:height, half:])
            low_ref[i, seen : seen + height, :] = extras[-1][:, :rank]
            seen += height
        weight = jnp.concatenate([x.astype(F32)[:, rank : rank + 1] for x in extras], axis=0)
        grad = (first[at : at + slot] + second[at + capacity : at + capacity + slot]) * weight
        grad = jnp.where(live, grad, 0.0)
        gate = gate_ref[start + i].astype(F32)
        up = up_ref[start + i].astype(F32)
        sig = 1.0 / (1.0 + jnp.exp(-gate))
        slope = sig * (1.0 + gate * (1.0 - sig))
        dgate = (grad * up * slope).astype(BF)
        dup = (grad * gate * sig).astype(BF)
        dgate_ref[i] = dgate
        dup_ref[i] = dup
        lows[i][...] = SCALE * (dot(dgate, lora_gate[...], NT) + dot(dup, lora_up[...], NT))


def stack(groups, slot, sources, target):
    at = 0
    for size, source in zip(groups, sources):
        for i in range(size):
            target[at : at + slot, :] = source[i]
            at += slot


def lora_kernel(slot, groups, *refs):
    pieces = len(groups)
    dgates, dups, lows = refs[:pieces], refs[pieces : 2 * pieces], refs[2 * pieces : 3 * pieces]
    lora_out, dgate, dup, low = refs[3 * pieces :]
    rank = lora_out.shape[0] // 2
    stack(groups, slot, dgates, dgate)
    stack(groups, slot, dups, dup)
    stack(groups, slot, lows, low)
    lora_out[:rank, :] = (SCALE * dot(low[...], dgate[...], TN)).astype(BF)
    lora_out[rank:, :] = (SCALE * dot(low[...], dup[...], TN)).astype(BF)


def partial_kernel(capacity, slot, groups, cut, *refs):
    members, pieces = sum(groups), len(groups)
    dgates, dups, refs = refs[:pieces], refs[pieces : 2 * pieces], refs[2 * pieces :]
    gate_ref, up_ref, outs, (dgate, dup, tile) = refs[0], refs[1], refs[2:-3], refs[-3:]
    half = gate_ref.shape[0] // 2
    stack(groups, slot, dgates, dgate)
    stack(groups, slot, dups, dup)

    for t in range(0, half, TILE):
        sums = []
        for at in (t, t + half):
            sums.append(
                dot(dgate[...], gate_ref[at : at + TILE, :], NT)
                + dot(dup[...], up_ref[at : at + TILE, :], NT)
            )
        for i in range(members):
            at = i * slot
            tile[:capacity, :] = sums[0][at : at + capacity]
            tile[capacity:, :] = sums[1][at : at + capacity]
            outs[2 * i][:, t : t + TILE] = tile[:cut, :].astype(BF)
            outs[2 * i + 1][:, t : t + TILE] = tile[cut:, :].astype(BF)


def adapter_kernel(capacity, choice_ref, tokens_ref, low_in, low_ref, keep_ref, send_ref):
    count, part, share = keep_ref.shape
    low = low_in[0].astype(BF)
    low_ref[...] = low
    upper, _ = pick_rows(choice_ref[...], capacity)
    low = dot(upper[: low.shape[0]], low, TN).astype(BF)
    me, core = lax.axis_index("expert"), lax.axis_index("dp")
    for i in range(count):
        columns = pl.ds(pl.multiple_of((me ^ i) * share, 128), share)
        down = dot(low, tokens_ref[:, columns], TN)
        keep_ref[i] = jnp.where(core == 0, down[:part], down[part:]).astype(BF)
        send_ref[i] = jnp.where(core == 0, down[part:], down[:part]).astype(BF)


def join_kernel(down_ref, there_ref, lora_ref, lora_there, down_out, gate_out, up_out):
    part = down_ref.shape[0]
    core = lax.axis_index("dp")
    down, there = down_ref[...].astype(F32), there_ref[...].astype(F32)
    down_out[:part, :] = jnp.where(core == 0, down, there)
    down_out[part:, :] = jnp.where(core == 0, there, down)
    rank = gate_out.shape[0]
    gate_out[...] = lora_ref[:rank, :].astype(F32) + lora_there[:rank, :].astype(F32)
    up_out[...] = lora_ref[rank:, :].astype(F32) + lora_there[rank:, :].astype(F32)


def finish_kernel(capacity, choice_ref, *refs):
    tops, rests, (low_ref, down_ref, out_ref, low_tall) = refs[:3], refs[3:6], refs[6:]
    cut, half = tops[0].shape
    upper, lower = pick_rows(choice_ref[...], capacity)
    low = low_ref[...].astype(F32)[:capacity]
    zero = jnp.zeros_like(low)
    low_tall[:capacity, :] = low
    low_tall[capacity:, :] = zero
    low_upper = low_tall[...].astype(BF)
    low_tall[:capacity, :] = zero
    low_tall[capacity:, :] = low
    low_lower = low_tall[...].astype(BF)
    adapter = dot(low_upper, down_ref[:, :half]) + dot(low_lower, down_ref[:, half:])
    top = sum(x[...].astype(F32) for x in tops) + adapter[:cut]
    rest = sum(x[...].astype(F32) for x in rests) + adapter[cut:]
    top, rest = top.astype(BF), rest.astype(BF)
    for pick, at in ((upper, 0), (lower, half)):
        picked = dot(pick[:cut], top, TN) + dot(pick[cut:], rest, TN)
        out_ref[:, at : at + half] = picked.astype(BF)


def in_hbm(x):
    return pltpu.with_memory_space_constraint(x, pltpu.HBM)


def in_vmem(x):
    return pltpu.with_memory_space_constraint(x, pltpu.VMEM)


def on_device(
    ring,
    tokens,
    output_gradient,
    token_expert_choice,
    routing_weight_table,
    stored_gate_rows,
    stored_up_rows,
    gate_weight,
    up_weight,
    down_weight,
    adapter_down_factor,
    adapter_gate_factor,
    adapter_up_factor,
):
    n = len(ring)
    tokens, output_gradient = tokens[0], output_gradient[0]
    own_count, width = tokens.shape
    half = width // 2
    capacity = stored_gate_rows.shape[1] // n
    hidden = stored_gate_rows.shape[2]
    rank = adapter_down_factor.shape[0]
    tall = -(-2 * capacity // 128) * 128
    slot = -(-capacity // 8) * 8
    cut = capacity // 16 * 16
    wide = half + 2 * rank
    middle = n // 2
    choice = token_expert_choice[0].T
    weights = routing_weight_table[0].T

    place = [0] * n
    for i, e in enumerate(ring):
        place[e] = i
    to_right = [(ring[i], ring[(i + 1) % n]) for i in range(n)]
    to_left = [(ring[i], ring[(i - 1) % n]) for i in range(n)]
    passes = [[0, -1, 1]] + [[-s, s] for s in range(2, middle)] + [[middle]]
    sizes = [len(group) for group in passes]
    order = [r for group in passes for r in group]
    heights = [cut, 2 * capacity - cut]

    def call(kernel, name, shapes, args, scratch=(), work=(0, 0), **more):
        return pl.pallas_call(
            kernel,
            out_shape=[jax.ShapeDtypeStruct(shape, dtype) for shape, dtype in shapes],
            scratch_shapes=list(scratch),
            compiler_params=pltpu.CompilerParams(vmem_limit_bytes=VMEM_LIMIT),
            cost_estimate=pl.CostEstimate(
                flops=int(work[0]), bytes_accessed=int(work[1]), transcendentals=0
            ),
            name=name,
            **more,
        )(*args)

    def right(x):
        return lax.ppermute(x, "expert", to_right)

    def left(x):
        return lax.ppermute(x, "expert", to_left)

    (block,) = call(
        functools.partial(prepare_kernel, capacity),
        "prepare",
        [((2 * capacity, wide), BF)],
        [in_hbm(x) for x in (choice, weights, output_gradient, tokens, adapter_down_factor)],
        [
            pltpu.VMEM(choice.shape, choice.dtype),
            pltpu.VMEM(weights.shape, BF),
            pltpu.VMEM(output_gradient.shape, BF),
            pltpu.VMEM(tokens.shape, BF),
            pltpu.VMEM(adapter_down_factor.shape, BF),
            pltpu.SemaphoreType.DMA((6,)),
        ],
        (4e8, 4.5e6),
        in_specs=[pl.BlockSpec(memory_space=pl.ANY)] * 5,
    )
    gate_rows, up_rows = call(
        functools.partial(reorder_kernel, place, capacity),
        "reorder",
        [((n, slot, hidden), BF)] * 2,
        [stored_gate_rows[0], stored_up_rows[0]],
        [pltpu.VMEM((n * capacity + slot, hidden), F32)],
        (0, 8 * n * slot * hidden),
    )

    down_here, gate_here, up_here = in_vmem(down_weight), in_vmem(gate_weight), in_vmem(up_weight)
    dgates, dups, low_rows, lows = [], [], [], []
    got = {0: (block,)}

    def hidden_pass(group):
        size, start, pieces = len(group), len(lows), len(got[group[0]])
        tall = -(-2 * capacity // 128) * 128 if size < 3 else -(-2 * capacity // 16) * 16
        results = call(
            functools.partial(hidden_kernel, capacity, slot, start, size, pieces),
            "hidden_rows",
            [((size, slot, hidden), BF)] * 2
            + [((size, slot, rank), BF)]
            + [((slot, rank), F32)] * size,
            [piece for r in group for piece in got[r]]
            + [gate_rows, up_rows, down_here, adapter_gate_factor, adapter_up_factor],
            [pltpu.VMEM((size * tall, half), BF)],
            (2 * size * tall * width * hidden, 2 * hidden * width),
        )
        dgates.append(results[0])
        dups.append(results[1])
        low_rows.append(results[2])
        lows.extend(results[3:])

    going_right = going_left = block
    for s in range(1, middle):
        going_right, going_left = right(going_right), left(going_left)
        if s == 1:
            going_right, going_left, gate_rows, up_rows = lax.optimization_barrier(
                (going_right, going_left, gate_rows, up_rows)
            )
        else:
            hidden_pass(passes[s - 2])
            going_right, going_left, dgates[-1], dups[-1] = lax.optimization_barrier(
                (going_right, going_left, dgates[-1], dups[-1])
            )
        got[-s], got[s] = (going_right,), (going_left,)
    right_top, left_rest = call(
        cut_kernel, "cut", [((h, wide), BF) for h in heights], [going_right, going_left]
    )
    right_top, left_rest = right(right_top), left(left_rest)
    hidden_pass(passes[-2])
    right_top, left_rest, dgates[-1], dups[-1] = lax.optimization_barrier(
        (right_top, left_rest, dgates[-1], dups[-1])
    )
    got[middle] = (right_top, left_rest)
    hidden_pass(passes[-1])

    low_keep, low_send = call(
        functools.partial(low_order_kernel, ring, place, order),
        "low_order",
        [((n // 2, slot, rank), F32)] * 2,
        lows,
    )
    own = call(
        functools.partial(partial_kernel, capacity, slot, sizes, cut),
        "partials",
        [((h, half), BF) for h in heights] * n,
        [*dgates, *dups, gate_here, up_here],
        [
            pltpu.VMEM((n * slot, hidden), BF),
            pltpu.VMEM((n * slot, hidden), BF),
            pltpu.VMEM((2 * capacity, TILE), F32),
        ],
        (4 * n * slot * width * hidden, 4 * hidden * width),
    )
    def add(a, b):
        return (a.astype(F32) + b.astype(F32)).astype(BF)

    def exchange(keep, send, bit):
        other = lax.ppermute(send, "expert", [(e, e ^ bit) for e in range(n)])
        count = keep.shape[0]
        parts = 2 if count > 1 else 1
        shape = (count // parts,) + keep.shape[1:]
        return call(halve_kernel, "halve", [(shape, keep.dtype)] * parts, [keep, other])

    pair = exchange(low_keep, low_send, 1)
    pair, own = lax.optimization_barrier((pair, own))
    own = {r: (own[2 * i], own[2 * i + 1]) for i, r in enumerate(order)}
    right_top, left_rest = right(own[middle][0]), left(own[middle][1])
    right_rest, left_top = right(own[middle - 1][1]), left(own[1 - middle][0])
    pair = exchange(*pair, 2)
    right_top, left_rest, pair = lax.optimization_barrier((right_top, left_rest, pair))
    for s in range(middle - 1, 0, -1):
        right_top, left_rest = add(right_top, own[s][0]), add(left_rest, own[-s][1])
        right_top, left_rest = right(right_top), left(left_rest)
        if s > 1:
            right_rest, left_top = add(right_rest, own[s - 1][1]), add(left_top, own[1 - s][0])
            right_rest, left_top = right(right_rest), left(left_top)
    bits = [1 << i for i in range(n.bit_length() - 1)]
    for bit in bits[2:]:
        pair = exchange(*pair, bit)

    share = width // n
    part = rank // 2
    swap = [(0, 1), (1, 0)]

    def adapter_gradient(low_total):
        if share % 128 == 0:
            low, keep, send = call(
                functools.partial(adapter_kernel, capacity),
                "adapter_gradient",
                [((slot, rank), BF)] + [((n, part, share), BF)] * 2,
                [choice, tokens, low_total],
                work=(2 * own_count * rank * width, 2 * own_count * width),
            )
        else:
            me, core = lax.axis_index("expert"), lax.axis_index("dp")
            upper, _ = pick_rows(choice, capacity)
            low = low_total[0].astype(BF)
            low_tokens = dot(upper[:slot], low, TN).astype(BF)
            down = dot(low_tokens, tokens, TN).astype(BF).reshape(rank, n, share)
            down = down.transpose(1, 0, 2)[jnp.arange(n, dtype=jnp.int32) ^ me]
            keep = jnp.where(core == 0, down[:, :part], down[:, part:])
            send = jnp.where(core == 0, down[:, part:], down[:, :part])
        other = lax.ppermute(send, "dp", swap)
        return low, call(halve_kernel, "halve", [((n // 2, part, share), BF)] * 2, [keep, other])

    def lora_gradients():
        (local,) = call(
            functools.partial(lora_kernel, slot, sizes),
            "lora_rows",
            [((2 * rank, hidden), BF)],
            [*dgates, *dups, *low_rows],
            [
                pltpu.VMEM((n * slot, hidden), BF),
                pltpu.VMEM((n * slot, hidden), BF),
                pltpu.VMEM((n * slot, rank), BF),
            ],
            (4 * n * slot * rank * hidden, 4 * n * slot * hidden),
        )
        return local, lax.ppermute(local, "dp", swap)

    low, pair = adapter_gradient(pair[0])
    low_rows, _ = lax.optimization_barrier((low_rows, pair))
    lora, lora_there = lora_gradients()
    for bit in bits:
        pair = exchange(*pair, bit)
    down = pair[0][0]
    there = lax.ppermute(down, "dp", swap)
    grad_down, grad_gate, grad_up = call(
        join_kernel,
        "join",
        [((rank, hidden), F32)] * 3,
        [down, there, lora, lora_there],
    )

    (input_gradient,) = call(
        functools.partial(finish_kernel, capacity),
        "finish",
        [((own_count, width), BF)],
        [choice, right_top, left_top, own[0][0], right_rest, left_rest, own[0][1], low, adapter_down_factor],
        [pltpu.VMEM((2 * capacity, rank), F32)],
        (4e8, 4.5e6),
    )
    return (input_gradient[None], grad_down, grad_gate, grad_up)


def solution(mesh):
    placed = (
        P(("groups", "dp"), "expert", None),
        P(("groups", "dp"), "expert", None),
        P(("groups", "dp"), "expert", None),
        P(("groups", "dp"), "expert", None),
        P(("groups", "dp"), None, "expert"),
        P(("groups", "dp"), None, "expert"),
        P(None, "expert"),
        P(None, "expert"),
        P("expert", None),
        P("groups", None),
        P("groups", "expert"),
        P("groups", "expert"),
    )
    return jax.shard_map(
        functools.partial(on_device, ring_order(mesh)),
        mesh=mesh,
        in_specs=placed,
        out_specs=(
            P(("groups", "dp"), "expert", None),
            P("groups", "expert"),
            P("groups", "expert"),
            P("groups", "expert"),
        ),
        check_vma=False,
    )
```

```python
import functools

import jax
import jax.numpy as jnp
from jax import lax
from jax.experimental import pallas as pl
from jax.experimental.pallas import tpu as pltpu
from jax.sharding import PartitionSpec as P

SCALE = 0.25
NT = (((1,), (1,)), ((), ()))
TN = (((0,), (0,)), ((), ()))
BF = jnp.bfloat16
F32 = jnp.float32
VMEM_LIMIT = 10 * 1024 * 1024
TILE = 256


def ring_order(mesh):
    count = mesh.shape["expert"]
    plain = list(range(count))
    if count < 4 or count % 2:
        return plain
    snake = list(range(0, count, 2)) + list(range(count - 1, 0, -2))
    spots = [getattr(d, "coords", None) for d in mesh.devices[0, :, 0]]
    if any(s is None for s in spots):
        return snake if count == 8 else plain

    def length(order):
        hops = zip(order, order[1:] + order[:1])
        return sum(sum(abs(a - b) for a, b in zip(spots[i], spots[j])) for i, j in hops)

    return min((plain, snake), key=length)


def dot(a, b, dims=None):
    if dims is None:
        dims = (((1,), (0,)), ((), ()))
    return lax.dot_general(a, b, dims, preferred_element_type=F32)


def pick_rows(choice, capacity):
    tokens = choice.shape[1]
    named = jnp.max((choice == 0).astype(F32), axis=0, keepdims=True)
    before = lax.broadcasted_iota(jnp.int32, (tokens, tokens), 0)
    after = lax.broadcasted_iota(jnp.int32, (tokens, tokens), 1)
    upto = (before <= after).astype(BF)
    count = dot(jnp.broadcast_to(named, (8, tokens)).astype(BF), upto)[:1]
    slot = jnp.where(named > 0, count - 1.0, -1000.0).astype(jnp.int32)
    row = lax.broadcasted_iota(jnp.int32, (2 * capacity, tokens), 0)
    return (row == slot).astype(BF), (row - capacity == slot).astype(BF)


def prepare_kernel(capacity, choice_hbm, weight_hbm, grad_hbm, tokens_hbm, down_hbm, block_ref,
                   choice_ref, weight_ref, grad_ref, tokens_ref, down_ref, sems):
    half = grad_ref.shape[1] // 2
    rank = down_ref.shape[0]
    pairs = [
        (choice_hbm, choice_ref),
        (grad_hbm.at[:, :half], grad_ref.at[:, :half]),
        (grad_hbm.at[:, half:], grad_ref.at[:, half:]),
        (weight_hbm, weight_ref),
        (down_hbm, down_ref),
        (tokens_hbm, tokens_ref),
    ]
    copies = [pltpu.make_async_copy(a, b, sems.at[i]) for i, (a, b) in enumerate(pairs)]
    for copy in copies:
        copy.start()
    copies[0].wait()
    choice = choice_ref[...]
    upper, lower = pick_rows(choice, capacity)
    copies[1].wait()
    first = dot(upper, grad_ref[:, :half])
    copies[2].wait()
    block_ref[:, :half] = (first + dot(lower, grad_ref[:, half:])).astype(BF)
    copies[3].wait()
    weight = jnp.sum(
        jnp.where(choice == 0, weight_ref[...].astype(F32), 0.0), axis=0, keepdims=True
    )
    column = jnp.sum(upper.astype(F32) * weight, axis=1, keepdims=True)
    block_ref[:, half + rank :] = jnp.broadcast_to(column, (2 * capacity, rank)).astype(BF)
    copies[4].wait()
    copies[5].wait()
    low = dot(tokens_ref[...], down_ref[...], NT).astype(BF)
    block_ref[:, half : half + rank] = dot(upper, low).astype(BF)


def cut_kernel(right_in, left_in, top, rest):
    cut = top.shape[0]
    top[...] = right_in[:cut, :]
    rest[...] = left_in[cut:, :]


def place_here(place):
    me = lax.axis_index("expert")
    return me, sum(jnp.where(me == e, p, 0) for e, p in enumerate(place))


def reorder_kernel(place, capacity, gate_in, up_in, *refs):
    gate_out, up_out, tall = refs[-3:]
    count, slot, hidden = gate_out.shape
    _, here = place_here(place)
    live = lax.broadcasted_iota(jnp.int32, (slot, hidden), 0) < capacity
    for source, target in ((gate_in, gate_out), (up_in, up_out)):
        tall[: count * capacity, :] = source[...].astype(F32)
        tall[count * capacity :, :] = jnp.zeros((slot, hidden), F32)
        for e in range(count):
            away = lax.rem(place[e] - here + count, count)
            at = jnp.where(2 * away < count, 2 * away, 2 * (count - away) - 1)
            rows = tall[e * capacity : e * capacity + slot, :]
            target[at] = jnp.where(live, rows, 0.0).astype(BF)


def low_order_kernel(ring, place, order, *refs):
    lows, (keep, send) = refs[:-2], refs[-2:]
    count = len(ring)
    me, here = place_here(place)
    for low, r in zip(lows, order):
        spot = lax.rem(here + r + count, count)
        owner = sum(jnp.where(spot == i, e, 0) for i, e in enumerate(ring))
        key = owner ^ me

        @pl.when(key % 2 == 0)
        def _(low=low, key=key):
            keep[key // 2] = low[...]

        @pl.when(key % 2 == 1)
        def _(low=low, key=key):
            send[key // 2] = low[...]


def halve_kernel(ours, theirs, *outs):
    count = ours.shape[0]
    for i in range(count):
        total = ours[i].astype(F32) + theirs[i].astype(F32)
        out = outs[i % len(outs)]
        out[i // len(outs)] = total.astype(out.dtype)


def hidden_kernel(capacity, slot, start, count, pieces, *refs):
    blocks, refs = [refs[i * pieces : (i + 1) * pieces] for i in range(count)], refs[count * pieces :]
    (gate_ref, up_ref, down_ref, lora_gate, lora_up, dgate_ref, dup_ref, low_ref), refs = refs[:8], refs[8:]
    lows, rows = refs[:count], refs[count]
    hidden, width = down_ref.shape
    half = width // 2
    rank = lora_gate.shape[0]
    tall = rows.shape[0] // count
    for i, block in enumerate(blocks):
        at = i * tall
        for piece in block:
            rows[at : at + piece.shape[0], :] = piece[:, :half]
            at += piece.shape[0]
    if tall % 128 == 0:
        first = dot(down_ref[:, :half], rows[...], NT).T
        second = dot(down_ref[:, half:], rows[...], NT).T
    else:
        first = dot(rows[...], down_ref[:, :half], NT)
        second = dot(rows[...], down_ref[:, half:], NT)
    live = lax.broadcasted_iota(jnp.int32, (slot, hidden), 0) < capacity
    for i in range(count):
        at = i * tall
        extras, seen = [], 0
        for piece in blocks[i]:
            height = min(piece.shape[0], slot - seen)
            extras.append(piece[:height, half:])
            low_ref[i, seen : seen + height, :] = extras[-1][:, :rank]
            seen += height
        weight = jnp.concatenate([x.astype(F32)[:, rank : rank + 1] for x in extras], axis=0)
        grad = (first[at : at + slot] + second[at + capacity : at + capacity + slot]) * weight
        grad = jnp.where(live, grad, 0.0)
        gate = gate_ref[start + i].astype(F32)
        up = up_ref[start + i].astype(F32)
        sig = 1.0 / (1.0 + jnp.exp(-gate))
        slope = sig * (1.0 + gate * (1.0 - sig))
        dgate = (grad * up * slope).astype(BF)
        dup = (grad * gate * sig).astype(BF)
        dgate_ref[i] = dgate
        dup_ref[i] = dup
        lows[i][...] = SCALE * (dot(dgate, lora_gate[...], NT) + dot(dup, lora_up[...], NT))


def stack(groups, slot, sources, target):
    at = 0
    for size, source in zip(groups, sources):
        for i in range(size):
            target[at : at + slot, :] = source[i]
            at += slot


def lora_kernel(slot, groups, *refs):
    pieces = len(groups)
    dgates, dups, lows = refs[:pieces], refs[pieces : 2 * pieces], refs[2 * pieces : 3 * pieces]
    lora_out, dgate, dup, low = refs[3 * pieces :]
    rank = lora_out.shape[0] // 2
    stack(groups, slot, dgates, dgate)
    stack(groups, slot, dups, dup)
    stack(groups, slot, lows, low)
    lora_out[:rank, :] = (SCALE * dot(low[...], dgate[...], TN)).astype(BF)
    lora_out[rank:, :] = (SCALE * dot(low[...], dup[...], TN)).astype(BF)


def partial_kernel(capacity, slot, groups, cut, *refs):
    members, pieces = sum(groups), len(groups)
    dgates, dups, refs = refs[:pieces], refs[pieces : 2 * pieces], refs[2 * pieces :]
    gate_ref, up_ref, outs, (dgate, dup, tile) = refs[0], refs[1], refs[2:-3], refs[-3:]
    half = gate_ref.shape[0] // 2
    stack(groups, slot, dgates, dgate)
    stack(groups, slot, dups, dup)

    for t in range(0, half, TILE):
        sums = []
        for at in (t, t + half):
            sums.append(
                dot(dgate[...], gate_ref[at : at + TILE, :], NT)
                + dot(dup[...], up_ref[at : at + TILE, :], NT)
            )
        for i in range(members):
            at = i * slot
            tile[:capacity, :] = sums[0][at : at + capacity]
            tile[capacity:, :] = sums[1][at : at + capacity]
            outs[2 * i][:, t : t + TILE] = tile[:cut, :].astype(BF)
            outs[2 * i + 1][:, t : t + TILE] = tile[cut:, :].astype(BF)


def adapter_kernel(capacity, choice_ref, tokens_ref, low_in, low_ref, keep_ref, send_ref):
    count, part, share = keep_ref.shape
    low = low_in[0].astype(BF)
    low_ref[...] = low
    upper, _ = pick_rows(choice_ref[...], capacity)
    low = dot(upper[: low.shape[0]], low, TN).astype(BF)
    me, core = lax.axis_index("expert"), lax.axis_index("dp")
    for i in range(count):
        columns = pl.ds(pl.multiple_of((me ^ i) * share, 128), share)
        down = dot(low, tokens_ref[:, columns], TN)
        keep_ref[i] = jnp.where(core == 0, down[:part], down[part:]).astype(BF)
        send_ref[i] = jnp.where(core == 0, down[part:], down[:part]).astype(BF)


def join_kernel(down_ref, there_ref, lora_ref, lora_there, down_out, gate_out, up_out):
    part = down_ref.shape[0]
    core = lax.axis_index("dp")
    down, there = down_ref[...].astype(F32), there_ref[...].astype(F32)
    down_out[:part, :] = jnp.where(core == 0, down, there)
    down_out[part:, :] = jnp.where(core == 0, there, down)
    rank = gate_out.shape[0]
    gate_out[...] = lora_ref[:rank, :].astype(F32) + lora_there[:rank, :].astype(F32)
    up_out[...] = lora_ref[rank:, :].astype(F32) + lora_there[rank:, :].astype(F32)


def finish_kernel(capacity, choice_ref, *refs):
    tops, rests, (low_ref, down_ref, out_ref, low_tall) = refs[:3], refs[3:6], refs[6:]
    cut, half = tops[0].shape
    upper, lower = pick_rows(choice_ref[...], capacity)
    low = low_ref[...].astype(F32)[:capacity]
    zero = jnp.zeros_like(low)
    low_tall[:capacity, :] = low
    low_tall[capacity:, :] = zero
    low_upper = low_tall[...].astype(BF)
    low_tall[:capacity, :] = zero
    low_tall[capacity:, :] = low
    low_lower = low_tall[...].astype(BF)
    adapter = dot(low_upper, down_ref[:, :half]) + dot(low_lower, down_ref[:, half:])
    top = sum(x[...].astype(F32) for x in tops) + adapter[:cut]
    rest = sum(x[...].astype(F32) for x in rests) + adapter[cut:]
    top, rest = top.astype(BF), rest.astype(BF)
    for pick, at in ((upper, 0), (lower, half)):
        picked = dot(pick[:cut], top, TN) + dot(pick[cut:], rest, TN)
        out_ref[:, at : at + half] = picked.astype(BF)


def in_hbm(x):
    return pltpu.with_memory_space_constraint(x, pltpu.HBM)


def in_vmem(x):
    return pltpu.with_memory_space_constraint(x, pltpu.VMEM)


def on_device(
    ring,
    tokens,
    output_gradient,
    token_expert_choice,
    routing_weight_table,
    stored_gate_rows,
    stored_up_rows,
    gate_weight,
    up_weight,
    down_weight,
    adapter_down_factor,
    adapter_gate_factor,
    adapter_up_factor,
):
    n = len(ring)
    tokens, output_gradient = tokens[0], output_gradient[0]
    own_count, width = tokens.shape
    half = width // 2
    capacity = stored_gate_rows.shape[1] // n
    hidden = stored_gate_rows.shape[2]
    rank = adapter_down_factor.shape[0]
    tall = -(-2 * capacity // 128) * 128
    slot = -(-capacity // 8) * 8
    cut = capacity // 16 * 16
    wide = half + 2 * rank
    middle = n // 2
    choice = token_expert_choice[0].T
    weights = routing_weight_table[0].T

    place = [0] * n
    for i, e in enumerate(ring):
        place[e] = i
    to_right = [(ring[i], ring[(i + 1) % n]) for i in range(n)]
    to_left = [(ring[i], ring[(i - 1) % n]) for i in range(n)]
    passes = [[0, -1, 1]] + [[-s, s] for s in range(2, middle)] + [[middle]]
    sizes = [len(group) for group in passes]
    order = [r for group in passes for r in group]
    heights = [cut, 2 * capacity - cut]

    def call(kernel, name, shapes, args, scratch=(), work=(0, 0), **more):
        return pl.pallas_call(
            kernel,
            out_shape=[jax.ShapeDtypeStruct(shape, dtype) for shape, dtype in shapes],
            scratch_shapes=list(scratch),
            compiler_params=pltpu.CompilerParams(vmem_limit_bytes=VMEM_LIMIT),
            cost_estimate=pl.CostEstimate(
                flops=int(work[0]), bytes_accessed=int(work[1]), transcendentals=0
            ),
            name=name,
            **more,
        )(*args)

    def right(x):
        return lax.ppermute(x, "expert", to_right)

    def left(x):
        return lax.ppermute(x, "expert", to_left)

    (block,) = call(
        functools.partial(prepare_kernel, capacity),
        "prepare",
        [((2 * capacity, wide), BF)],
        [in_hbm(x) for x in (choice, weights, output_gradient, tokens, adapter_down_factor)],
        [
            pltpu.VMEM(choice.shape, choice.dtype),
            pltpu.VMEM(weights.shape, BF),
            pltpu.VMEM(output_gradient.shape, BF),
            pltpu.VMEM(tokens.shape, BF),
            pltpu.VMEM(adapter_down_factor.shape, BF),
            pltpu.SemaphoreType.DMA((6,)),
        ],
        (4e8, 4.5e6),
        in_specs=[pl.BlockSpec(memory_space=pl.ANY)] * 5,
    )
    down_here, gate_here, up_here = in_vmem(down_weight), in_vmem(gate_weight), in_vmem(up_weight)
    gate_factor, up_factor = in_vmem(adapter_gate_factor), in_vmem(adapter_up_factor)
    gate_rows, up_rows = call(
        functools.partial(reorder_kernel, place, capacity),
        "reorder",
        [((n, slot, hidden), BF)] * 2,
        [stored_gate_rows[0], stored_up_rows[0], down_here, gate_factor, up_factor],
        [pltpu.VMEM((n * capacity + slot, hidden), F32)],
        (0, 8 * n * slot * hidden),
    )

    dgates, dups, low_rows, lows = [], [], [], []
    got = {0: (block,)}

    def hidden_pass(group):
        size, start, pieces = len(group), len(lows), len(got[group[0]])
        tall = -(-2 * capacity // 128) * 128 if size < 3 else -(-2 * capacity // 16) * 16
        results = call(
            functools.partial(hidden_kernel, capacity, slot, start, size, pieces),
            "hidden_rows",
            [((size, slot, hidden), BF)] * 2
            + [((size, slot, rank), BF)]
            + [((slot, rank), F32)] * size,
            [piece for r in group for piece in got[r]]
            + [gate_rows, up_rows, down_here, gate_factor, up_factor],
            [pltpu.VMEM((size * tall, half), BF)],
            (2 * size * tall * width * hidden, 2 * hidden * width),
        )
        dgates.append(results[0])
        dups.append(results[1])
        low_rows.append(results[2])
        lows.extend(results[3:])

    going_right = going_left = block
    for s in range(1, middle):
        going_right, going_left = right(going_right), left(going_left)
        if s == 1:
            going_right, going_left, gate_rows, up_rows = lax.optimization_barrier(
                (going_right, going_left, gate_rows, up_rows)
            )
        else:
            hidden_pass(passes[s - 2])
            going_right, going_left, dgates[-1], dups[-1] = lax.optimization_barrier(
                (going_right, going_left, dgates[-1], dups[-1])
            )
        got[-s], got[s] = (going_right,), (going_left,)
    right_top, left_rest = call(
        cut_kernel, "cut", [((h, wide), BF) for h in heights], [going_right, going_left]
    )
    right_top, left_rest = right(right_top), left(left_rest)
    hidden_pass(passes[-2])
    right_top, left_rest, dgates[-1], dups[-1] = lax.optimization_barrier(
        (right_top, left_rest, dgates[-1], dups[-1])
    )
    got[middle] = (right_top, left_rest)
    hidden_pass(passes[-1])

    low_keep, low_send = call(
        functools.partial(low_order_kernel, ring, place, order),
        "low_order",
        [((n // 2, slot, rank), F32)] * 2,
        lows,
    )
    own = call(
        functools.partial(partial_kernel, capacity, slot, sizes, cut),
        "partials",
        [((h, half), BF) for h in heights] * n,
        [*dgates, *dups, gate_here, up_here],
        [
            pltpu.VMEM((n * slot, hidden), BF),
            pltpu.VMEM((n * slot, hidden), BF),
            pltpu.VMEM((2 * capacity, TILE), F32),
        ],
        (4 * n * slot * width * hidden, 4 * hidden * width),
    )
    def add(a, b):
        return (a.astype(F32) + b.astype(F32)).astype(BF)

    def exchange(keep, send, bit):
        other = lax.ppermute(send, "expert", [(e, e ^ bit) for e in range(n)])
        count = keep.shape[0]
        parts = 2 if count > 1 else 1
        shape = (count // parts,) + keep.shape[1:]
        return call(halve_kernel, "halve", [(shape, keep.dtype)] * parts, [keep, other])


    share = width // n
    part = rank // 2
    swap = [(0, 1), (1, 0)]

    def adapter_gradient(low_total):
        if share % 128 == 0:
            low, keep, send = call(
                functools.partial(adapter_kernel, capacity),
                "adapter_gradient",
                [((slot, rank), BF)] + [((n, part, share), BF)] * 2,
                [choice, tokens, low_total],
                work=(2 * own_count * rank * width, 2 * own_count * width),
            )
        else:
            me, core = lax.axis_index("expert"), lax.axis_index("dp")
            upper, _ = pick_rows(choice, capacity)
            low = low_total[0].astype(BF)
            low_tokens = dot(upper[:slot], low, TN).astype(BF)
            down = dot(low_tokens, tokens, TN).astype(BF).reshape(rank, n, share)
            down = down.transpose(1, 0, 2)[jnp.arange(n, dtype=jnp.int32) ^ me]
            keep = jnp.where(core == 0, down[:, :part], down[:, part:])
            send = jnp.where(core == 0, down[:, part:], down[:, :part])
        other = lax.ppermute(send, "dp", swap)
        return low, call(halve_kernel, "halve", [((n // 2, part, share), BF)] * 2, [keep, other])

    def lora_gradients():
        (local,) = call(
            functools.partial(lora_kernel, slot, sizes),
            "lora_rows",
            [((2 * rank, hidden), BF)],
            [*dgates, *dups, *low_rows],
            [
                pltpu.VMEM((n * slot, hidden), BF),
                pltpu.VMEM((n * slot, hidden), BF),
                pltpu.VMEM((n * slot, rank), BF),
            ],
            (4 * n * slot * rank * hidden, 4 * n * slot * hidden),
        )
        return local, lax.ppermute(local, "dp", swap)

    bits = [1 << i for i in range(n.bit_length() - 1)]
    pair = exchange(low_keep, low_send, bits[0])
    pair, own = lax.optimization_barrier((pair, own))
    own = {r: (own[2 * i], own[2 * i + 1]) for i, r in enumerate(order)}
    right_top, left_rest = right(own[middle][0]), left(own[middle][1])
    pair = exchange(*pair, bits[1])
    right_rest, left_top, pair = lax.optimization_barrier((own[middle - 1][1], own[1 - middle][0], pair))
    right_rest, left_top = right(right_rest), left(left_top)
    for bit in bits[2:]:
        pair = exchange(*pair, bit)
    low, pair = adapter_gradient(pair[0])
    done = 0
    for s in range(middle - 1, 0, -1):
        right_top, left_rest = add(right_top, own[s][0]), add(left_rest, own[-s][1])
        if s == middle - 2:
            keep, right_top, left_rest = lax.optimization_barrier((pair[0], right_top, left_rest))
            pair = exchange(keep, pair[1], bits[done])
            done += 1
        right_top, left_rest = right(right_top), left(left_rest)
        if s > 1:
            right_rest, left_top = add(right_rest, own[s - 1][1]), add(left_top, own[1 - s][0])
            right_rest, left_top = right(right_rest), left(left_top)
    keep, right_rest, left_top = lax.optimization_barrier((pair[0], right_rest, left_top))
    pair = exchange(keep, pair[1], bits[done])
    done += 1
    low_rows, _ = lax.optimization_barrier((low_rows, pair))
    lora, lora_there = lora_gradients()
    for bit in bits[done:]:
        pair = exchange(*pair, bit)
    down = pair[0][0]
    there = lax.ppermute(down, "dp", swap)
    (input_gradient,) = call(
        functools.partial(finish_kernel, capacity),
        "finish",
        [((own_count, width), BF)],
        [choice, right_top, left_top, own[0][0], right_rest, left_rest, own[0][1], low, adapter_down_factor],
        [pltpu.VMEM((2 * capacity, rank), F32)],
        (4e8, 4.5e6),
    )
    there, input_gradient = lax.optimization_barrier((there, input_gradient))
    grad_down, grad_gate, grad_up = call(
        join_kernel,
        "join",
        [((rank, hidden), F32)] * 3,
        [down, there, lora, lora_there],
    )
    return (input_gradient[None], grad_down, grad_gate, grad_up)


def solution(mesh):
    placed = (
        P(("groups", "dp"), "expert", None),
        P(("groups", "dp"), "expert", None),
        P(("groups", "dp"), "expert", None),
        P(("groups", "dp"), "expert", None),
        P(("groups", "dp"), None, "expert"),
        P(("groups", "dp"), None, "expert"),
        P(None, "expert"),
        P(None, "expert"),
        P("expert", None),
        P("groups", None),
        P("groups", "expert"),
        P("groups", "expert"),
    )
    return jax.shard_map(
        functools.partial(on_device, ring_order(mesh)),
        mesh=mesh,
        in_specs=placed,
        out_specs=(
            P(("groups", "dp"), "expert", None),
            P("groups", "expert"),
            P("groups", "expert"),
            P("groups", "expert"),
        ),
        check_vma=False,
    )
```

```python
import functools

import jax
import jax.numpy as jnp
from jax import lax
from jax.experimental import pallas as pl
from jax.experimental.pallas import tpu as pltpu
from jax.sharding import PartitionSpec as P

SCALE = 0.25
NT = (((1,), (1,)), ((), ()))
TN = (((0,), (0,)), ((), ()))
BF = jnp.bfloat16
F32 = jnp.float32
VMEM_LIMIT = 10 * 1024 * 1024
TILE = 256


def ring_order(mesh):
    count = mesh.shape["expert"]
    plain = list(range(count))
    if count < 4 or count % 2:
        return plain
    snake = list(range(0, count, 2)) + list(range(count - 1, 0, -2))
    spots = [getattr(d, "coords", None) for d in mesh.devices[0, :, 0]]
    if any(s is None for s in spots):
        return snake if count == 8 else plain

    def length(order):
        hops = zip(order, order[1:] + order[:1])
        return sum(sum(abs(a - b) for a, b in zip(spots[i], spots[j])) for i, j in hops)

    return min((plain, snake), key=length)


def dot(a, b, dims=None):
    if dims is None:
        dims = (((1,), (0,)), ((), ()))
    return lax.dot_general(a, b, dims, preferred_element_type=F32)


def pick_rows(choice, capacity):
    tokens = choice.shape[1]
    named = jnp.max((choice == 0).astype(F32), axis=0, keepdims=True)
    before = lax.broadcasted_iota(jnp.int32, (tokens, tokens), 0)
    after = lax.broadcasted_iota(jnp.int32, (tokens, tokens), 1)
    upto = (before <= after).astype(BF)
    count = dot(jnp.broadcast_to(named, (8, tokens)).astype(BF), upto)[:1]
    slot = jnp.where(named > 0, count - 1.0, -1000.0).astype(jnp.int32)
    row = lax.broadcasted_iota(jnp.int32, (2 * capacity, tokens), 0)
    return (row == slot).astype(BF), (row - capacity == slot).astype(BF)


def prepare_kernel(capacity, choice_hbm, weight_hbm, grad_hbm, tokens_hbm, down_hbm, block_ref,
                   choice_ref, weight_ref, grad_ref, tokens_ref, down_ref, sems):
    half = grad_ref.shape[1] // 2
    rank = down_ref.shape[0]
    pairs = [
        (choice_hbm, choice_ref),
        (grad_hbm.at[:, :half], grad_ref.at[:, :half]),
        (grad_hbm.at[:, half:], grad_ref.at[:, half:]),
        (weight_hbm, weight_ref),
        (down_hbm, down_ref),
        (tokens_hbm, tokens_ref),
    ]
    copies = [pltpu.make_async_copy(a, b, sems.at[i]) for i, (a, b) in enumerate(pairs)]
    for copy in copies:
        copy.start()
    copies[0].wait()
    choice = choice_ref[...]
    upper, lower = pick_rows(choice, capacity)
    copies[1].wait()
    first = dot(upper, grad_ref[:, :half])
    copies[2].wait()
    block_ref[:, :half] = (first + dot(lower, grad_ref[:, half:])).astype(BF)
    copies[3].wait()
    weight = jnp.sum(
        jnp.where(choice == 0, weight_ref[...].astype(F32), 0.0), axis=0, keepdims=True
    )
    column = jnp.sum(upper.astype(F32) * weight, axis=1, keepdims=True)
    block_ref[:, half + rank :] = jnp.broadcast_to(column, (2 * capacity, rank)).astype(BF)
    copies[4].wait()
    copies[5].wait()
    low = dot(tokens_ref[...], down_ref[...], NT).astype(BF)
    block_ref[:, half : half + rank] = dot(upper, low).astype(BF)


def cut_kernel(right_in, left_in, top, rest):
    cut = top.shape[0]
    top[...] = right_in[:cut, :]
    rest[...] = left_in[cut:, :]


def place_here(place):
    me = lax.axis_index("expert")
    return me, sum(jnp.where(me == e, p, 0) for e, p in enumerate(place))


def reorder_kernel(place, capacity, gate_in, up_in, gate_out, up_out, tall):
    count, slot, hidden = gate_out.shape
    _, here = place_here(place)
    live = lax.broadcasted_iota(jnp.int32, (slot, hidden), 0) < capacity
    for source, target in ((gate_in, gate_out), (up_in, up_out)):
        tall[: count * capacity, :] = source[...].astype(F32)
        tall[count * capacity :, :] = jnp.zeros((slot, hidden), F32)
        for e in range(count):
            away = lax.rem(place[e] - here + count, count)
            at = jnp.where(2 * away < count, 2 * away, 2 * (count - away) - 1)
            rows = tall[e * capacity : e * capacity + slot, :]
            target[at] = jnp.where(live, rows, 0.0).astype(BF)


def low_order_kernel(ring, place, order, *refs):
    lows, (keep, send) = refs[:-2], refs[-2:]
    count = len(ring)
    me, here = place_here(place)
    for low, r in zip(lows, order):
        spot = lax.rem(here + r + count, count)
        owner = sum(jnp.where(spot == i, e, 0) for i, e in enumerate(ring))
        key = owner ^ me

        @pl.when(key % 2 == 0)
        def _(low=low, key=key):
            keep[key // 2] = low[...]

        @pl.when(key % 2 == 1)
        def _(low=low, key=key):
            send[key // 2] = low[...]


def halve_kernel(ours, theirs, *outs):
    count = ours.shape[0]
    for i in range(count):
        total = ours[i].astype(F32) + theirs[i].astype(F32)
        out = outs[i % len(outs)]
        out[i // len(outs)] = total.astype(out.dtype)


def hidden_kernel(capacity, slot, start, count, pieces, *refs):
    blocks, refs = [refs[i * pieces : (i + 1) * pieces] for i in range(count)], refs[count * pieces :]
    (gate_ref, up_ref, down_ref, lora_gate, lora_up, dgate_ref, dup_ref, low_ref), refs = refs[:8], refs[8:]
    lows, rows = refs[:count], refs[count]
    hidden, width = down_ref.shape
    half = width // 2
    rank = lora_gate.shape[0]
    tall = rows.shape[0] // count
    for i, block in enumerate(blocks):
        at = i * tall
        for piece in block:
            rows[at : at + piece.shape[0], :] = piece[:, :half]
            at += piece.shape[0]
    if tall % 128 == 0:
        first = dot(down_ref[:, :half], rows[...], NT).T
        second = dot(down_ref[:, half:], rows[...], NT).T
    else:
        first = dot(rows[...], down_ref[:, :half], NT)
        second = dot(rows[...], down_ref[:, half:], NT)
    live = lax.broadcasted_iota(jnp.int32, (slot, hidden), 0) < capacity
    for i in range(count):
        at = i * tall
        extras, seen = [], 0
        for piece in blocks[i]:
            height = min(piece.shape[0], slot - seen)
            extras.append(piece[:height, half:])
            low_ref[i, seen : seen + height, :] = extras[-1][:, :rank]
            seen += height
        weight = jnp.concatenate([x.astype(F32)[:, rank : rank + 1] for x in extras], axis=0)
        grad = (first[at : at + slot] + second[at + capacity : at + capacity + slot]) * weight
        grad = jnp.where(live, grad, 0.0)
        gate = gate_ref[start + i].astype(F32)
        up = up_ref[start + i].astype(F32)
        sig = 1.0 / (1.0 + jnp.exp(-gate))
        slope = sig * (1.0 + gate * (1.0 - sig))
        dgate = (grad * up * slope).astype(BF)
        dup = (grad * gate * sig).astype(BF)
        dgate_ref[i] = dgate
        dup_ref[i] = dup
        lows[i][...] = SCALE * (dot(dgate, lora_gate[...], NT) + dot(dup, lora_up[...], NT))


def stack(groups, slot, sources, target):
    at = 0
    for size, source in zip(groups, sources):
        for i in range(size):
            target[at : at + slot, :] = source[i]
            at += slot


def lora_kernel(slot, groups, *refs):
    pieces = len(groups)
    dgates, dups, lows = refs[:pieces], refs[pieces : 2 * pieces], refs[2 * pieces : 3 * pieces]
    lora_out, dgate, dup, low = refs[3 * pieces :]
    rank = lora_out.shape[0] // 2
    stack(groups, slot, dgates, dgate)
    stack(groups, slot, dups, dup)
    stack(groups, slot, lows, low)
    lora_out[:rank, :] = (SCALE * dot(low[...], dgate[...], TN)).astype(BF)
    lora_out[rank:, :] = (SCALE * dot(low[...], dup[...], TN)).astype(BF)


def partial_kernel(capacity, slot, groups, cut, *refs):
    members, pieces = sum(groups), len(groups)
    dgates, dups, refs = refs[:pieces], refs[pieces : 2 * pieces], refs[2 * pieces :]
    gate_ref, up_ref, outs, (dgate, dup, tile) = refs[0], refs[1], refs[2:-3], refs[-3:]
    half = gate_ref.shape[0] // 2
    stack(groups, slot, dgates, dgate)
    stack(groups, slot, dups, dup)

    for t in range(0, half, TILE):
        sums = []
        for at in (t, t + half):
            sums.append(
                dot(dgate[...], gate_ref[at : at + TILE, :], NT)
                + dot(dup[...], up_ref[at : at + TILE, :], NT)
            )
        for i in range(members):
            at = i * slot
            tile[:capacity, :] = sums[0][at : at + capacity]
            tile[capacity:, :] = sums[1][at : at + capacity]
            outs[2 * i][:, t : t + TILE] = tile[:cut, :].astype(BF)
            outs[2 * i + 1][:, t : t + TILE] = tile[cut:, :].astype(BF)


def adapter_kernel(capacity, choice_ref, tokens_ref, low_in, low_ref, keep_ref, send_ref):
    count, part, share = keep_ref.shape
    low = low_in[0].astype(BF)
    low_ref[...] = low
    upper, _ = pick_rows(choice_ref[...], capacity)
    low = dot(upper[: low.shape[0]], low, TN).astype(BF)
    me, core = lax.axis_index("expert"), lax.axis_index("dp")
    for i in range(count):
        columns = pl.ds(pl.multiple_of((me ^ i) * share, 128), share)
        down = dot(low, tokens_ref[:, columns], TN)
        keep_ref[i] = jnp.where(core == 0, down[:part], down[part:]).astype(BF)
        send_ref[i] = jnp.where(core == 0, down[part:], down[:part]).astype(BF)


def join_kernel(down_ref, there_ref, lora_ref, lora_there, down_out, gate_out, up_out):
    part = down_ref.shape[0]
    core = lax.axis_index("dp")
    down, there = down_ref[...].astype(F32), there_ref[...].astype(F32)
    down_out[:part, :] = jnp.where(core == 0, down, there)
    down_out[part:, :] = jnp.where(core == 0, there, down)
    rank = gate_out.shape[0]
    gate_out[...] = lora_ref[:rank, :].astype(F32) + lora_there[:rank, :].astype(F32)
    up_out[...] = lora_ref[rank:, :].astype(F32) + lora_there[rank:, :].astype(F32)


def finish_kernel(capacity, choice_ref, *refs):
    tops, rests, (low_ref, down_ref, out_ref, low_tall) = refs[:3], refs[3:6], refs[6:]
    cut, half = tops[0].shape
    upper, lower = pick_rows(choice_ref[...], capacity)
    low = low_ref[...].astype(F32)[:capacity]
    zero = jnp.zeros_like(low)
    low_tall[:capacity, :] = low
    low_tall[capacity:, :] = zero
    low_upper = low_tall[...].astype(BF)
    low_tall[:capacity, :] = zero
    low_tall[capacity:, :] = low
    low_lower = low_tall[...].astype(BF)
    adapter = dot(low_upper, down_ref[:, :half]) + dot(low_lower, down_ref[:, half:])
    top = sum(x[...].astype(F32) for x in tops) + adapter[:cut]
    rest = sum(x[...].astype(F32) for x in rests) + adapter[cut:]
    top, rest = top.astype(BF), rest.astype(BF)
    for pick, at in ((upper, 0), (lower, half)):
        picked = dot(pick[:cut], top, TN) + dot(pick[cut:], rest, TN)
        out_ref[:, at : at + half] = picked.astype(BF)


def in_hbm(x):
    return pltpu.with_memory_space_constraint(x, pltpu.HBM)


def in_vmem(x):
    return pltpu.with_memory_space_constraint(x, pltpu.VMEM)


def on_device(
    ring,
    tokens,
    output_gradient,
    token_expert_choice,
    routing_weight_table,
    stored_gate_rows,
    stored_up_rows,
    gate_weight,
    up_weight,
    down_weight,
    adapter_down_factor,
    adapter_gate_factor,
    adapter_up_factor,
):
    n = len(ring)
    tokens, output_gradient = tokens[0], output_gradient[0]
    own_count, width = tokens.shape
    half = width // 2
    capacity = stored_gate_rows.shape[1] // n
    hidden = stored_gate_rows.shape[2]
    rank = adapter_down_factor.shape[0]
    tall = -(-2 * capacity // 128) * 128
    slot = -(-capacity // 8) * 8
    cut = capacity // 16 * 16
    wide = half + 2 * rank
    middle = n // 2
    choice = token_expert_choice[0].T
    weights = routing_weight_table[0].T

    place = [0] * n
    for i, e in enumerate(ring):
        place[e] = i
    to_right = [(ring[i], ring[(i + 1) % n]) for i in range(n)]
    to_left = [(ring[i], ring[(i - 1) % n]) for i in range(n)]
    passes = [[0, -1, 1]] + [[-s, s] for s in range(2, middle)] + [[middle]]
    sizes = [len(group) for group in passes]
    order = [r for group in passes for r in group]
    heights = [cut, 2 * capacity - cut]

    def call(kernel, name, shapes, args, scratch=(), work=(0, 0), **more):
        return pl.pallas_call(
            kernel,
            out_shape=[jax.ShapeDtypeStruct(shape, dtype) for shape, dtype in shapes],
            scratch_shapes=list(scratch),
            compiler_params=pltpu.CompilerParams(vmem_limit_bytes=VMEM_LIMIT),
            cost_estimate=pl.CostEstimate(
                flops=int(work[0]), bytes_accessed=int(work[1]), transcendentals=0
            ),
            name=name,
            **more,
        )(*args)

    def right(x):
        return lax.ppermute(x, "expert", to_right)

    def left(x):
        return lax.ppermute(x, "expert", to_left)

    (block,) = call(
        functools.partial(prepare_kernel, capacity),
        "prepare",
        [((2 * capacity, wide), BF)],
        [in_hbm(x) for x in (choice, weights, output_gradient, tokens, adapter_down_factor)],
        [
            pltpu.VMEM(choice.shape, choice.dtype),
            pltpu.VMEM(weights.shape, BF),
            pltpu.VMEM(output_gradient.shape, BF),
            pltpu.VMEM(tokens.shape, BF),
            pltpu.VMEM(adapter_down_factor.shape, BF),
            pltpu.SemaphoreType.DMA((6,)),
        ],
        (4e8, 4.5e6),
        in_specs=[pl.BlockSpec(memory_space=pl.ANY)] * 5,
    )
    gate_rows, up_rows = call(
        functools.partial(reorder_kernel, place, capacity),
        "reorder",
        [((n, slot, hidden), BF)] * 2,
        [stored_gate_rows[0], stored_up_rows[0]],
        [pltpu.VMEM((n * capacity + slot, hidden), F32)],
        (0, 8 * n * slot * hidden),
    )

    down_here, gate_here, up_here = in_vmem(down_weight), in_vmem(gate_weight), in_vmem(up_weight)
    dgates, dups, low_rows, lows = [], [], [], []
    got = {0: (block,)}

    def hidden_pass(group):
        size, start, pieces = len(group), len(lows), len(got[group[0]])
        tall = -(-2 * capacity // 128) * 128 if size < 3 else -(-2 * capacity // 16) * 16
        results = call(
            functools.partial(hidden_kernel, capacity, slot, start, size, pieces),
            "hidden_rows",
            [((size, slot, hidden), BF)] * 2
            + [((size, slot, rank), BF)]
            + [((slot, rank), F32)] * size,
            [piece for r in group for piece in got[r]]
            + [gate_rows, up_rows, down_here, adapter_gate_factor, adapter_up_factor],
            [pltpu.VMEM((size * tall, half), BF)],
            (2 * size * tall * width * hidden, 2 * hidden * width),
        )
        dgates.append(results[0])
        dups.append(results[1])
        low_rows.append(results[2])
        lows.extend(results[3:])

    going_right = going_left = block
    for s in range(1, middle):
        going_right, going_left = right(going_right), left(going_left)
        if s == 1:
            going_right, going_left, gate_rows, up_rows = lax.optimization_barrier(
                (going_right, going_left, gate_rows, up_rows)
            )
        else:
            hidden_pass(passes[s - 2])
            going_right, going_left, dgates[-1], dups[-1] = lax.optimization_barrier(
                (going_right, going_left, dgates[-1], dups[-1])
            )
        got[-s], got[s] = (going_right,), (going_left,)
    right_top, left_rest = call(
        cut_kernel, "cut", [((h, wide), BF) for h in heights], [going_right, going_left]
    )
    right_top, left_rest = right(right_top), left(left_rest)
    hidden_pass(passes[-2])
    right_top, left_rest, dgates[-1], dups[-1] = lax.optimization_barrier(
        (right_top, left_rest, dgates[-1], dups[-1])
    )
    got[middle] = (right_top, left_rest)
    hidden_pass(passes[-1])

    low_keep, low_send = call(
        functools.partial(low_order_kernel, ring, place, order),
        "low_order",
        [((n // 2, slot, rank), F32)] * 2,
        lows,
    )
    own = call(
        functools.partial(partial_kernel, capacity, slot, sizes, cut),
        "partials",
        [((h, half), BF) for h in heights] * n,
        [*dgates, *dups, gate_here, up_here],
        [
            pltpu.VMEM((n * slot, hidden), BF),
            pltpu.VMEM((n * slot, hidden), BF),
            pltpu.VMEM((2 * capacity, TILE), F32),
        ],
        (4 * n * slot * width * hidden, 4 * hidden * width),
    )
    def add(a, b):
        return (a.astype(F32) + b.astype(F32)).astype(BF)

    def exchange(keep, send, bit):
        other = lax.ppermute(send, "expert", [(e, e ^ bit) for e in range(n)])
        count = keep.shape[0]
        parts = 2 if count > 1 else 1
        shape = (count // parts,) + keep.shape[1:]
        return call(halve_kernel, "halve", [(shape, keep.dtype)] * parts, [keep, other])

    pair = exchange(low_keep, low_send, 1)
    pair, own = lax.optimization_barrier((pair, own))
    own = {r: (own[2 * i], own[2 * i + 1]) for i, r in enumerate(order)}
    right_top, left_rest = right(own[middle][0]), left(own[middle][1])
    right_rest, left_top = right(own[middle - 1][1]), left(own[1 - middle][0])

    share = width // n
    part = rank // 2
    swap = [(0, 1), (1, 0)]

    def adapter_gradient(low_total):
        if share % 128 == 0:
            low, keep, send = call(
                functools.partial(adapter_kernel, capacity),
                "adapter_gradient",
                [((slot, rank), BF)] + [((n, part, share), BF)] * 2,
                [choice, tokens, low_total],
                work=(2 * own_count * rank * width, 2 * own_count * width),
            )
        else:
            me, core = lax.axis_index("expert"), lax.axis_index("dp")
            upper, _ = pick_rows(choice, capacity)
            low = low_total[0].astype(BF)
            low_tokens = dot(upper[:slot], low, TN).astype(BF)
            down = dot(low_tokens, tokens, TN).astype(BF).reshape(rank, n, share)
            down = down.transpose(1, 0, 2)[jnp.arange(n, dtype=jnp.int32) ^ me]
            keep = jnp.where(core == 0, down[:, :part], down[:, part:])
            send = jnp.where(core == 0, down[:, part:], down[:, :part])
        other = lax.ppermute(send, "dp", swap)
        return low, call(halve_kernel, "halve", [((n // 2, part, share), BF)] * 2, [keep, other])

    def lora_gradients():
        (local,) = call(
            functools.partial(lora_kernel, slot, sizes),
            "lora_rows",
            [((2 * rank, hidden), BF)],
            [*dgates, *dups, *low_rows],
            [
                pltpu.VMEM((n * slot, hidden), BF),
                pltpu.VMEM((n * slot, hidden), BF),
                pltpu.VMEM((n * slot, rank), BF),
            ],
            (4 * n * slot * rank * hidden, 4 * n * slot * hidden),
        )
        return local, lax.ppermute(local, "dp", swap)

    bits = [1 << i for i in range(n.bit_length() - 1)]
    keep, right_rest = lax.optimization_barrier((pair[0], right_rest))
    pair = exchange(keep, pair[1], bits[1])
    keep, right_top, left_rest = lax.optimization_barrier((pair[0], right_top, left_rest))
    for bit in bits[2:]:
        pair = exchange(keep, pair[1], bit)
        keep = pair[0]
    low, pair = adapter_gradient(keep)
    for s in range(middle - 1, 0, -1):
        right_top, left_rest = add(right_top, own[s][0]), add(left_rest, own[-s][1])
        if s == 1:
            keep, right_top, left_rest = lax.optimization_barrier((pair[0], right_top, left_rest))
            pair = exchange(keep, pair[1], bits[0])
        right_top, left_rest = right(right_top), left(left_rest)
        if s > 1:
            right_rest, left_top = add(right_rest, own[s - 1][1]), add(left_top, own[1 - s][0])
            right_rest, left_top = right(right_rest), left(left_top)
    keep, right_rest, left_top = lax.optimization_barrier((pair[0], right_rest, left_top))
    pair = exchange(keep, pair[1], bits[1])
    low_rows, _ = lax.optimization_barrier((low_rows, pair))
    lora, lora_there = lora_gradients()
    for bit in bits[2:]:
        pair = exchange(*pair, bit)
    down = pair[0][0]
    there = lax.ppermute(down, "dp", swap)
    (input_gradient,) = call(
        functools.partial(finish_kernel, capacity),
        "finish",
        [((own_count, width), BF)],
        [choice, right_top, left_top, own[0][0], right_rest, left_rest, own[0][1], low, adapter_down_factor],
        [pltpu.VMEM((2 * capacity, rank), F32)],
        (4e8, 4.5e6),
    )
    there, input_gradient = lax.optimization_barrier((there, input_gradient))
    grad_down, grad_gate, grad_up = call(
        join_kernel,
        "join",
        [((rank, hidden), F32)] * 3,
        [down, there, lora, lora_there],
    )
    return (input_gradient[None], grad_down, grad_gate, grad_up)


def solution(mesh):
    placed = (
        P(("groups", "dp"), "expert", None),
        P(("groups", "dp"), "expert", None),
        P(("groups", "dp"), "expert", None),
        P(("groups", "dp"), "expert", None),
        P(("groups", "dp"), None, "expert"),
        P(("groups", "dp"), None, "expert"),
        P(None, "expert"),
        P(None, "expert"),
        P("expert", None),
        P("groups", None),
        P("groups", "expert"),
        P("groups", "expert"),
    )
    return jax.shard_map(
        functools.partial(on_device, ring_order(mesh)),
        mesh=mesh,
        in_specs=placed,
        out_specs=(
            P(("groups", "dp"), "expert", None),
            P("groups", "expert"),
            P("groups", "expert"),
            P("groups", "expert"),
        ),
        check_vma=False,
    )
```

```python
import functools

import jax
import jax.numpy as jnp
from jax import lax
from jax.experimental import pallas as pl
from jax.experimental.pallas import tpu as pltpu
from jax.sharding import PartitionSpec as P

SCALE = 0.25
NT = (((1,), (1,)), ((), ()))
TN = (((0,), (0,)), ((), ()))
BF = jnp.bfloat16
F32 = jnp.float32
VMEM_LIMIT = 10 * 1024 * 1024
TILE = 256


def ring_order(mesh):
    count = mesh.shape["expert"]
    plain = list(range(count))
    if count < 4 or count % 2:
        return plain
    snake = list(range(0, count, 2)) + list(range(count - 1, 0, -2))
    spots = [getattr(d, "coords", None) for d in mesh.devices[0, :, 0]]
    if any(s is None for s in spots):
        return snake if count == 8 else plain

    def length(order):
        hops = zip(order, order[1:] + order[:1])
        return sum(sum(abs(a - b) for a, b in zip(spots[i], spots[j])) for i, j in hops)

    return min((plain, snake), key=length)


def dot(a, b, dims=None):
    if dims is None:
        dims = (((1,), (0,)), ((), ()))
    return lax.dot_general(a, b, dims, preferred_element_type=F32)


def pick_rows(choice, capacity):
    tokens = choice.shape[1]
    named = jnp.max((choice == 0).astype(F32), axis=0, keepdims=True)
    before = lax.broadcasted_iota(jnp.int32, (tokens, tokens), 0)
    after = lax.broadcasted_iota(jnp.int32, (tokens, tokens), 1)
    upto = (before <= after).astype(BF)
    count = dot(jnp.broadcast_to(named, (8, tokens)).astype(BF), upto)[:1]
    slot = jnp.where(named > 0, count - 1.0, -1000.0).astype(jnp.int32)
    row = lax.broadcasted_iota(jnp.int32, (2 * capacity, tokens), 0)
    return (row == slot).astype(BF), (row - capacity == slot).astype(BF)


def prepare_kernel(capacity, choice_hbm, weight_hbm, grad_hbm, tokens_hbm, down_hbm, block_ref,
                   choice_ref, weight_ref, grad_ref, tokens_ref, down_ref, sems):
    half = grad_ref.shape[1] // 2
    rank = down_ref.shape[0]
    pairs = [
        (choice_hbm, choice_ref),
        (grad_hbm.at[:, :half], grad_ref.at[:, :half]),
        (grad_hbm.at[:, half:], grad_ref.at[:, half:]),
        (weight_hbm, weight_ref),
        (down_hbm, down_ref),
        (tokens_hbm, tokens_ref),
    ]
    copies = [pltpu.make_async_copy(a, b, sems.at[i]) for i, (a, b) in enumerate(pairs)]
    for copy in copies:
        copy.start()
    copies[0].wait()
    choice = choice_ref[...]
    upper, lower = pick_rows(choice, capacity)
    copies[1].wait()
    first = dot(upper, grad_ref[:, :half])
    copies[2].wait()
    block_ref[:, :half] = (first + dot(lower, grad_ref[:, half:])).astype(BF)
    copies[3].wait()
    weight = jnp.sum(
        jnp.where(choice == 0, weight_ref[...].astype(F32), 0.0), axis=0, keepdims=True
    )
    column = jnp.sum(upper.astype(F32) * weight, axis=1, keepdims=True)
    block_ref[:, half + rank :] = jnp.broadcast_to(column, (2 * capacity, rank)).astype(BF)
    copies[4].wait()
    copies[5].wait()
    low = dot(tokens_ref[...], down_ref[...], NT).astype(BF)
    block_ref[:, half : half + rank] = dot(upper, low).astype(BF)


def cut_kernel(right_in, left_in, top, rest):
    cut = top.shape[0]
    top[...] = right_in[:cut, :]
    rest[...] = left_in[cut:, :]


def place_here(place):
    me = lax.axis_index("expert")
    return me, sum(jnp.where(me == e, p, 0) for e, p in enumerate(place))


def reorder_kernel(place, capacity, gate_in, up_in, *refs):
    gate_out, up_out, tall = refs[-3:]
    count, slot, hidden = gate_out.shape
    _, here = place_here(place)
    live = lax.broadcasted_iota(jnp.int32, (slot, hidden), 0) < capacity
    for source, target in ((gate_in, gate_out), (up_in, up_out)):
        tall[: count * capacity, :] = source[...].astype(F32)
        tall[count * capacity :, :] = jnp.zeros((slot, hidden), F32)
        for e in range(count):
            away = lax.rem(place[e] - here + count, count)
            at = jnp.where(2 * away < count, 2 * away, 2 * (count - away) - 1)
            rows = tall[e * capacity : e * capacity + slot, :]
            target[at] = jnp.where(live, rows, 0.0).astype(BF)


def halve_kernel(ours, theirs, *outs):
    count = ours.shape[0]
    for i in range(count):
        total = ours[i].astype(F32) + theirs[i].astype(F32)
        out = outs[i % len(outs)]
        out[i // len(outs)] = total.astype(out.dtype)


def hidden_kernel(capacity, slot, start, count, pieces, *refs):
    blocks, refs = [refs[i * pieces : (i + 1) * pieces] for i in range(count)], refs[count * pieces :]
    (gate_ref, up_ref, down_ref, lora_gate, lora_up, dgate_ref, dup_ref, low_ref), refs = refs[:8], refs[8:]
    lows, rows = refs[:count], refs[count]
    hidden, width = down_ref.shape
    half = width // 2
    rank = lora_gate.shape[0]
    tall = rows.shape[0] // count
    for i, block in enumerate(blocks):
        at = i * tall
        for piece in block:
            rows[at : at + piece.shape[0], :] = piece[:, :half]
            at += piece.shape[0]
    if tall % 128 == 0:
        first = dot(down_ref[:, :half], rows[...], NT).T
        second = dot(down_ref[:, half:], rows[...], NT).T
    else:
        first = dot(rows[...], down_ref[:, :half], NT)
        second = dot(rows[...], down_ref[:, half:], NT)
    live = lax.broadcasted_iota(jnp.int32, (slot, hidden), 0) < capacity
    for i in range(count):
        at = i * tall
        extras, seen = [], 0
        for piece in blocks[i]:
            height = min(piece.shape[0], slot - seen)
            extras.append(piece[:height, half:])
            low_ref[i, seen : seen + height, :] = extras[-1][:, :rank]
            seen += height
        weight = jnp.concatenate([x.astype(F32)[:, rank : rank + 1] for x in extras], axis=0)
        grad = (first[at : at + slot] + second[at + capacity : at + capacity + slot]) * weight
        grad = jnp.where(live, grad, 0.0)
        gate = gate_ref[start + i].astype(F32)
        up = up_ref[start + i].astype(F32)
        sig = 1.0 / (1.0 + jnp.exp(-gate))
        slope = sig * (1.0 + gate * (1.0 - sig))
        dgate = (grad * up * slope).astype(BF)
        dup = (grad * gate * sig).astype(BF)
        dgate_ref[i] = dgate
        dup_ref[i] = dup
        lows[i][...] = SCALE * (dot(dgate, lora_gate[...], NT) + dot(dup, lora_up[...], NT))


def stack(groups, slot, sources, target):
    at = 0
    for size, source in zip(groups, sources):
        for i in range(size):
            target[at : at + slot, :] = source[i]
            at += slot


def lora_kernel(slot, groups, *refs):
    pieces = len(groups)
    dgates, dups, lows = refs[:pieces], refs[pieces : 2 * pieces], refs[2 * pieces : 3 * pieces]
    lora_out, dgate, dup, low = refs[3 * pieces :]
    rank = lora_out.shape[0] // 2
    stack(groups, slot, dgates, dgate)
    stack(groups, slot, dups, dup)
    stack(groups, slot, lows, low)
    lora_out[:rank, :] = (SCALE * dot(low[...], dgate[...], TN)).astype(BF)
    lora_out[rank:, :] = (SCALE * dot(low[...], dup[...], TN)).astype(BF)


def partial_kernel(capacity, slot, groups, cut, *refs):
    members, pieces = sum(groups), len(groups)
    dgates, dups, refs = refs[:pieces], refs[pieces : 2 * pieces], refs[2 * pieces :]
    gate_ref, up_ref, outs, (dgate, dup, tile) = refs[0], refs[1], refs[2:-3], refs[-3:]
    half = gate_ref.shape[0] // 2
    stack(groups, slot, dgates, dgate)
    stack(groups, slot, dups, dup)

    for t in range(0, half, TILE):
        sums = []
        for at in (t, t + half):
            sums.append(
                dot(dgate[...], gate_ref[at : at + TILE, :], NT)
                + dot(dup[...], up_ref[at : at + TILE, :], NT)
            )
        for i in range(members):
            at = i * slot
            tile[:capacity, :] = sums[0][at : at + capacity]
            tile[capacity:, :] = sums[1][at : at + capacity]
            outs[2 * i][:, t : t + TILE] = tile[:cut, :].astype(BF)
            outs[2 * i + 1][:, t : t + TILE] = tile[cut:, :].astype(BF)


def adapter_kernel(capacity, choice_ref, tokens_ref, *refs):
    lows, (low_ref, keep_ref, send_ref) = refs[:-3], refs[-3:]
    count, part, share = keep_ref.shape
    low = sum(x[...] for x in lows).astype(BF)
    low_ref[...] = low
    upper, _ = pick_rows(choice_ref[...], capacity)
    low = dot(upper[: low.shape[0]], low, TN).astype(BF)
    me, core = lax.axis_index("expert"), lax.axis_index("dp")
    for i in range(count):
        columns = pl.ds(pl.multiple_of((me ^ i) * share, 128), share)
        down = dot(low, tokens_ref[:, columns], TN)
        keep_ref[i] = jnp.where(core == 0, down[:part], down[part:]).astype(BF)
        send_ref[i] = jnp.where(core == 0, down[part:], down[:part]).astype(BF)


def join_kernel(down_ref, there_ref, lora_ref, lora_there, down_out, gate_out, up_out):
    part = down_ref.shape[0]
    core = lax.axis_index("dp")
    down, there = down_ref[...].astype(F32), there_ref[...].astype(F32)
    down_out[:part, :] = jnp.where(core == 0, down, there)
    down_out[part:, :] = jnp.where(core == 0, there, down)
    rank = gate_out.shape[0]
    gate_out[...] = lora_ref[:rank, :].astype(F32) + lora_there[:rank, :].astype(F32)
    up_out[...] = lora_ref[rank:, :].astype(F32) + lora_there[rank:, :].astype(F32)


def finish_kernel(capacity, choice_ref, *refs):
    tops, rests, (low_ref, down_ref, out_ref, low_tall) = refs[:3], refs[3:6], refs[6:]
    cut, half = tops[0].shape
    upper, lower = pick_rows(choice_ref[...], capacity)
    low = low_ref[...].astype(F32)[:capacity]
    zero = jnp.zeros_like(low)
    low_tall[:capacity, :] = low
    low_tall[capacity:, :] = zero
    low_upper = low_tall[...].astype(BF)
    low_tall[:capacity, :] = zero
    low_tall[capacity:, :] = low
    low_lower = low_tall[...].astype(BF)
    adapter = dot(low_upper, down_ref[:, :half]) + dot(low_lower, down_ref[:, half:])
    top = sum(x[...].astype(F32) for x in tops) + adapter[:cut]
    rest = sum(x[...].astype(F32) for x in rests) + adapter[cut:]
    top, rest = top.astype(BF), rest.astype(BF)
    for pick, at in ((upper, 0), (lower, half)):
        picked = dot(pick[:cut], top, TN) + dot(pick[cut:], rest, TN)
        out_ref[:, at : at + half] = picked.astype(BF)


def in_hbm(x):
    return pltpu.with_memory_space_constraint(x, pltpu.HBM)


def in_vmem(x):
    return pltpu.with_memory_space_constraint(x, pltpu.VMEM)


def on_device(
    ring,
    tokens,
    output_gradient,
    token_expert_choice,
    routing_weight_table,
    stored_gate_rows,
    stored_up_rows,
    gate_weight,
    up_weight,
    down_weight,
    adapter_down_factor,
    adapter_gate_factor,
    adapter_up_factor,
):
    n = len(ring)
    tokens, output_gradient = tokens[0], output_gradient[0]
    own_count, width = tokens.shape
    half = width // 2
    capacity = stored_gate_rows.shape[1] // n
    hidden = stored_gate_rows.shape[2]
    rank = adapter_down_factor.shape[0]
    tall = -(-2 * capacity // 128) * 128
    slot = -(-capacity // 8) * 8
    cut = capacity // 16 * 16
    wide = half + 2 * rank
    middle = n // 2
    choice = token_expert_choice[0].T
    weights = routing_weight_table[0].T

    place = [0] * n
    for i, e in enumerate(ring):
        place[e] = i
    to_right = [(ring[i], ring[(i + 1) % n]) for i in range(n)]
    to_left = [(ring[i], ring[(i - 1) % n]) for i in range(n)]
    passes = [[0, -1, 1]] + [[-s, s] for s in range(2, middle)] + [[middle]]
    sizes = [len(group) for group in passes]
    order = [r for group in passes for r in group]
    heights = [cut, 2 * capacity - cut]

    def call(kernel, name, shapes, args, scratch=(), work=(0, 0), **more):
        return pl.pallas_call(
            kernel,
            out_shape=[jax.ShapeDtypeStruct(shape, dtype) for shape, dtype in shapes],
            scratch_shapes=list(scratch),
            compiler_params=pltpu.CompilerParams(vmem_limit_bytes=VMEM_LIMIT),
            cost_estimate=pl.CostEstimate(
                flops=int(work[0]), bytes_accessed=int(work[1]), transcendentals=0
            ),
            name=name,
            **more,
        )(*args)

    def right(x):
        return lax.ppermute(x, "expert", to_right)

    def left(x):
        return lax.ppermute(x, "expert", to_left)

    (block,) = call(
        functools.partial(prepare_kernel, capacity),
        "prepare",
        [((2 * capacity, wide), BF)],
        [in_hbm(x) for x in (choice, weights, output_gradient, tokens, adapter_down_factor)],
        [
            pltpu.VMEM(choice.shape, choice.dtype),
            pltpu.VMEM(weights.shape, BF),
            pltpu.VMEM(output_gradient.shape, BF),
            pltpu.VMEM(tokens.shape, BF),
            pltpu.VMEM(adapter_down_factor.shape, BF),
            pltpu.SemaphoreType.DMA((6,)),
        ],
        (4e8, 4.5e6),
        in_specs=[pl.BlockSpec(memory_space=pl.ANY)] * 5,
    )
    down_here, gate_here, up_here = in_vmem(down_weight), in_vmem(gate_weight), in_vmem(up_weight)
    gate_factor, up_factor = in_vmem(adapter_gate_factor), in_vmem(adapter_up_factor)
    gate_rows, up_rows = call(
        functools.partial(reorder_kernel, place, capacity),
        "reorder",
        [((n, slot, hidden), BF)] * 2,
        [stored_gate_rows[0], stored_up_rows[0], down_here, gate_factor, up_factor],
        [pltpu.VMEM((n * capacity + slot, hidden), F32)],
        (0, 8 * n * slot * hidden),
    )

    dgates, dups, low_rows, lows = [], [], [], []
    got = {0: (block,)}

    def hidden_pass(group):
        size, start, pieces = len(group), len(lows), len(got[group[0]])
        tall = -(-2 * capacity // 128) * 128 if size < 3 else -(-2 * capacity // 16) * 16
        results = call(
            functools.partial(hidden_kernel, capacity, slot, start, size, pieces),
            "hidden_rows",
            [((size, slot, hidden), BF)] * 2
            + [((size, slot, rank), BF)]
            + [((slot, rank), F32)] * size,
            [piece for r in group for piece in got[r]]
            + [gate_rows, up_rows, down_here, gate_factor, up_factor],
            [pltpu.VMEM((size * tall, half), BF)],
            (2 * size * tall * width * hidden, 2 * hidden * width),
        )
        dgates.append(results[0])
        dups.append(results[1])
        low_rows.append(results[2])
        lows.extend(results[3:])

    def to_owner(at):
        r = order[at]
        lows[at] = lax.ppermute(lows[at], "expert", [(ring[i], ring[(i + r) % n]) for i in range(n)])

    going_right = going_left = block
    for s in range(1, middle):
        going_right, going_left = right(going_right), left(going_left)
        if s == 1:
            going_right, going_left, gate_rows, up_rows = lax.optimization_barrier(
                (going_right, going_left, gate_rows, up_rows)
            )
        else:
            before = len(lows)
            hidden_pass(passes[s - 2])
            for at in range(max(before, 1), len(lows)):
                to_owner(at)
            going_right, going_left, dgates[-1], dups[-1], lows[before:] = lax.optimization_barrier(
                (going_right, going_left, dgates[-1], dups[-1], lows[before:])
            )
        got[-s], got[s] = (going_right,), (going_left,)
    right_top, left_rest = call(
        cut_kernel, "cut", [((h, wide), BF) for h in heights], [going_right, going_left]
    )
    right_top, left_rest = right(right_top), left(left_rest)
    before = len(lows)
    hidden_pass(passes[-2])
    for at in range(max(before, 1), len(lows)):
        to_owner(at)
    right_top, left_rest, dgates[-1], dups[-1] = lax.optimization_barrier(
        (right_top, left_rest, dgates[-1], dups[-1])
    )
    got[middle] = (right_top, left_rest)
    hidden_pass(passes[-1])
    to_owner(n - 1)

    own = call(
        functools.partial(partial_kernel, capacity, slot, sizes, cut),
        "partials",
        [((h, half), BF) for h in heights] * n,
        [*dgates, *dups, gate_here, up_here],
        [
            pltpu.VMEM((n * slot, hidden), BF),
            pltpu.VMEM((n * slot, hidden), BF),
            pltpu.VMEM((2 * capacity, TILE), F32),
        ],
        (4 * n * slot * width * hidden, 4 * hidden * width),
    )
    def add(a, b):
        return (a.astype(F32) + b.astype(F32)).astype(BF)

    def exchange(keep, send, bit):
        other = lax.ppermute(send, "expert", [(e, e ^ bit) for e in range(n)])
        count = keep.shape[0]
        parts = 2 if count > 1 else 1
        shape = (count // parts,) + keep.shape[1:]
        return call(halve_kernel, "halve", [(shape, keep.dtype)] * parts, [keep, other])

    lows, own = lax.optimization_barrier((lows, own))
    own = {r: (own[2 * i], own[2 * i + 1]) for i, r in enumerate(order)}
    right_top, left_rest = right(own[middle][0]), left(own[middle][1])
    right_rest, left_top = right(own[middle - 1][1]), left(own[1 - middle][0])
    for s in range(middle - 1, 0, -1):
        right_top, left_rest = add(right_top, own[s][0]), add(left_rest, own[-s][1])
        right_top, left_rest = right(right_top), left(left_rest)
        if s > 1:
            right_rest, left_top = add(right_rest, own[s - 1][1]), add(left_top, own[1 - s][0])
            right_rest, left_top = right(right_rest), left(left_top)
    bits = [1 << i for i in range(n.bit_length() - 1)]

    share = width // n
    part = rank // 2
    swap = [(0, 1), (1, 0)]

    def adapter_gradient():
        if share % 128 == 0:
            low, keep, send = call(
                functools.partial(adapter_kernel, capacity),
                "adapter_gradient",
                [((slot, rank), BF)] + [((n, part, share), BF)] * 2,
                [choice, tokens, *lows],
                work=(2 * own_count * rank * width, 2 * own_count * width),
            )
        else:
            me, core = lax.axis_index("expert"), lax.axis_index("dp")
            upper, _ = pick_rows(choice, capacity)
            low = sum(lows).astype(BF)
            low_tokens = dot(upper[:slot], low, TN).astype(BF)
            down = dot(low_tokens, tokens, TN).astype(BF).reshape(rank, n, share)
            down = down.transpose(1, 0, 2)[jnp.arange(n, dtype=jnp.int32) ^ me]
            keep = jnp.where(core == 0, down[:, :part], down[:, part:])
            send = jnp.where(core == 0, down[:, part:], down[:, :part])
        other = lax.ppermute(send, "dp", swap)
        return low, call(halve_kernel, "halve", [((n // 2, part, share), BF)] * 2, [keep, other])

    def lora_gradients():
        (local,) = call(
            functools.partial(lora_kernel, slot, sizes),
            "lora_rows",
            [((2 * rank, hidden), BF)],
            [*dgates, *dups, *low_rows],
            [
                pltpu.VMEM((n * slot, hidden), BF),
                pltpu.VMEM((n * slot, hidden), BF),
                pltpu.VMEM((n * slot, rank), BF),
            ],
            (4 * n * slot * rank * hidden, 4 * n * slot * hidden),
        )
        return local, lax.ppermute(local, "dp", swap)

    low, pair = adapter_gradient()
    low_rows, _ = lax.optimization_barrier((low_rows, pair))
    lora, lora_there = lora_gradients()
    for bit in bits:
        pair = exchange(*pair, bit)
    down = pair[0][0]
    there = lax.ppermute(down, "dp", swap)
    grad_down, grad_gate, grad_up = call(
        join_kernel,
        "join",
        [((rank, hidden), F32)] * 3,
        [down, there, lora, lora_there],
    )

    (input_gradient,) = call(
        functools.partial(finish_kernel, capacity),
        "finish",
        [((own_count, width), BF)],
        [choice, right_top, left_top, own[0][0], right_rest, left_rest, own[0][1], low, adapter_down_factor],
        [pltpu.VMEM((2 * capacity, rank), F32)],
        (4e8, 4.5e6),
    )
    return (input_gradient[None], grad_down, grad_gate, grad_up)


def solution(mesh):
    placed = (
        P(("groups", "dp"), "expert", None),
        P(("groups", "dp"), "expert", None),
        P(("groups", "dp"), "expert", None),
        P(("groups", "dp"), "expert", None),
        P(("groups", "dp"), None, "expert"),
        P(("groups", "dp"), None, "expert"),
        P(None, "expert"),
        P(None, "expert"),
        P("expert", None),
        P("groups", None),
        P("groups", "expert"),
        P("groups", "expert"),
    )
    return jax.shard_map(
        functools.partial(on_device, ring_order(mesh)),
        mesh=mesh,
        in_specs=placed,
        out_specs=(
            P(("groups", "dp"), "expert", None),
            P("groups", "expert"),
            P("groups", "expert"),
            P("groups", "expert"),
        ),
        check_vma=False,
    )
```

```python
import functools

import jax
import jax.numpy as jnp
from jax import lax
from jax.experimental import pallas as pl
from jax.experimental.pallas import tpu as pltpu
from jax.sharding import PartitionSpec as P

SCALE = 0.25
NT = (((1,), (1,)), ((), ()))
TN = (((0,), (0,)), ((), ()))
BF = jnp.bfloat16
F32 = jnp.float32
VMEM_LIMIT = 10 * 1024 * 1024
TILE = 256


def ring_order(mesh):
    count = mesh.shape["expert"]
    plain = list(range(count))
    if count < 4 or count % 2:
        return plain
    snake = list(range(0, count, 2)) + list(range(count - 1, 0, -2))
    spots = [getattr(d, "coords", None) for d in mesh.devices[0, :, 0]]
    if any(s is None for s in spots):
        return snake if count == 8 else plain

    def length(order):
        hops = zip(order, order[1:] + order[:1])
        return sum(sum(abs(a - b) for a, b in zip(spots[i], spots[j])) for i, j in hops)

    return min((plain, snake), key=length)


def dot(a, b, dims=None):
    if dims is None:
        dims = (((1,), (0,)), ((), ()))
    return lax.dot_general(a, b, dims, preferred_element_type=F32)


def pick_rows(choice, capacity):
    tokens = choice.shape[1]
    named = jnp.max((choice == 0).astype(F32), axis=0, keepdims=True)
    before = lax.broadcasted_iota(jnp.int32, (tokens, tokens), 0)
    after = lax.broadcasted_iota(jnp.int32, (tokens, tokens), 1)
    upto = (before <= after).astype(BF)
    count = dot(jnp.broadcast_to(named, (8, tokens)).astype(BF), upto)[:1]
    slot = jnp.where(named > 0, count - 1.0, -1000.0).astype(jnp.int32)
    row = lax.broadcasted_iota(jnp.int32, (2 * capacity, tokens), 0)
    return (row == slot).astype(BF), (row - capacity == slot).astype(BF)


def prepare_kernel(capacity, choice_hbm, weight_hbm, grad_hbm, tokens_hbm, down_hbm, block_ref,
                   choice_ref, weight_ref, grad_ref, tokens_ref, down_ref, sems):
    half = grad_ref.shape[1] // 2
    rank = down_ref.shape[0]
    pairs = [
        (choice_hbm, choice_ref),
        (grad_hbm.at[:, :half], grad_ref.at[:, :half]),
        (grad_hbm.at[:, half:], grad_ref.at[:, half:]),
        (weight_hbm, weight_ref),
        (down_hbm, down_ref),
        (tokens_hbm, tokens_ref),
    ]
    copies = [pltpu.make_async_copy(a, b, sems.at[i]) for i, (a, b) in enumerate(pairs)]
    for copy in copies:
        copy.start()
    copies[0].wait()
    choice = choice_ref[...]
    upper, lower = pick_rows(choice, capacity)
    copies[1].wait()
    first = dot(upper, grad_ref[:, :half])
    copies[2].wait()
    block_ref[:, :half] = (first + dot(lower, grad_ref[:, half:])).astype(BF)
    copies[3].wait()
    weight = jnp.sum(
        jnp.where(choice == 0, weight_ref[...].astype(F32), 0.0), axis=0, keepdims=True
    )
    column = jnp.sum(upper.astype(F32) * weight, axis=1, keepdims=True)
    block_ref[:, half + rank :] = jnp.broadcast_to(column, (2 * capacity, rank)).astype(BF)
    copies[4].wait()
    copies[5].wait()
    low = dot(tokens_ref[...], down_ref[...], NT).astype(BF)
    block_ref[:, half : half + rank] = dot(upper, low).astype(BF)


def cut_kernel(right_in, left_in, top, rest):
    cut = top.shape[0]
    top[...] = right_in[:cut, :]
    rest[...] = left_in[cut:, :]


def place_here(place):
    me = lax.axis_index("expert")
    return me, sum(jnp.where(me == e, p, 0) for e, p in enumerate(place))


def reorder_kernel(place, capacity, gate_in, up_in, *refs):
    gate_out, up_out, tall = refs[-3:]
    count, slot, hidden = gate_out.shape
    _, here = place_here(place)
    live = lax.broadcasted_iota(jnp.int32, (slot, hidden), 0) < capacity
    for source, target in ((gate_in, gate_out), (up_in, up_out)):
        tall[: count * capacity, :] = source[...].astype(F32)
        tall[count * capacity :, :] = jnp.zeros((slot, hidden), F32)
        for e in range(count):
            away = lax.rem(place[e] - here + count, count)
            at = jnp.where(2 * away < count, 2 * away, 2 * (count - away) - 1)
            rows = tall[e * capacity : e * capacity + slot, :]
            target[at] = jnp.where(live, rows, 0.0).astype(BF)


def halve_kernel(ours, theirs, *outs):
    count = ours.shape[0]
    for i in range(count):
        total = ours[i].astype(F32) + theirs[i].astype(F32)
        out = outs[i % len(outs)]
        out[i // len(outs)] = total.astype(out.dtype)


def hidden_kernel(capacity, slot, start, count, pieces, *refs):
    blocks, refs = [refs[i * pieces : (i + 1) * pieces] for i in range(count)], refs[count * pieces :]
    (gate_ref, up_ref, down_ref, lora_gate, lora_up, dgate_ref, dup_ref, low_ref), refs = refs[:8], refs[8:]
    lows, rows = refs[:count], refs[count]
    hidden, width = down_ref.shape
    half = width // 2
    rank = lora_gate.shape[0]
    tall = rows.shape[0] // count
    for i, block in enumerate(blocks):
        at = i * tall
        for piece in block:
            rows[at : at + piece.shape[0], :] = piece[:, :half]
            at += piece.shape[0]
    if tall % 128 == 0:
        first = dot(down_ref[:, :half], rows[...], NT).T
        second = dot(down_ref[:, half:], rows[...], NT).T
    else:
        first = dot(rows[...], down_ref[:, :half], NT)
        second = dot(rows[...], down_ref[:, half:], NT)
    live = lax.broadcasted_iota(jnp.int32, (slot, hidden), 0) < capacity
    for i in range(count):
        at = i * tall
        extras, seen = [], 0
        for piece in blocks[i]:
            height = min(piece.shape[0], slot - seen)
            extras.append(piece[:height, half:])
            low_ref[i, seen : seen + height, :] = extras[-1][:, :rank]
            seen += height
        weight = jnp.concatenate([x.astype(F32)[:, rank : rank + 1] for x in extras], axis=0)
        grad = (first[at : at + slot] + second[at + capacity : at + capacity + slot]) * weight
        grad = jnp.where(live, grad, 0.0)
        gate = gate_ref[start + i].astype(F32)
        up = up_ref[start + i].astype(F32)
        sig = 1.0 / (1.0 + jnp.exp(-gate))
        slope = sig * (1.0 + gate * (1.0 - sig))
        dgate = (grad * up * slope).astype(BF)
        dup = (grad * gate * sig).astype(BF)
        dgate_ref[i] = dgate
        dup_ref[i] = dup
        lows[i][...] = SCALE * (dot(dgate, lora_gate[...], NT) + dot(dup, lora_up[...], NT))


def stack(groups, slot, sources, target):
    at = 0
    for size, source in zip(groups, sources):
        for i in range(size):
            target[at : at + slot, :] = source[i]
            at += slot


def lora_kernel(slot, groups, *refs):
    pieces = len(groups)
    dgates, dups, lows = refs[:pieces], refs[pieces : 2 * pieces], refs[2 * pieces : 3 * pieces]
    lora_out, dgate, dup, low = refs[3 * pieces :]
    rank = lora_out.shape[0] // 2
    stack(groups, slot, dgates, dgate)
    stack(groups, slot, dups, dup)
    stack(groups, slot, lows, low)
    lora_out[:rank, :] = (SCALE * dot(low[...], dgate[...], TN)).astype(BF)
    lora_out[rank:, :] = (SCALE * dot(low[...], dup[...], TN)).astype(BF)


def partial_kernel(capacity, slot, groups, cut, *refs):
    members, pieces = sum(groups), len(groups)
    dgates, dups, refs = refs[:pieces], refs[pieces : 2 * pieces], refs[2 * pieces :]
    gate_ref, up_ref, outs, (dgate, dup, tile) = refs[0], refs[1], refs[2:-3], refs[-3:]
    half = gate_ref.shape[0] // 2
    stack(groups, slot, dgates, dgate)
    stack(groups, slot, dups, dup)

    for t in range(0, half, TILE):
        sums = []
        for at in (t, t + half):
            sums.append(
                dot(dgate[...], gate_ref[at : at + TILE, :], NT)
                + dot(dup[...], up_ref[at : at + TILE, :], NT)
            )
        for i in range(members):
            at = i * slot
            tile[:capacity, :] = sums[0][at : at + capacity]
            tile[capacity:, :] = sums[1][at : at + capacity]
            outs[2 * i][:, t : t + TILE] = tile[:cut, :].astype(BF)
            outs[2 * i + 1][:, t : t + TILE] = tile[cut:, :].astype(BF)


def adapter_kernel(capacity, choice_ref, tokens_ref, *refs):
    lows, (low_ref, keep_ref, send_ref) = refs[:-3], refs[-3:]
    count, part, share = keep_ref.shape
    low = sum(x[...] for x in lows).astype(BF)
    low_ref[...] = low
    upper, _ = pick_rows(choice_ref[...], capacity)
    low = dot(upper[: low.shape[0]], low, TN).astype(BF)
    me, core = lax.axis_index("expert"), lax.axis_index("dp")
    for i in range(count):
        columns = pl.ds(pl.multiple_of((me ^ i) * share, 128), share)
        down = dot(low, tokens_ref[:, columns], TN)
        keep_ref[i] = jnp.where(core == 0, down[:part], down[part:]).astype(BF)
        send_ref[i] = jnp.where(core == 0, down[part:], down[:part]).astype(BF)


def join_kernel(down_ref, there_ref, lora_ref, lora_there, down_out, gate_out, up_out):
    part = down_ref.shape[0]
    core = lax.axis_index("dp")
    down, there = down_ref[...].astype(F32), there_ref[...].astype(F32)
    down_out[:part, :] = jnp.where(core == 0, down, there)
    down_out[part:, :] = jnp.where(core == 0, there, down)
    rank = gate_out.shape[0]
    gate_out[...] = lora_ref[:rank, :].astype(F32) + lora_there[:rank, :].astype(F32)
    up_out[...] = lora_ref[rank:, :].astype(F32) + lora_there[rank:, :].astype(F32)


def finish_kernel(capacity, choice_ref, *refs):
    tops, rests, (low_ref, down_ref, out_ref, low_tall) = refs[:3], refs[3:6], refs[6:]
    cut, half = tops[0].shape
    upper, lower = pick_rows(choice_ref[...], capacity)
    low = low_ref[...].astype(F32)[:capacity]
    zero = jnp.zeros_like(low)
    low_tall[:capacity, :] = low
    low_tall[capacity:, :] = zero
    low_upper = low_tall[...].astype(BF)
    low_tall[:capacity, :] = zero
    low_tall[capacity:, :] = low
    low_lower = low_tall[...].astype(BF)
    adapter = dot(low_upper, down_ref[:, :half]) + dot(low_lower, down_ref[:, half:])
    top = sum(x[...].astype(F32) for x in tops) + adapter[:cut]
    rest = sum(x[...].astype(F32) for x in rests) + adapter[cut:]
    top, rest = top.astype(BF), rest.astype(BF)
    for pick, at in ((upper, 0), (lower, half)):
        picked = dot(pick[:cut], top, TN) + dot(pick[cut:], rest, TN)
        out_ref[:, at : at + half] = picked.astype(BF)


def in_hbm(x):
    return pltpu.with_memory_space_constraint(x, pltpu.HBM)


def in_vmem(x):
    return pltpu.with_memory_space_constraint(x, pltpu.VMEM)


def on_device(
    ring,
    tokens,
    output_gradient,
    token_expert_choice,
    routing_weight_table,
    stored_gate_rows,
    stored_up_rows,
    gate_weight,
    up_weight,
    down_weight,
    adapter_down_factor,
    adapter_gate_factor,
    adapter_up_factor,
):
    n = len(ring)
    tokens, output_gradient = tokens[0], output_gradient[0]
    own_count, width = tokens.shape
    half = width // 2
    capacity = stored_gate_rows.shape[1] // n
    hidden = stored_gate_rows.shape[2]
    rank = adapter_down_factor.shape[0]
    tall = -(-2 * capacity // 128) * 128
    slot = -(-capacity // 8) * 8
    cut = capacity // 16 * 16
    wide = half + 2 * rank
    middle = n // 2
    choice = token_expert_choice[0].T
    weights = routing_weight_table[0].T

    place = [0] * n
    for i, e in enumerate(ring):
        place[e] = i
    to_right = [(ring[i], ring[(i + 1) % n]) for i in range(n)]
    to_left = [(ring[i], ring[(i - 1) % n]) for i in range(n)]
    passes = [[0, -1, 1]] + [[-s, s] for s in range(2, middle)] + [[middle]]
    sizes = [len(group) for group in passes]
    order = [r for group in passes for r in group]
    heights = [cut, 2 * capacity - cut]

    def call(kernel, name, shapes, args, scratch=(), work=(0, 0), **more):
        return pl.pallas_call(
            kernel,
            out_shape=[jax.ShapeDtypeStruct(shape, dtype) for shape, dtype in shapes],
            scratch_shapes=list(scratch),
            compiler_params=pltpu.CompilerParams(vmem_limit_bytes=VMEM_LIMIT),
            cost_estimate=pl.CostEstimate(
                flops=int(work[0]), bytes_accessed=int(work[1]), transcendentals=0
            ),
            name=name,
            **more,
        )(*args)

    def right(x):
        return lax.ppermute(x, "expert", to_right)

    def left(x):
        return lax.ppermute(x, "expert", to_left)

    (block,) = call(
        functools.partial(prepare_kernel, capacity),
        "prepare",
        [((2 * capacity, wide), BF)],
        [in_hbm(x) for x in (choice, weights, output_gradient, tokens, adapter_down_factor)],
        [
            pltpu.VMEM(choice.shape, choice.dtype),
            pltpu.VMEM(weights.shape, BF),
            pltpu.VMEM(output_gradient.shape, BF),
            pltpu.VMEM(tokens.shape, BF),
            pltpu.VMEM(adapter_down_factor.shape, BF),
            pltpu.SemaphoreType.DMA((6,)),
        ],
        (4e8, 4.5e6),
        in_specs=[pl.BlockSpec(memory_space=pl.ANY)] * 5,
    )
    down_here, gate_here, up_here = in_vmem(down_weight), in_vmem(gate_weight), in_vmem(up_weight)
    gate_factor, up_factor = in_vmem(adapter_gate_factor), in_vmem(adapter_up_factor)
    gate_rows, up_rows = call(
        functools.partial(reorder_kernel, place, capacity),
        "reorder",
        [((n, slot, hidden), BF)] * 2,
        [stored_gate_rows[0], stored_up_rows[0], down_here, gate_factor, up_factor],
        [pltpu.VMEM((n * capacity + slot, hidden), F32)],
        (0, 8 * n * slot * hidden),
    )

    dgates, dups, low_rows, lows = [], [], [], []
    got = {0: (block,)}

    def hidden_pass(group):
        size, start, pieces = len(group), len(lows), len(got[group[0]])
        tall = -(-2 * capacity // 128) * 128 if size < 3 else -(-2 * capacity // 16) * 16
        results = call(
            functools.partial(hidden_kernel, capacity, slot, start, size, pieces),
            "hidden_rows",
            [((size, slot, hidden), BF)] * 2
            + [((size, slot, rank), BF)]
            + [((slot, rank), F32)] * size,
            [piece for r in group for piece in got[r]]
            + [gate_rows, up_rows, down_here, gate_factor, up_factor],
            [pltpu.VMEM((size * tall, half), BF)],
            (2 * size * tall * width * hidden, 2 * hidden * width),
        )
        dgates.append(results[0])
        dups.append(results[1])
        low_rows.append(results[2])
        lows.extend(results[3:])

    def to_owner(at):
        r = order[at]
        lows[at] = lax.ppermute(lows[at], "expert", [(ring[i], ring[(i + r) % n]) for i in range(n)])

    going_right = going_left = block
    for s in range(1, middle):
        going_right, going_left = right(going_right), left(going_left)
        if s == 1:
            going_right, going_left, gate_rows, up_rows = lax.optimization_barrier(
                (going_right, going_left, gate_rows, up_rows)
            )
        else:
            before = len(lows)
            hidden_pass(passes[s - 2])
            for at in range(max(before, 1), len(lows)):
                to_owner(at)
            going_right, going_left, dgates[-1], dups[-1], lows[before:] = lax.optimization_barrier(
                (going_right, going_left, dgates[-1], dups[-1], lows[before:])
            )
        got[-s], got[s] = (going_right,), (going_left,)
    right_top, left_rest = call(
        cut_kernel, "cut", [((h, wide), BF) for h in heights], [going_right, going_left]
    )
    right_top, left_rest = right(right_top), left(left_rest)
    before = len(lows)
    hidden_pass(passes[-2])
    for at in range(max(before, 1), len(lows)):
        to_owner(at)
    right_top, left_rest, dgates[-1], dups[-1] = lax.optimization_barrier(
        (right_top, left_rest, dgates[-1], dups[-1])
    )
    got[middle] = (right_top, left_rest)
    hidden_pass(passes[-1])
    to_owner(n - 1)

    own = call(
        functools.partial(partial_kernel, capacity, slot, sizes, cut),
        "partials",
        [((h, half), BF) for h in heights] * n,
        [*dgates, *dups, gate_here, up_here],
        [
            pltpu.VMEM((n * slot, hidden), BF),
            pltpu.VMEM((n * slot, hidden), BF),
            pltpu.VMEM((2 * capacity, TILE), F32),
        ],
        (4 * n * slot * width * hidden, 4 * hidden * width),
    )
    def add(a, b):
        return (a.astype(F32) + b.astype(F32)).astype(BF)

    def exchange(keep, send, bit):
        other = lax.ppermute(send, "expert", [(e, e ^ bit) for e in range(n)])
        count = keep.shape[0]
        parts = 2 if count > 1 else 1
        shape = (count // parts,) + keep.shape[1:]
        return call(halve_kernel, "halve", [(shape, keep.dtype)] * parts, [keep, other])

    lows, own = lax.optimization_barrier((lows, own))
    own = {r: (own[2 * i], own[2 * i + 1]) for i, r in enumerate(order)}
    right_top, left_rest = right(own[middle][0]), left(own[middle][1])
    right_rest, left_top = right(own[middle - 1][1]), left(own[1 - middle][0])
    bits = [1 << i for i in range(n.bit_length() - 1)]

    share = width // n
    part = rank // 2
    swap = [(0, 1), (1, 0)]

    def adapter_gradient():
        if share % 128 == 0:
            low, keep, send = call(
                functools.partial(adapter_kernel, capacity),
                "adapter_gradient",
                [((slot, rank), BF)] + [((n, part, share), BF)] * 2,
                [choice, tokens, *lows],
                work=(2 * own_count * rank * width, 2 * own_count * width),
            )
        else:
            me, core = lax.axis_index("expert"), lax.axis_index("dp")
            upper, _ = pick_rows(choice, capacity)
            low = sum(lows).astype(BF)
            low_tokens = dot(upper[:slot], low, TN).astype(BF)
            down = dot(low_tokens, tokens, TN).astype(BF).reshape(rank, n, share)
            down = down.transpose(1, 0, 2)[jnp.arange(n, dtype=jnp.int32) ^ me]
            keep = jnp.where(core == 0, down[:, :part], down[:, part:])
            send = jnp.where(core == 0, down[:, part:], down[:, :part])
        other = lax.ppermute(send, "dp", swap)
        return low, call(halve_kernel, "halve", [((n // 2, part, share), BF)] * 2, [keep, other])

    def lora_gradients():
        (local,) = call(
            functools.partial(lora_kernel, slot, sizes),
            "lora_rows",
            [((2 * rank, hidden), BF)],
            [*dgates, *dups, *low_rows],
            [
                pltpu.VMEM((n * slot, hidden), BF),
                pltpu.VMEM((n * slot, hidden), BF),
                pltpu.VMEM((n * slot, rank), BF),
            ],
            (4 * n * slot * rank * hidden, 4 * n * slot * hidden),
        )
        return local, lax.ppermute(local, "dp", swap)

    low, pair = adapter_gradient()
    pair = exchange(*pair, bits[0])
    for s in range(middle - 1, 0, -1):
        right_top, left_rest = add(right_top, own[s][0]), add(left_rest, own[-s][1])
        right_top, left_rest = right(right_top), left(left_rest)
        if s > 1:
            right_rest, left_top = add(right_rest, own[s - 1][1]), add(left_top, own[1 - s][0])
            right_rest, left_top = right(right_rest), left(left_top)
    keep, right_rest, left_top = lax.optimization_barrier((pair[0], right_rest, left_top))
    pair = exchange(keep, pair[1], bits[1])
    low_rows, _ = lax.optimization_barrier((low_rows, pair))
    (input_gradient,) = call(
        functools.partial(finish_kernel, capacity),
        "finish",
        [((own_count, width), BF)],
        [choice, right_top, left_top, own[0][0], right_rest, left_rest, own[0][1], low, adapter_down_factor],
        [pltpu.VMEM((2 * capacity, rank), F32)],
        (4e8, 4.5e6),
    )
    lora, lora_there = lora_gradients()
    for bit in bits[2:]:
        keep, input_gradient = lax.optimization_barrier((pair[0], input_gradient))
        pair = exchange(keep, pair[1], bit)
    down = pair[0][0]
    there = lax.ppermute(down, "dp", swap)
    grad_down, grad_gate, grad_up = call(
        join_kernel,
        "join",
        [((rank, hidden), F32)] * 3,
        [down, there, lora, lora_there],
    )
    return (input_gradient[None], grad_down, grad_gate, grad_up)


def solution(mesh):
    placed = (
        P(("groups", "dp"), "expert", None),
        P(("groups", "dp"), "expert", None),
        P(("groups", "dp"), "expert", None),
        P(("groups", "dp"), "expert", None),
        P(("groups", "dp"), None, "expert"),
        P(("groups", "dp"), None, "expert"),
        P(None, "expert"),
        P(None, "expert"),
        P("expert", None),
        P("groups", None),
        P("groups", "expert"),
        P("groups", "expert"),
    )
    return jax.shard_map(
        functools.partial(on_device, ring_order(mesh)),
        mesh=mesh,
        in_specs=placed,
        out_specs=(
            P(("groups", "dp"), "expert", None),
            P("groups", "expert"),
            P("groups", "expert"),
            P("groups", "expert"),
        ),
        check_vma=False,
    )
```

```python
import functools

import jax
import jax.numpy as jnp
from jax import lax
from jax.experimental import pallas as pl
from jax.experimental.pallas import tpu as pltpu
from jax.sharding import PartitionSpec as P

SCALE = 0.25
NT = (((1,), (1,)), ((), ()))
TN = (((0,), (0,)), ((), ()))
BF = jnp.bfloat16
F32 = jnp.float32
VMEM_LIMIT = 10 * 1024 * 1024
TILE = 256


def ring_order(mesh):
    count = mesh.shape["expert"]
    plain = list(range(count))
    if count < 4 or count % 2:
        return plain
    snake = list(range(0, count, 2)) + list(range(count - 1, 0, -2))
    spots = [getattr(d, "coords", None) for d in mesh.devices[0, :, 0]]
    if any(s is None for s in spots):
        return snake if count == 8 else plain

    def length(order):
        hops = zip(order, order[1:] + order[:1])
        return sum(sum(abs(a - b) for a, b in zip(spots[i], spots[j])) for i, j in hops)

    return min((plain, snake), key=length)


def dot(a, b, dims=None):
    if dims is None:
        dims = (((1,), (0,)), ((), ()))
    return lax.dot_general(a, b, dims, preferred_element_type=F32)


def pick_rows(choice, capacity):
    tokens = choice.shape[1]
    named = jnp.max((choice == 0).astype(F32), axis=0, keepdims=True)
    before = lax.broadcasted_iota(jnp.int32, (tokens, tokens), 0)
    after = lax.broadcasted_iota(jnp.int32, (tokens, tokens), 1)
    upto = (before <= after).astype(BF)
    count = dot(jnp.broadcast_to(named, (8, tokens)).astype(BF), upto)[:1]
    slot = jnp.where(named > 0, count - 1.0, -1000.0).astype(jnp.int32)
    row = lax.broadcasted_iota(jnp.int32, (2 * capacity, tokens), 0)
    return (row == slot).astype(BF), (row - capacity == slot).astype(BF)


def prepare_kernel(capacity, choice_hbm, weight_hbm, grad_hbm, tokens_hbm, down_hbm, block_ref,
                   choice_ref, weight_ref, grad_ref, tokens_ref, down_ref, sems):
    half = grad_ref.shape[1] // 2
    rank = down_ref.shape[0]
    pairs = [
        (choice_hbm, choice_ref),
        (grad_hbm.at[:, :half], grad_ref.at[:, :half]),
        (grad_hbm.at[:, half:], grad_ref.at[:, half:]),
        (weight_hbm, weight_ref),
        (down_hbm, down_ref),
        (tokens_hbm, tokens_ref),
    ]
    copies = [pltpu.make_async_copy(a, b, sems.at[i]) for i, (a, b) in enumerate(pairs)]
    for copy in copies:
        copy.start()
    copies[0].wait()
    choice = choice_ref[...]
    upper, lower = pick_rows(choice, capacity)
    copies[1].wait()
    first = dot(upper, grad_ref[:, :half])
    copies[2].wait()
    block_ref[:, :half] = (first + dot(lower, grad_ref[:, half:])).astype(BF)
    copies[3].wait()
    weight = jnp.sum(
        jnp.where(choice == 0, weight_ref[...].astype(F32), 0.0), axis=0, keepdims=True
    )
    column = jnp.sum(upper.astype(F32) * weight, axis=1, keepdims=True)
    block_ref[:, half + rank :] = jnp.broadcast_to(column, (2 * capacity, rank)).astype(BF)
    copies[4].wait()
    copies[5].wait()
    low = dot(tokens_ref[...], down_ref[...], NT).astype(BF)
    block_ref[:, half : half + rank] = dot(upper, low).astype(BF)


def cut_kernel(right_in, left_in, top, rest):
    cut = top.shape[0]
    top[...] = right_in[:cut, :]
    rest[...] = left_in[cut:, :]


def place_here(place):
    me = lax.axis_index("expert")
    return me, sum(jnp.where(me == e, p, 0) for e, p in enumerate(place))


def reorder_kernel(place, capacity, gate_in, up_in, *refs):
    gate_out, up_out, tall = refs[-3:]
    count, slot, hidden = gate_out.shape
    _, here = place_here(place)
    live = lax.broadcasted_iota(jnp.int32, (slot, hidden), 0) < capacity
    for source, target in ((gate_in, gate_out), (up_in, up_out)):
        tall[: count * capacity, :] = source[...].astype(F32)
        tall[count * capacity :, :] = jnp.zeros((slot, hidden), F32)
        for e in range(count):
            away = lax.rem(place[e] - here + count, count)
            at = jnp.where(2 * away < count, 2 * away, 2 * (count - away) - 1)
            rows = tall[e * capacity : e * capacity + slot, :]
            target[at] = jnp.where(live, rows, 0.0).astype(BF)


def halve_kernel(ours, theirs, *outs):
    count = ours.shape[0]
    for i in range(count):
        total = ours[i].astype(F32) + theirs[i].astype(F32)
        out = outs[i % len(outs)]
        out[i // len(outs)] = total.astype(out.dtype)


def hidden_kernel(capacity, slot, start, count, pieces, *refs):
    blocks, refs = [refs[i * pieces : (i + 1) * pieces] for i in range(count)], refs[count * pieces :]
    (gate_ref, up_ref, down_ref, lora_gate, lora_up, dgate_ref, dup_ref, low_ref), refs = refs[:8], refs[8:]
    lows, rows = refs[:count], refs[count]
    hidden, width = down_ref.shape
    half = width // 2
    rank = lora_gate.shape[0]
    tall = rows.shape[0] // count
    for i, block in enumerate(blocks):
        at = i * tall
        for piece in block:
            rows[at : at + piece.shape[0], :] = piece[:, :half]
            at += piece.shape[0]
    if tall % 128 == 0:
        first = dot(down_ref[:, :half], rows[...], NT).T
        second = dot(down_ref[:, half:], rows[...], NT).T
    else:
        first = dot(rows[...], down_ref[:, :half], NT)
        second = dot(rows[...], down_ref[:, half:], NT)
    live = lax.broadcasted_iota(jnp.int32, (slot, hidden), 0) < capacity
    for i in range(count):
        at = i * tall
        extras, seen = [], 0
        for piece in blocks[i]:
            height = min(piece.shape[0], slot - seen)
            extras.append(piece[:height, half:])
            low_ref[i, seen : seen + height, :] = extras[-1][:, :rank]
            seen += height
        weight = jnp.concatenate([x.astype(F32)[:, rank : rank + 1] for x in extras], axis=0)
        grad = (first[at : at + slot] + second[at + capacity : at + capacity + slot]) * weight
        grad = jnp.where(live, grad, 0.0)
        gate = gate_ref[start + i].astype(F32)
        up = up_ref[start + i].astype(F32)
        sig = 1.0 / (1.0 + jnp.exp(-gate))
        slope = sig * (1.0 + gate * (1.0 - sig))
        dgate = (grad * up * slope).astype(BF)
        dup = (grad * gate * sig).astype(BF)
        dgate_ref[i] = dgate
        dup_ref[i] = dup
        lows[i][...] = SCALE * (dot(dgate, lora_gate[...], NT) + dot(dup, lora_up[...], NT))


def stack(groups, slot, sources, target):
    at = 0
    for size, source in zip(groups, sources):
        for i in range(size):
            target[at : at + slot, :] = source[i]
            at += slot


def lora_kernel(slot, groups, *refs):
    pieces = len(groups)
    dgates, dups, lows = refs[:pieces], refs[pieces : 2 * pieces], refs[2 * pieces : 3 * pieces]
    lora_out, dgate, dup, low = refs[3 * pieces :]
    rank = lora_out.shape[0] // 2
    stack(groups, slot, dgates, dgate)
    stack(groups, slot, dups, dup)
    stack(groups, slot, lows, low)
    lora_out[:rank, :] = (SCALE * dot(low[...], dgate[...], TN)).astype(BF)
    lora_out[rank:, :] = (SCALE * dot(low[...], dup[...], TN)).astype(BF)


def partial_kernel(capacity, slot, groups, cut, *refs):
    members, pieces = sum(groups), len(groups)
    dgates, dups, refs = refs[:pieces], refs[pieces : 2 * pieces], refs[2 * pieces :]
    gate_ref, up_ref, outs, (dgate, dup, tile) = refs[0], refs[1], refs[2:-3], refs[-3:]
    half = gate_ref.shape[0] // 2
    stack(groups, slot, dgates, dgate)
    stack(groups, slot, dups, dup)

    for t in range(0, half, TILE):
        sums = []
        for at in (t, t + half):
            sums.append(
                dot(dgate[...], gate_ref[at : at + TILE, :], NT)
                + dot(dup[...], up_ref[at : at + TILE, :], NT)
            )
        for i in range(members):
            at = i * slot
            tile[:capacity, :] = sums[0][at : at + capacity]
            tile[capacity:, :] = sums[1][at : at + capacity]
            outs[2 * i][:, t : t + TILE] = tile[:cut, :].astype(BF)
            outs[2 * i + 1][:, t : t + TILE] = tile[cut:, :].astype(BF)


def adapter_kernel(capacity, choice_ref, tokens_ref, *refs):
    lows, (low_ref, keep_ref, send_ref) = refs[:-3], refs[-3:]
    count, part, share = keep_ref.shape
    low = sum(x[...] for x in lows).astype(BF)
    low_ref[...] = low
    upper, _ = pick_rows(choice_ref[...], capacity)
    low = dot(upper[: low.shape[0]], low, TN).astype(BF)
    me, core = lax.axis_index("expert"), lax.axis_index("dp")
    for i in range(count):
        columns = pl.ds(pl.multiple_of((me ^ i) * share, 128), share)
        down = dot(low, tokens_ref[:, columns], TN)
        keep_ref[i] = jnp.where(core == 0, down[:part], down[part:]).astype(BF)
        send_ref[i] = jnp.where(core == 0, down[part:], down[:part]).astype(BF)


def join_kernel(down_ref, there_ref, lora_ref, lora_there, down_out, gate_out, up_out):
    part = down_ref.shape[0]
    core = lax.axis_index("dp")
    down, there = down_ref[...].astype(F32), there_ref[...].astype(F32)
    down_out[:part, :] = jnp.where(core == 0, down, there)
    down_out[part:, :] = jnp.where(core == 0, there, down)
    rank = gate_out.shape[0]
    gate_out[...] = lora_ref[:rank, :].astype(F32) + lora_there[:rank, :].astype(F32)
    up_out[...] = lora_ref[rank:, :].astype(F32) + lora_there[rank:, :].astype(F32)


def finish_kernel(capacity, choice_ref, *refs):
    tops, rests, (low_ref, down_ref, out_ref, low_tall) = refs[:3], refs[3:6], refs[6:]
    cut, half = tops[0].shape
    upper, lower = pick_rows(choice_ref[...], capacity)
    low = low_ref[...].astype(F32)[:capacity]
    zero = jnp.zeros_like(low)
    low_tall[:capacity, :] = low
    low_tall[capacity:, :] = zero
    low_upper = low_tall[...].astype(BF)
    low_tall[:capacity, :] = zero
    low_tall[capacity:, :] = low
    low_lower = low_tall[...].astype(BF)
    adapter = dot(low_upper, down_ref[:, :half]) + dot(low_lower, down_ref[:, half:])
    top = sum(x[...].astype(F32) for x in tops) + adapter[:cut]
    rest = sum(x[...].astype(F32) for x in rests) + adapter[cut:]
    top, rest = top.astype(BF), rest.astype(BF)
    for pick, at in ((upper, 0), (lower, half)):
        picked = dot(pick[:cut], top, TN) + dot(pick[cut:], rest, TN)
        out_ref[:, at : at + half] = picked.astype(BF)


def in_hbm(x):
    return pltpu.with_memory_space_constraint(x, pltpu.HBM)


def in_vmem(x):
    return pltpu.with_memory_space_constraint(x, pltpu.VMEM)


def on_device(
    ring,
    tokens,
    output_gradient,
    token_expert_choice,
    routing_weight_table,
    stored_gate_rows,
    stored_up_rows,
    gate_weight,
    up_weight,
    down_weight,
    adapter_down_factor,
    adapter_gate_factor,
    adapter_up_factor,
):
    n = len(ring)
    tokens, output_gradient = tokens[0], output_gradient[0]
    own_count, width = tokens.shape
    half = width // 2
    capacity = stored_gate_rows.shape[1] // n
    hidden = stored_gate_rows.shape[2]
    rank = adapter_down_factor.shape[0]
    tall = -(-2 * capacity // 128) * 128
    slot = -(-capacity // 8) * 8
    cut = capacity // 16 * 16
    wide = half + 2 * rank
    middle = n // 2
    choice = token_expert_choice[0].T
    weights = routing_weight_table[0].T

    place = [0] * n
    for i, e in enumerate(ring):
        place[e] = i
    to_right = [(ring[i], ring[(i + 1) % n]) for i in range(n)]
    to_left = [(ring[i], ring[(i - 1) % n]) for i in range(n)]
    passes = [[0, -1, 1]] + [[-s, s] for s in range(2, middle)] + [[middle]]
    sizes = [len(group) for group in passes]
    order = [r for group in passes for r in group]
    heights = [cut, 2 * capacity - cut]

    def call(kernel, name, shapes, args, scratch=(), work=(0, 0), **more):
        return pl.pallas_call(
            kernel,
            out_shape=[jax.ShapeDtypeStruct(shape, dtype) for shape, dtype in shapes],
            scratch_shapes=list(scratch),
            compiler_params=pltpu.CompilerParams(vmem_limit_bytes=VMEM_LIMIT),
            cost_estimate=pl.CostEstimate(
                flops=int(work[0]), bytes_accessed=int(work[1]), transcendentals=0
            ),
            name=name,
            **more,
        )(*args)

    def right(x):
        return lax.ppermute(x, "expert", to_right)

    def left(x):
        return lax.ppermute(x, "expert", to_left)

    (block,) = call(
        functools.partial(prepare_kernel, capacity),
        "prepare",
        [((2 * capacity, wide), BF)],
        [in_hbm(x) for x in (choice, weights, output_gradient, tokens, adapter_down_factor)],
        [
            pltpu.VMEM(choice.shape, choice.dtype),
            pltpu.VMEM(weights.shape, BF),
            pltpu.VMEM(output_gradient.shape, BF),
            pltpu.VMEM(tokens.shape, BF),
            pltpu.VMEM(adapter_down_factor.shape, BF),
            pltpu.SemaphoreType.DMA((6,)),
        ],
        (4e8, 4.5e6),
        in_specs=[pl.BlockSpec(memory_space=pl.ANY)] * 5,
    )
    down_here, gate_here, up_here = in_vmem(down_weight), in_vmem(gate_weight), in_vmem(up_weight)
    gate_factor, up_factor = in_vmem(adapter_gate_factor), in_vmem(adapter_up_factor)
    gate_rows, up_rows = call(
        functools.partial(reorder_kernel, place, capacity),
        "reorder",
        [((n, slot, hidden), BF)] * 2,
        [stored_gate_rows[0], stored_up_rows[0], down_here, gate_factor, up_factor],
        [pltpu.VMEM((n * capacity + slot, hidden), F32)],
        (0, 8 * n * slot * hidden),
    )

    dgates, dups, low_rows, lows = [], [], [], []
    got = {0: (block,)}

    def hidden_pass(group):
        size, start, pieces = len(group), len(lows), len(got[group[0]])
        tall = -(-2 * capacity // 128) * 128 if size < 3 else -(-2 * capacity // 16) * 16
        results = call(
            functools.partial(hidden_kernel, capacity, slot, start, size, pieces),
            "hidden_rows",
            [((size, slot, hidden), BF)] * 2
            + [((size, slot, rank), BF)]
            + [((slot, rank), F32)] * size,
            [piece for r in group for piece in got[r]]
            + [gate_rows, up_rows, down_here, gate_factor, up_factor],
            [pltpu.VMEM((size * tall, half), BF)],
            (2 * size * tall * width * hidden, 2 * hidden * width),
        )
        dgates.append(results[0])
        dups.append(results[1])
        low_rows.append(results[2])
        lows.extend(results[3:])

    def to_owner(at):
        r = order[at]
        lows[at] = lax.ppermute(lows[at], "expert", [(ring[i], ring[(i + r) % n]) for i in range(n)])

    going_right = going_left = block
    for s in range(1, middle):
        going_right, going_left = right(going_right), left(going_left)
        if s == 1:
            going_right, going_left, gate_rows, up_rows = lax.optimization_barrier(
                (going_right, going_left, gate_rows, up_rows)
            )
        else:
            before = len(lows)
            hidden_pass(passes[s - 2])
            for at in range(max(before, 1), len(lows)):
                to_owner(at)
            going_right, going_left, dgates[-1], dups[-1], lows[before:] = lax.optimization_barrier(
                (going_right, going_left, dgates[-1], dups[-1], lows[before:])
            )
        got[-s], got[s] = (going_right,), (going_left,)
    right_top, left_rest = call(
        cut_kernel, "cut", [((h, wide), BF) for h in heights], [going_right, going_left]
    )
    right_top, left_rest = right(right_top), left(left_rest)
    before = len(lows)
    hidden_pass(passes[-2])
    right_top, left_rest, dgates[-1], dups[-1] = lax.optimization_barrier(
        (right_top, left_rest, dgates[-1], dups[-1])
    )
    got[middle] = (right_top, left_rest)
    hidden_pass(passes[-1])
    lows[before:] = lax.optimization_barrier(lows[before:])
    for at in range(max(before, 1), n):
        to_owner(at)

    own = call(
        functools.partial(partial_kernel, capacity, slot, sizes, cut),
        "partials",
        [((h, half), BF) for h in heights] * n,
        [*dgates, *dups, gate_here, up_here],
        [
            pltpu.VMEM((n * slot, hidden), BF),
            pltpu.VMEM((n * slot, hidden), BF),
            pltpu.VMEM((2 * capacity, TILE), F32),
        ],
        (4 * n * slot * width * hidden, 4 * hidden * width),
    )
    def add(a, b):
        return (a.astype(F32) + b.astype(F32)).astype(BF)

    def exchange(keep, send, bit):
        other = lax.ppermute(send, "expert", [(e, e ^ bit) for e in range(n)])
        count = keep.shape[0]
        parts = 2 if count > 1 else 1
        shape = (count // parts,) + keep.shape[1:]
        return call(halve_kernel, "halve", [(shape, keep.dtype)] * parts, [keep, other])

    lows, own = lax.optimization_barrier((lows, own))
    own = {r: (own[2 * i], own[2 * i + 1]) for i, r in enumerate(order)}
    right_top, left_rest = right(own[middle][0]), left(own[middle][1])
    right_rest, left_top = right(own[middle - 1][1]), left(own[1 - middle][0])
    bits = [1 << i for i in range(n.bit_length() - 1)]

    share = width // n
    part = rank // 2
    swap = [(0, 1), (1, 0)]

    def adapter_gradient():
        if share % 128 == 0:
            low, keep, send = call(
                functools.partial(adapter_kernel, capacity),
                "adapter_gradient",
                [((slot, rank), BF)] + [((n, part, share), BF)] * 2,
                [choice, tokens, *lows],
                work=(2 * own_count * rank * width, 2 * own_count * width),
            )
        else:
            me, core = lax.axis_index("expert"), lax.axis_index("dp")
            upper, _ = pick_rows(choice, capacity)
            low = sum(lows).astype(BF)
            low_tokens = dot(upper[:slot], low, TN).astype(BF)
            down = dot(low_tokens, tokens, TN).astype(BF).reshape(rank, n, share)
            down = down.transpose(1, 0, 2)[jnp.arange(n, dtype=jnp.int32) ^ me]
            keep = jnp.where(core == 0, down[:, :part], down[:, part:])
            send = jnp.where(core == 0, down[:, part:], down[:, :part])
        other = lax.ppermute(send, "dp", swap)
        return low, call(halve_kernel, "halve", [((n // 2, part, share), BF)] * 2, [keep, other])

    def lora_gradients():
        (local,) = call(
            functools.partial(lora_kernel, slot, sizes),
            "lora_rows",
            [((2 * rank, hidden), BF)],
            [*dgates, *dups, *low_rows],
            [
                pltpu.VMEM((n * slot, hidden), BF),
                pltpu.VMEM((n * slot, hidden), BF),
                pltpu.VMEM((n * slot, rank), BF),
            ],
            (4 * n * slot * rank * hidden, 4 * n * slot * hidden),
        )
        return local, lax.ppermute(local, "dp", swap)

    low, pair = adapter_gradient()
    pair = exchange(*pair, bits[0])
    for s in range(middle - 1, 0, -1):
        right_top, left_rest = add(right_top, own[s][0]), add(left_rest, own[-s][1])
        right_top, left_rest = right(right_top), left(left_rest)
        if s > 1:
            right_rest, left_top = add(right_rest, own[s - 1][1]), add(left_top, own[1 - s][0])
            right_rest, left_top = right(right_rest), left(left_top)
    keep, right_rest, left_top = lax.optimization_barrier((pair[0], right_rest, left_top))
    pair = exchange(keep, pair[1], bits[1])
    low_rows, _ = lax.optimization_barrier((low_rows, pair))
    (input_gradient,) = call(
        functools.partial(finish_kernel, capacity),
        "finish",
        [((own_count, width), BF)],
        [choice, right_top, left_top, own[0][0], right_rest, left_rest, own[0][1], low, adapter_down_factor],
        [pltpu.VMEM((2 * capacity, rank), F32)],
        (4e8, 4.5e6),
    )
    lora, lora_there = lora_gradients()
    for bit in bits[2:]:
        keep, input_gradient = lax.optimization_barrier((pair[0], input_gradient))
        pair = exchange(keep, pair[1], bit)
    down = pair[0][0]
    there = lax.ppermute(down, "dp", swap)
    grad_down, grad_gate, grad_up = call(
        join_kernel,
        "join",
        [((rank, hidden), F32)] * 3,
        [down, there, lora, lora_there],
    )
    return (input_gradient[None], grad_down, grad_gate, grad_up)


def solution(mesh):
    placed = (
        P(("groups", "dp"), "expert", None),
        P(("groups", "dp"), "expert", None),
        P(("groups", "dp"), "expert", None),
        P(("groups", "dp"), "expert", None),
        P(("groups", "dp"), None, "expert"),
        P(("groups", "dp"), None, "expert"),
        P(None, "expert"),
        P(None, "expert"),
        P("expert", None),
        P("groups", None),
        P("groups", "expert"),
        P("groups", "expert"),
    )
    return jax.shard_map(
        functools.partial(on_device, ring_order(mesh)),
        mesh=mesh,
        in_specs=placed,
        out_specs=(
            P(("groups", "dp"), "expert", None),
            P("groups", "expert"),
            P("groups", "expert"),
            P("groups", "expert"),
        ),
        check_vma=False,
    )
```
